32 devices in a mesh: dp: 8 (over z, y), chan: 4 (over x, core).
Axes of the slice: x: 2, y: 2, z: 4, core: 2. Of those that a mesh axis runs over, the one named last changes fastest.
Arguments:
- obs_now: bfloat16 [7744, 2048], P('dp', 'chan'), may hold values from -6 to 8
- obs_next: bfloat16 [7744, 2048], P('dp', 'chan'), may hold values from -6 to 6
- games: int32 [64], replicated, may hold values from 0 to 39
- actions: int32 [64], P('dp'), may hold values from 0 to 17, as said below
- next_actions: int32 [64], P('dp'), may hold values from 0 to 17, as said below
- legal: int32 [64, 18], P('dp'), may hold values from 0 to 1, as said below
- done: int32 [64], P('dp'), may hold values 0 or 1
- proj_index: int32 [64, 51], P('dp'), may hold values from 0 to 49
- proj_frac: float32 [64, 51], P('dp'), may hold values from 0 to 1
- weight_in: float32 [2, 2048, 512], P(None, 'chan'), may hold values from -0.125 to 0.125
- weight_mid: float32 [2, 512, 144], P(None, 'chan'), may hold values from -0.5 to 0.5
- weight_out: float32 [2, 512, 2048], P(None, None, 'chan'), may hold values from -0.25 to 0.25
- bottle_gains: float32 [2, 4, 512], P(None, None, 'chan'), may hold values from 0.5 to 1.5
- stream_gains: float32 [2, 2, 2048], P(None, None, 'chan'), may hold values from 0.5 to 1.5
- weight_head: float32 [40, 2048, 918], P('chan', 'dp'), may hold values from -0.25 to 0.25
- first_in: float32 [2, 2048, 512], P(None, 'chan'), may hold values from -7.1525574e-07 to 7.1525574e-07
- first_mid: float32 [2, 512, 144], P(None, 'chan'), may hold values from -7.1525574e-07 to 7.1525574e-07
- first_out: float32 [2, 512, 2048], P(None, None, 'chan'), may hold values from -7.1525574e-07 to 7.1525574e-07
- first_bottle: float32 [2, 4, 512], P(None, None, 'chan'), may hold values from -7.1525574e-07 to 7.1525574e-07
- first_stream: float32 [2, 2, 2048], P(None, None, 'chan'), may hold values from -7.1525574e-07 to 7.1525574e-07
- first_head: float32 [40, 2048, 918], P('chan', 'dp'), may hold values from -7.1525574e-07 to 7.1525574e-07
- second_in: float32 [2, 2048, 512], P(None, 'chan'), may hold values from 1.2569666e-15 to 5.0278664e-15
- second_mid: float32 [2, 512, 144], P(None, 'chan'), may hold values from 3.1424167e-14 to 2.5139333e-13
- second_out: float32 [2, 512, 2048], P(None, None, 'chan'), may hold values from 1.2569666e-15 to 5.0278664e-15
- second_bottle: float32 [2, 4, 512], P(None, None, 'chan'), may hold values from 1.2569666e-15 to 5.0278664e-15
- second_stream: float32 [2, 2, 2048], P(None, None, 'chan'), may hold values from 1.2569666e-15 to 5.0278664e-15
- second_head: float32 [40, 2048, 918], P('chan', 'dp'), may hold values from 1.2569666e-15 to 5.0278664e-15
- target_in: bfloat16 [2, 2048, 512], P(None, 'chan'), may hold values from -0.125 to 0.125
- target_mid: bfloat16 [2, 512, 144], P(None, 'chan'), may hold values from -0.5 to 0.5
- target_out: bfloat16 [2, 512, 2048], P(None, None, 'chan'), may hold values from -0.25 to 0.25
- target_bottle: float32 [2, 4, 512], P(None, None, 'chan'), may hold values from 0.5 to 1.5
- target_stream: float32 [2, 2, 2048], P(None, None, 'chan'), may hold values from 0.5 to 1.5
- target_head: bfloat16 [40, 2048, 918], P('chan', 'dp'), may hold values from -0.25 to 0.25
Outputs:
- fresh_in: float32 [2, 2048, 512], P(None, 'chan')
- momentum_in: float32 [2, 2048, 512], P(None, 'chan')
- variance_in: float32 [2, 2048, 512], P(None, 'chan')
- fresh_mid: float32 [2, 512, 144], P(None, 'chan')
- momentum_mid: float32 [2, 512, 144], P(None, 'chan')
- variance_mid: float32 [2, 512, 144], P(None, 'chan')
- fresh_out: float32 [2, 512, 2048], P(None, None, 'chan')
- momentum_out: float32 [2, 512, 2048], P(None, None, 'chan')
- variance_out: float32 [2, 512, 2048], P(None, None, 'chan')
- fresh_bottle: float32 [2, 4, 512], P(None, None, 'chan')
- momentum_bottle: float32 [2, 4, 512], P(None, None, 'chan')
- variance_bottle: float32 [2, 4, 512], P(None, None, 'chan')
- fresh_stream: float32 [2, 2, 2048], P(None, None, 'chan')
- momentum_stream: float32 [2, 2, 2048], P(None, None, 'chan')
- variance_stream: float32 [2, 2, 2048], P(None, None, 'chan')
- fresh_head: float32 [40, 2048, 918], P('chan', 'dp')
- momentum_head: float32 [40, 2048, 918], P('chan', 'dp')
- variance_head: float32 [40, 2048, 918], P('chan', 'dp')
- gradient_norm: float32 [], replicated
- loss_sum: float32 [], replicated
The draws below stay inside these ranges and needn't reach their ends.
Inputs may be any that keep to these rules, and one draw needn't show every extreme that they name: Each row of legal has ones in its first k columns and zeros after, k from 4 to 18; some row has all 18. `actions`: each action is legal in its row. `next_actions`: each action is legal in its row.
All inputs are finite; a program needn't handle non-finite values. No bound on the sum of `done` on one device may be relied on, other than what follows from the above.
Results may differ from the reference program's by a relative error of at most 0.025.
Values may be sent and summed in bfloat16 or wider, within the bound.
No kernel may reach another device: no remote copies, remote signals or barrier semaphores. Data moves between devices by JAX's collectives and lax.ppermute only.
A program may use at most 768 MiB of HBM per device.

```python
import math
import jax
import jax.numpy as jnp
from jax import lax

WIDTH = 2048
NECK = 512
GROUPS = 32
LAYERS = 2
ACTIONS = 18
ATOMS = 51
MAP = 11
PIX = 121
GAMES = 40
TR_DEV = 8
TRANS = 64
STEP = 10
PARAMS = 79556608
N_DP = 8


def legal_count(key):
    count = jax.random.randint(jax.random.fold_in(key, 11), (TRANS,), 4, ACTIONS + 1)
    return count.at[0].set(ACTIONS)


def draw_legal(key, part):
    count = legal_count(key)
    return (jnp.arange(ACTIONS)[None, :] < count[:, None]).astype(jnp.int32)


def draw_actions(key, part):
    count = legal_count(key)
    key = jax.random.fold_in(key, 2)
    picks = jax.random.randint(key, (TRANS,), 0, count)
    return picks.at[0].set(ACTIONS - 1).astype(jnp.int32)


def draw_next_actions(key, part):
    count = legal_count(key)
    key = jax.random.fold_in(key, 3)
    picks = jax.random.randint(key, (TRANS,), 0, count)
    return picks.at[0].set(ACTIONS - 1).astype(jnp.int32)


def draw_obs_now(key, part):
    key = jax.random.fold_in(key, 5)
    ramp = jnp.arange(WIDTH).astype(jnp.float32) / (WIDTH - 1)
    noise = jnp.clip(jax.random.normal(key, (TRANS * PIX, WIDTH), jnp.float32), -6.0, 6.0)
    offset = 2.0 * ramp
    return (noise + offset[None, :]).astype(jnp.bfloat16)


def touch_ends(entries, stream_key, low, largest):
    longest = entries.shape.index(max(entries.shape))
    spots = []
    for shift in (0, 1):
        where = [jax.random.randint(jax.random.fold_in(stream_key, axis), (), 0, length) for axis, length in enumerate(entries.shape)]
        where[longest] = (where[longest] + shift) % entries.shape[longest]
        spots.append(tuple(where))
    return entries.at[spots[0]].set(low).at[spots[1]].set(largest)


def level_of(own_key, shape, shards, least, largest):
    loudness, own = 1.0, jax.random.fold_in(own_key, 6)
    for axis_at, blocks in shards:
        steps = jnp.exp(jax.random.uniform(jax.random.fold_in(own, axis_at), (blocks,), jnp.float32, least / len(shards), largest / len(shards)))
        loudness = loudness * jnp.repeat(steps, shape[axis_at] // blocks).reshape([-1 if axis == axis_at else 1 for axis in range(len(shape))])
    return loudness


def centred(rng, extent, deviation, most, pieces=(), dtype=jnp.bfloat16):
    level = level_of(rng, extent, pieces, -0.22, 0.18) if pieces else 1.0
    entries = jax.random.normal(rng, extent, jnp.float32) * deviation * level
    return jnp.minimum(jnp.maximum(entries, -most), most).astype(dtype)


def setup_inputs(seed: int = 0) -> dict:
    seeds = jax.random.split(jax.random.key(seed), 34)
    obs_now = draw_obs_now(jax.random.fold_in(seeds[33], 71), 0)
    obs_next = centred(seeds[1], (TRANS * PIX, WIDTH), 1.0, 6.0, ((0, 8), (1, 4)))
    games = touch_ends(jax.random.randint(seeds[2], (TRANS,), 0, GAMES), jax.random.fold_in(seeds[2], 1), 0, GAMES - 1).astype(jnp.int32)
    actions = draw_actions(jax.random.fold_in(seeds[33], 71), 0)
    next_actions = draw_next_actions(jax.random.fold_in(seeds[33], 71), 0)
    legal = draw_legal(jax.random.fold_in(seeds[33], 71), 0)
    done = touch_ends((jax.random.randint(seeds[6], (TRANS,), 0, 4) < 1).astype(jnp.int32), jax.random.fold_in(seeds[6], 1), 0, 1)
    proj_index = touch_ends(jax.random.randint(seeds[7], (TRANS, ATOMS), 0, ATOMS - 1), jax.random.fold_in(seeds[7], 1), 0, (ATOMS - 1) - 1).astype(jnp.int32)
    proj_frac = jnp.clip(1.0 * jax.random.uniform(seeds[8], (TRANS, ATOMS), jnp.float32) ** level_of(seeds[8], (TRANS, ATOMS), ((0, 8),), -0.2, 0.2), 0.0, 1.0)
    weight_in = centred(seeds[9], (LAYERS, WIDTH, NECK), WIDTH ** -0.5, 0.125, ((1, 4),), jnp.float32)
    weight_mid = centred(seeds[10], (LAYERS, NECK, 9 * NECK // GROUPS), (9 * NECK // GROUPS) ** -0.5, 0.5, ((1, 4),), jnp.float32)
    weight_out = centred(seeds[11], (LAYERS, NECK, WIDTH), NECK ** -0.5, 0.25, ((2, 4),), jnp.float32)
    bottle_gains = jnp.clip(1.0 + 0.1 * jax.random.normal(seeds[12], (LAYERS, 4, NECK), jnp.float32), 0.5, 1.5)
    stream_gains = jnp.clip(1.0 + 0.1 * jax.random.normal(seeds[13], (LAYERS, 2, WIDTH), jnp.float32), 0.5, 1.5)
    weight_head = centred(seeds[14], (GAMES, WIDTH, ACTIONS * ATOMS), (WIDTH // 4) ** -0.5, 0.25, ((0, 4), (1, 8)), jnp.float32)
    first_in = centred(seeds[15], (LAYERS, WIDTH, NECK), (0.0011 * PARAMS ** -0.5), 7.152557373046875e-07, ((1, 4),), jnp.float32)
    first_mid = centred(seeds[16], (LAYERS, NECK, 9 * NECK // GROUPS), (0.0011 * PARAMS ** -0.5), 7.152557373046875e-07, ((1, 4),), jnp.float32)
    first_out = centred(seeds[17], (LAYERS, NECK, WIDTH), (0.0011 * PARAMS ** -0.5), 7.152557373046875e-07, ((2, 4),), jnp.float32)
    first_bottle = centred(seeds[18], (LAYERS, 4, NECK), (0.0011 * PARAMS ** -0.5), 7.152557373046875e-07, ((2, 4),), jnp.float32)
    first_stream = centred(seeds[19], (LAYERS, 2, WIDTH), (0.0011 * PARAMS ** -0.5), 7.152557373046875e-07, ((2, 4),), jnp.float32)
    first_head = centred(seeds[20], (GAMES, WIDTH, ACTIONS * ATOMS), (0.0011 * PARAMS ** -0.5), 7.152557373046875e-07, ((0, 4), (1, 8)), jnp.float32)
    second_in = jnp.clip(jnp.exp(math.log(5.0278664491900694e-15) - 1.3862944 * jax.random.uniform(seeds[21], (LAYERS, WIDTH, NECK), jnp.float32) ** level_of(seeds[21], (LAYERS, WIDTH, NECK), ((1, 4),), -0.2, 0.2)), 1.2569666122975174e-15, 5.0278664491900694e-15)
    second_mid = jnp.clip(jnp.exp(math.log(2.5139333431796473e-13) - 2.0794415 * jax.random.uniform(seeds[22], (LAYERS, NECK, 9 * NECK // GROUPS), jnp.float32) ** level_of(seeds[22], (LAYERS, NECK, 9 * NECK // GROUPS), ((1, 4),), -0.2, 0.2)), 3.142416678974559e-14, 2.5139333431796473e-13)
    second_out = jnp.clip(jnp.exp(math.log(5.0278664491900694e-15) - 1.3862944 * jax.random.uniform(seeds[23], (LAYERS, NECK, WIDTH), jnp.float32) ** level_of(seeds[23], (LAYERS, NECK, WIDTH), ((2, 4),), -0.2, 0.2)), 1.2569666122975174e-15, 5.0278664491900694e-15)
    second_bottle = jnp.clip(jnp.exp(math.log(5.0278664491900694e-15) - 1.3862944 * jax.random.uniform(seeds[24], (LAYERS, 4, NECK), jnp.float32) ** level_of(seeds[24], (LAYERS, 4, NECK), ((2, 4),), -0.2, 0.2)), 1.2569666122975174e-15, 5.0278664491900694e-15)
    second_stream = jnp.clip(jnp.exp(math.log(5.0278664491900694e-15) - 1.3862944 * jax.random.uniform(seeds[25], (LAYERS, 2, WIDTH), jnp.float32) ** level_of(seeds[25], (LAYERS, 2, WIDTH), ((2, 4),), -0.2, 0.2)), 1.2569666122975174e-15, 5.0278664491900694e-15)
    second_head = jnp.clip(jnp.exp(math.log(5.0278664491900694e-15) - 1.3862944 * jax.random.uniform(seeds[26], (GAMES, WIDTH, ACTIONS * ATOMS), jnp.float32) ** level_of(seeds[26], (GAMES, WIDTH, ACTIONS * ATOMS), ((0, 4), (1, 8)), -0.2, 0.2)), 1.2569666122975174e-15, 5.0278664491900694e-15)
    target_in = centred(seeds[27], (LAYERS, WIDTH, NECK), WIDTH ** -0.5, 0.125, ((1, 4),))
    target_mid = centred(seeds[28], (LAYERS, NECK, 9 * NECK // GROUPS), (9 * NECK // GROUPS) ** -0.5, 0.5, ((1, 4),))
    target_out = centred(seeds[29], (LAYERS, NECK, WIDTH), NECK ** -0.5, 0.25, ((2, 4),))
    target_bottle = jnp.clip(1.0 + 0.1 * jax.random.normal(seeds[30], (LAYERS, 4, NECK), jnp.float32), 0.5, 1.5)
    target_stream = jnp.clip(1.0 + 0.1 * jax.random.normal(seeds[31], (LAYERS, 2, WIDTH), jnp.float32), 0.5, 1.5)
    target_head = centred(seeds[32], (GAMES, WIDTH, ACTIONS * ATOMS), (WIDTH // 4) ** -0.5, 0.25, ((0, 4), (1, 8)))
    return {"obs_now": obs_now, "obs_next": obs_next, "games": games, "actions": actions, "next_actions": next_actions, "legal": legal, "done": done, "proj_index": proj_index, "proj_frac": proj_frac, "weight_in": weight_in, "weight_mid": weight_mid, "weight_out": weight_out, "bottle_gains": bottle_gains, "stream_gains": stream_gains, "weight_head": weight_head, "first_in": first_in, "first_mid": first_mid, "first_out": first_out, "first_bottle": first_bottle, "first_stream": first_stream, "first_head": first_head, "second_in": second_in, "second_mid": second_mid, "second_out": second_out, "second_bottle": second_bottle, "second_stream": second_stream, "second_head": second_head, "target_in": target_in, "target_mid": target_mid, "target_out": target_out, "target_bottle": target_bottle, "target_stream": target_stream, "target_head": target_head}


@jax.custom_vjp
def low(v):
    return lax.optimization_barrier(v.astype(jnp.bfloat16)).astype(jnp.float32)

@jax.custom_vjp
def low_back(v):
    return v

def low_keep(v):
    return (low(v), None)

def low_pass(kept, grad):
    return (grad,)

def back_keep(v):
    return (v, None)

def back_low(kept, grad):
    return (low(grad),)
low.defvjp(low_keep, low_pass)
low_back.defvjp(back_keep, back_low)
highest = lax.Precision.HIGHEST
rates = (0.02, 0.08, 0.02, 0.5, 0.5, 0.02)

def group_norm(value, gain, bias, size):
    rows, width = value.shape
    shaped = value.reshape(rows // PIX, PIX, width // size, size)
    center = shaped - lax.optimization_barrier(jnp.mean(shaped, axis=(1, 3), keepdims=True))
    spread = lax.optimization_barrier(jnp.mean(center * center, axis=(1, 3), keepdims=True))
    return (center * lax.rsqrt(spread + 1e-05)).reshape(rows, width) * gain + bias

def grouped_conv(value, weight, size):
    rows, width = value.shape
    images = rows // PIX
    grid = jnp.pad(value.reshape(images, MAP, MAP, width), ((0, 0), (1, 1), (1, 1), (0, 0)))
    taps = jnp.stack([grid[:, row_shift:row_shift + MAP, col_shift:col_shift + MAP, :] for row_shift in range(3) for col_shift in range(3)], axis=3)
    taps = taps.reshape(images, MAP, MAP, 9, width // size, size)
    kernel = weight.reshape(width // size, size, 9, size)
    result = jnp.einsum('nhwtgi,goti->nhwgo', taps, kernel, precision=highest)
    return result.reshape(rows, width)

def block(stream, w_first, w_conv, w_last, bottle, outer):
    size_mid = NECK // GROUPS
    first = low_back(jnp.dot(low(stream), w_first, precision=highest))
    one = low(jax.nn.silu(group_norm(first, bottle[0], bottle[1], size_mid)))
    second = low_back(grouped_conv(one, w_conv, size_mid))
    two = low(jax.nn.silu(group_norm(second, bottle[2], bottle[3], size_mid)))
    third = low_back(jnp.dot(two, w_last, precision=highest))
    return jax.nn.silu(stream + group_norm(third, outer[0], outer[1], WIDTH // GROUPS))

def torso(obs, weights):
    stream = obs
    for layer in range(LAYERS):
        stream = block(stream, low(weights[0][layer]), low(weights[1][layer]), low(weights[2][layer]), weights[3][layer], weights[4][layer])
    return lax.optimization_barrier(jnp.mean(stream.reshape(stream.shape[0] // PIX, PIX, WIDTH), axis=1))

def head_logits(pooled, table, game_rows):
    picked = low(jnp.take(table, game_rows, axis=0))
    return low_back(jnp.einsum('bc,bco->bo', low(pooled), picked, precision=highest))

def loss_rows(logits, target_logits, actions, next_actions, legal, done, proj_index, proj_frac):
    count = logits.shape[0]
    actions_range = jnp.arange(ACTIONS)
    logp = jax.nn.log_softmax(logits.reshape(count, ACTIONS, ATOMS), axis=-1)
    taken = lax.optimization_barrier(jnp.sum(jnp.where((actions_range[None, :] == actions[:, None])[:, :, None], logp, 0.0), axis=1))
    target_prob = jax.nn.softmax(target_logits.reshape(count, ACTIONS, ATOMS), axis=-1)
    chosen = lax.optimization_barrier(jnp.sum(jnp.where((actions_range[None, :] == next_actions[:, None])[:, :, None], target_prob, 0.0), axis=1))
    source = jnp.where(done[:, None] > 0, 1.0 / ATOMS, chosen)
    atoms = jnp.arange(ATOMS)
    lower = jnp.where(proj_index[:, :, None] == atoms[None, None, :], proj_frac[:, :, None], 0.0)
    upper = jnp.where(proj_index[:, :, None] + 1 == atoms[None, None, :], 1.0 - proj_frac[:, :, None], 0.0)
    projected = lax.optimization_barrier(jnp.sum(source[:, :, None] * (lower + upper), axis=1))
    cross = -lax.optimization_barrier(jnp.sum(projected * taken, axis=1))
    support = -10.0 + 20.0 * atoms.astype(jnp.float32) / (ATOMS - 1)
    values = lax.optimization_barrier(jnp.sum(jnp.exp(logp) * support, axis=2))
    masked = jnp.where(legal > 0, values, -1e+30)
    top = lax.optimization_barrier(jnp.max(masked, axis=1, keepdims=True))
    total = lax.optimization_barrier(jnp.sum(jnp.where(legal > 0, jnp.exp(masked - top), 0.0), axis=1))
    spread = top[:, 0] + jnp.log(total)
    picked = lax.optimization_barrier(jnp.sum(jnp.where(actions_range[None, :] == actions[:, None], values, 0.0), axis=1))
    return cross + 0.05 * (spread - picked)

def adamw(weight, first, second, grad, rate):
    momentum = 0.9 * first + 0.1 * grad
    variance = 0.999 * second + 0.001 * grad * grad
    scaled = momentum / (1.0 - 0.9 ** STEP) / (jnp.sqrt(variance / (1.0 - 0.999 ** STEP)) + 1e-08)
    return (weight - rate * (scaled + 0.1 * weight), momentum, variance)

def reference(obs_now, obs_next, games, actions, next_actions, legal, done, proj_index, proj_frac, weight_in, weight_mid, weight_out, bottle_gains, stream_gains, weight_head, first_in, first_mid, first_out, first_bottle, first_stream, first_head, second_in, second_mid, second_out, second_bottle, second_stream, second_head, target_in, target_mid, target_out, target_bottle, target_stream, target_head):
    params = (weight_in, weight_mid, weight_out, bottle_gains, stream_gains, weight_head)
    targets = (target_in.astype(jnp.float32), target_mid.astype(jnp.float32), target_out.astype(jnp.float32), target_bottle, target_stream, target_head.astype(jnp.float32))
    rows_block = TR_DEV * PIX
    blocks = (obs_now.astype(jnp.float32).reshape(N_DP, rows_block, WIDTH), obs_next.astype(jnp.float32).reshape(N_DP, rows_block, WIDTH), games.reshape(N_DP, TR_DEV), actions.reshape(N_DP, TR_DEV), next_actions.reshape(N_DP, TR_DEV), legal.reshape(N_DP, TR_DEV, ACTIONS), done.reshape(N_DP, TR_DEV), proj_index.reshape(N_DP, TR_DEV, ATOMS), proj_frac.reshape(N_DP, TR_DEV, ATOMS))

    def step(carry, piece):
        grads, total = carry
        now, later, game_rows, taken, chosen, allowed, ended, index, share = piece
        target_logits = head_logits(torso(later, targets[:5]), targets[5], game_rows)

        def objective(weights):
            logits = head_logits(torso(now, weights[:5]), weights[5], game_rows)
            losses = jnp.sum(loss_rows(logits, target_logits, taken, chosen, allowed, ended, index, share))
            return (losses / TRANS, losses)
        value, pullback, losses = jax.vjp(objective, params, has_aux=True)
        grad, = pullback(jnp.ones_like(value))
        return ((jax.tree.map(jnp.add, grads, grad), total + losses), None)
    start = (jax.tree.map(jnp.zeros_like, params), jnp.zeros((), jnp.float32))
    (grads, loss_sum), _ = lax.scan(step, start, blocks)
    squares = sum((jnp.sum(grad * grad) for grad in grads))
    gradient_norm = jnp.sqrt(squares)
    scale = jnp.minimum(1.0, 0.01 / (gradient_norm + 1e-06))
    firsts = (first_in, first_mid, first_out, first_bottle, first_stream, first_head)
    seconds = (second_in, second_mid, second_out, second_bottle, second_stream, second_head)
    result = []
    for weight, first, second, grad, rate in zip(params, firsts, seconds, grads, rates):
        result.extend(adamw(weight, first, second, grad * scale, rate))
    return (result[0], result[1], result[2], result[3], result[4], result[5], result[6], result[7], result[8], result[9], result[10], result[11], result[12], result[13], result[14], result[15], result[16], result[17], gradient_norm, loss_sum)
```

```python
import functools

import jax
import jax.numpy as jnp
import numpy as np
from jax import lax
from jax.experimental import pallas as pl
from jax.experimental.pallas import tpu as pltpu
from jax.sharding import PartitionSpec as P

WIDTH = 2048
NECK = 512
GROUPS = 32
LAYERS = 2
ACTIONS = 18
ATOMS = 51
MAP = 11
PIX = 121
STEP = 10
SLOT = 128
TAPS = 9
EPS = 1e-05

bf16 = jnp.bfloat16
f32 = jnp.float32
highest = lax.Precision.HIGHEST
rates = (0.02, 0.08, 0.02, 0.5, 0.5, 0.02)

NT = (((1,), (1,)), ((), ()))
TN = (((0,), (0,)), ((), ()))


def shift_matrices():
    table = np.zeros((TAPS, SLOT, SLOT), np.float32)
    for tap in range(TAPS):
        down, right = tap // 3 - 1, tap % 3 - 1
        for row in range(MAP):
            for col in range(MAP):
                if 0 <= row + down < MAP and 0 <= col + right < MAP:
                    table[tap, row * MAP + col, (row + down) * MAP + col + right] = 1.0
    return table.reshape(TAPS * SLOT, SLOT)


def call(kernel, outs, scratch=(), flops=0, **kw):
    return pl.pallas_call(
        kernel,
        out_shape=outs,
        scratch_shapes=list(scratch),
        compiler_params=pltpu.CompilerParams(vmem_limit_bytes=48 * 1024 * 1024),
        cost_estimate=pl.CostEstimate(
            flops=flops, bytes_accessed=8 * 1024 * 1024, transcendentals=0
        ),
        **kw,
    )


def shape(dims, dtype):
    return jax.ShapeDtypeStruct(dims, dtype)


def rows_of(i, count=SLOT):
    return slice(i * count, (i + 1) * count)


def each(count, step):
    for i in range(count):
        step(i)


def pixel_mask():
    return (lax.broadcasted_iota(jnp.int32, (SLOT, 1), 0) < PIX).astype(f32)


def group_matrix(width, size):
    bits = size.bit_length() - 1
    row = lax.shift_right_logical(lax.broadcasted_iota(jnp.int32, (width, width), 0), bits)
    col = lax.shift_right_logical(lax.broadcasted_iota(jnp.int32, (width, width), 1), bits)
    return jnp.where(row == col, 1.0 / (size * PIX), 0.0).astype(f32)


def group_mix(sums, size):
    count, width = sums.shape
    tile = min(width, 128)
    parts = width // tile
    tall = jnp.concatenate([sums[:, p * tile : (p + 1) * tile] for p in range(parts)], axis=0)
    mixed = jnp.dot(
        tall, group_matrix(tile, size), precision=highest, preferred_element_type=f32
    )
    return jnp.concatenate([mixed[p * count : (p + 1) * count] for p in range(parts)], axis=1)


def sigmoid(v):
    return 1.0 / (1.0 + jnp.exp(-v))


def tiles_of(width):
    tile = min(width, 128)
    return [slice(p * tile, (p + 1) * tile) for p in range(width // tile)]


def split_store(product, rows, keep_ref, send_ref, neck):
    for j in range(keep_ref.shape[0]):
        keep_ref[j, rows, :] = product[:, 2 * j * neck : (2 * j + 1) * neck]
        send_ref[j, rows, :] = product[:, (2 * j + 1) * neck : (2 * j + 2) * neck].astype(bf16)


def front_kernel(obs_ref, w_ref, x_ref, keep_ref, send_ref):
    rows = obs_ref.shape[0]
    neck = keep_ref.shape[2]
    for i in range(rows // PIX):
        start = i * PIX
        base = start // 16 * 16
        length = min(144, rows - base)
        place = lax.broadcasted_iota(jnp.int32, (SLOT, length), 0)
        at = lax.broadcasted_iota(jnp.int32, (SLOT, length), 1)
        pick = ((at == place + (start - base)) & (place < PIX)).astype(bf16)
        image = jnp.dot(pick, obs_ref[base : base + length, :], preferred_element_type=f32)
        image = image.astype(bf16)
        here = slice(i * SLOT, (i + 1) * SLOT)
        x_ref[here, :] = image
        split_store(
            jnp.dot(image, w_ref[...], preferred_element_type=f32), here, keep_ref, send_ref, neck
        )


def convolve(source, table, images, s_ref, w_ref, cols_ref):
    for i in range(images):
        here = slice(i * SLOT, (i + 1) * SLOT)
        wide = jnp.dot(table, source[here, :], preferred_element_type=f32).astype(bf16)
        cols_ref[here, :] = jnp.concatenate(
            [wide[t * SLOT : (t + 1) * SLOT] for t in range(TAPS)], axis=1
        )


def bottle_kernel(save, *refs):
    own_ref, got_ref, gain_ref, w_ref, table_ref = refs[:5]
    two_ref = refs[5]
    if save:
        one_ref, a1_ref, a2_ref, stat_ref = refs[6:10]
        sum_ref, cols_ref = refs[10:]
    else:
        one_ref, a1_ref, a2_ref, stat_ref, sum_ref, cols_ref = refs[6:]
    rows, neck = own_ref.shape
    images = rows // SLOT
    size = NECK // GROUPS
    mask = pixel_mask()

    def norm(value_ref, gain_at, stat_at, out_ref):
        for i in range(images):
            here = slice(i * SLOT, (i + 1) * SLOT)
            sum_ref[i : i + 1, :] = jnp.sum(value_ref[here, :], axis=0, keepdims=True)
        mean = group_mix(sum_ref[...], size)
        for i in range(images):
            here = slice(i * SLOT, (i + 1) * SLOT)
            center = (value_ref[here, :] - mean[i : i + 1]) * mask
            sum_ref[i : i + 1, :] = jnp.sum(center * center, axis=0, keepdims=True)
        scale = lax.rsqrt(group_mix(sum_ref[...], size) + EPS)
        stat_ref[stat_at, :, :] = mean
        stat_ref[stat_at + 1, :, :] = scale
        for i in range(images):
            here = slice(i * SLOT, (i + 1) * SLOT)
            v = (value_ref[here, :] - mean[i : i + 1]) * scale[i : i + 1]
            v = v * gain_ref[gain_at : gain_at + 1, :] + gain_ref[gain_at + 1 : gain_at + 2, :]
            out_ref[here, :] = (v * sigmoid(v) * mask).astype(bf16)

    a1_ref[...] = own_ref[...] + got_ref[...].astype(f32)
    norm(a1_ref, 0, 0, one_ref)
    convolve(one_ref, table_ref[...], images, None, None, cols_ref)
    for i in range(images // 2):
        here = slice(i * 2 * SLOT, (i + 1) * 2 * SLOT)
        a2_ref[here, :] = jnp.dot(cols_ref[here, :], w_ref[...], preferred_element_type=f32)
    norm(a2_ref, 2, 2, two_ref)


def third_kernel(parts, last, save, *refs):
    chunks, (x_ref, w3_ref, gain_ref), refs = refs[:parts], refs[parts : parts + 3], refs[parts + 3 :]
    if not last:
        w1_ref, refs = refs[0], refs[1:]
        y_ref, low_ref, keep_ref, send_ref = refs[:4]
        refs = refs[4:]
    else:
        pool_ref, refs = refs[0], refs[1:]
    a3_ref, stat_ref, sum_ref = refs
    rows, width = x_ref.shape
    neck = chunks[0].shape[1]
    images = rows // SLOT
    size = WIDTH // GROUPS
    tiles = tiles_of(width)
    mask = pixel_mask()

    def product(i):
        here = rows_of(i, 2 * SLOT)
        left = jnp.concatenate([c[here, :] for c in chunks], axis=1)
        a3_ref[here, :] = jnp.dot(left, w3_ref[...], preferred_element_type=f32)

    each(images // 2, product)

    def add(i):
        for t in tiles:
            sum_ref[slice(i, i + 1), t] = jnp.sum(a3_ref[rows_of(i), t], axis=0, keepdims=True)

    each(images, add)
    stat_ref[0, :, :] = group_mix(sum_ref[...], size)

    def square(i):
        for t in tiles:
            center = (a3_ref[rows_of(i), t] - stat_ref[0, slice(i, i + 1), t]) * mask
            sum_ref[slice(i, i + 1), t] = jnp.sum(center * center, axis=0, keepdims=True)

    each(images, square)
    stat_ref[1, :, :] = lax.rsqrt(group_mix(sum_ref[...], size) + EPS)

    def finish(i):
        here = rows_of(i)
        for t in tiles:
            v = (a3_ref[here, t] - stat_ref[0, slice(i, i + 1), t]) * stat_ref[1, slice(i, i + 1), t]
            v = x_ref[here, t].astype(f32) + (v * gain_ref[0:1, t] + gain_ref[1:2, t])
            y = v * sigmoid(v) * mask
            if last:
                pool_ref[slice(i, i + 1), t] = jnp.sum(y, axis=0, keepdims=True) * (1.0 / PIX)
            else:
                y_ref[here, t] = y
                low_ref[here, t] = y.astype(bf16)

    each(images, finish)
    if not last:

        def first(i):
            here = rows_of(i, 2 * SLOT)
            got = jnp.dot(low_ref[here, :], w1_ref[...], preferred_element_type=f32)
            split_store(got, here, keep_ref, send_ref, neck)

        each(images // 2, first)


def outer_back_kernel(parts, top, *refs):
    if top:
        up_ref, refs = refs[0], refs[1:]
    else:
        up_ref, chunks, w1_ref = refs[0], refs[1 : 1 + parts], refs[1 + parts]
        refs = refs[2 + parts :]
    x_ref, a3_ref, stat_ref, gain_ref, w3_ref = refs[:5]
    keep_ref, send_ref, da3_ref, dgain_ref, dv_ref = refs[5:10]
    p_ref, q_ref = refs[10:12]
    rows, width = x_ref.shape
    neck = keep_ref.shape[2]
    images = rows // SLOT
    size = WIDTH // GROUPS
    tiles = tiles_of(width)
    mask = pixel_mask()
    if top:
        pooled = jnp.sum(up_ref[...].astype(f32), axis=0) * (1.0 / PIX)
        p_ref[...] = pooled
    else:

        def arrive(i):
            here = rows_of(i, 2 * SLOT)
            left = jnp.concatenate([c[here, :] for c in chunks], axis=1)
            dv_ref[here, :] = up_ref[here, :] + lax.dot_general(
                left, w1_ref[...], NT, preferred_element_type=f32
            )

        each(images // 2, arrive)

    def through(i):
        here = rows_of(i)
        one = slice(i, i + 1)
        for t in tiles:
            hat = (a3_ref[here, t] - stat_ref[0, one, t]) * stat_ref[1, one, t]
            v = x_ref[here, t].astype(f32) + (hat * gain_ref[0:1, t] + gain_ref[1:2, t])
            s = sigmoid(v)
            slope = s * (1.0 + v * (1.0 - s)) * mask
            dv = slope * (p_ref[one, t] if top else dv_ref[here, t])
            dv_ref[here, t] = dv
            q_ref[one, t] = jnp.sum(dv * hat, axis=0, keepdims=True)
            p_ref[one, t] = jnp.sum(dv, axis=0, keepdims=True)

    each(images, through)
    dgain_ref[0:1, :] = jnp.sum(q_ref[...], axis=0, keepdims=True)
    dgain_ref[1:2, :] = jnp.sum(p_ref[...], axis=0, keepdims=True)
    p_ref[...] = group_mix(p_ref[...] * gain_ref[0:1, :], size)
    q_ref[...] = group_mix(q_ref[...] * gain_ref[0:1, :], size)

    def finish(i):
        here = rows_of(i)
        one = slice(i, i + 1)
        for t in tiles:
            scale = stat_ref[1, one, t]
            hat = (a3_ref[here, t] - stat_ref[0, one, t]) * scale
            d = dv_ref[here, t] * gain_ref[0:1, t] - p_ref[one, t] - hat * q_ref[one, t]
            da3_ref[here, t] = (d * scale * mask).astype(bf16)

    each(images, finish)

    def project(i):
        here = rows_of(i, 2 * SLOT)
        got = lax.dot_general(da3_ref[here, :], w3_ref[...], NT, preferred_element_type=f32)
        split_store(got, here, keep_ref, send_ref, neck)

    each(images // 2, project)


def bottle_back_kernel(
    own_ref,
    got_ref,
    a1_ref,
    a2_ref,
    stat_ref,
    gain_ref,
    w_ref,
    table_ref,
    da1_ref,
    da2_ref,
    dgain_ref,
    work_ref,
    p_ref,
    q_ref,
    cols_ref,
):
    rows, neck = own_ref.shape
    images = rows // SLOT
    size = NECK // GROUPS
    mask = pixel_mask()

    def back(value_ref, at, out_ref):
        gain = gain_ref[at : at + 1, :]
        bias = gain_ref[at + 1 : at + 2, :]
        for i in range(images):
            here = slice(i * SLOT, (i + 1) * SLOT)
            hat = (value_ref[here, :] - stat_ref[at, i : i + 1, :]) * stat_ref[
                at + 1, i : i + 1, :
            ]
            v = hat * gain + bias
            s = sigmoid(v)
            dv = work_ref[here, :] * (s * (1.0 + v * (1.0 - s)) * mask)
            work_ref[here, :] = dv
            q_ref[i : i + 1, :] = jnp.sum(dv * hat, axis=0, keepdims=True)
            p_ref[i : i + 1, :] = jnp.sum(dv, axis=0, keepdims=True)
        dgain_ref[at : at + 1, :] = jnp.sum(q_ref[...], axis=0, keepdims=True)
        dgain_ref[at + 1 : at + 2, :] = jnp.sum(p_ref[...], axis=0, keepdims=True)
        mixed_p = group_mix(p_ref[...] * gain, size)
        mixed_q = group_mix(q_ref[...] * gain, size)
        for i in range(images):
            here = slice(i * SLOT, (i + 1) * SLOT)
            scale = stat_ref[at + 1, i : i + 1, :]
            hat = (value_ref[here, :] - stat_ref[at, i : i + 1, :]) * scale
            d = work_ref[here, :] * gain - mixed_p[i : i + 1] - hat * mixed_q[i : i + 1]
            out_ref[here, :] = (d * scale * mask).astype(bf16)

    work_ref[...] = own_ref[...] + got_ref[...].astype(f32)
    back(a2_ref, 2, da2_ref)
    convolve(da2_ref, table_ref[...], images, None, None, cols_ref)
    for i in range(images // 2):
        here = slice(i * 2 * SLOT, (i + 1) * 2 * SLOT)
        work_ref[here, :] = jnp.dot(cols_ref[here, :], w_ref[...], preferred_element_type=f32)
    back(a1_ref, 0, da1_ref)


def conv_grad_kernel(one_ref, da2_ref, table_ref, out_ref, acc_ref, cols_ref):
    rows, neck = one_ref.shape
    size = NECK // GROUPS
    convolve(da2_ref, table_ref[...], rows // SLOT, None, None, cols_ref)
    acc_ref[...] = lax.dot_general(one_ref[...], cols_ref[...], TN, preferred_element_type=f32)
    bits = size.bit_length() - 1
    row = lax.shift_right_logical(lax.broadcasted_iota(jnp.int32, (neck, neck), 0), bits)
    col = lax.shift_right_logical(lax.broadcasted_iota(jnp.int32, (neck, neck), 1), bits)
    same = row == col
    fold = (
        lax.broadcasted_iota(jnp.int32, (size, neck), 0)
        == (lax.broadcasted_iota(jnp.int32, (size, neck), 1) & (size - 1))
    ).astype(bf16)
    for t in range(TAPS):
        at = slice(t * neck, (t + 1) * neck)
        part = jnp.where(same, acc_ref[:, at], 0.0).astype(bf16)
        out_ref[:, at] = jnp.dot(fold, part, preferred_element_type=f32)


def left_grad_kernel(parts, *refs):
    chunks, da3_ref, out_ref = refs[:parts], refs[parts], refs[parts + 1]
    neck = chunks[0].shape[1]
    for k in range(parts):
        out_ref[k * neck : (k + 1) * neck, :] = lax.dot_general(
            chunks[k][...], da3_ref[...], TN, preferred_element_type=f32
        ).astype(bf16)


def right_grad_kernel(parts, *refs):
    x_ref, chunks, out_ref = refs[0], refs[1 : 1 + parts], refs[parts + 1]
    right = jnp.concatenate([c[...] for c in chunks], axis=1)
    for t in tiles_of(x_ref.shape[1]):
        out_ref[t, :] = lax.dot_general(
            x_ref[:, t], right, TN, preferred_element_type=f32
        ).astype(bf16)


def head_kernel(p_ref, own_ref, w_ref, out_ref, acc_ref):
    game = pl.program_id(0)

    @pl.when(game == 0)
    def _():
        acc_ref[...] = jnp.zeros_like(acc_ref)

    scores = jnp.dot(p_ref[...], w_ref[0].astype(bf16), preferred_element_type=f32)
    acc_ref[...] += jnp.where(own_ref[0] > 0.0, scores, 0.0)

    @pl.when(game == pl.num_programs(0) - 1)
    def _():
        out_ref[...] = acc_ref[...].reshape(out_ref.shape).astype(out_ref.dtype)


def head_back_kernel(g_ref, own_ref, w_ref, out_ref, acc_ref):
    game = pl.program_id(0)

    @pl.when(game == 0)
    def _():
        acc_ref[...] = jnp.zeros_like(acc_ref)

    grad = jnp.where(own_ref[0] > 0.0, g_ref[...], jnp.zeros_like(g_ref))
    acc_ref[...] += lax.dot_general(
        grad, w_ref[0].astype(bf16), NT, preferred_element_type=f32
    )

    @pl.when(game == pl.num_programs(0) - 1)
    def _():
        out_ref[...] = acc_ref[...].reshape(out_ref.shape).astype(out_ref.dtype)


def adamw(weight, first, second, grad, rate):
    momentum = 0.9 * first + 0.1 * grad
    variance = 0.999 * second + 0.001 * grad * grad
    scaled = momentum / (1.0 - 0.9**STEP) / (jnp.sqrt(variance / (1.0 - 0.999**STEP)) + 1e-08)
    return (weight - rate * (scaled + 0.1 * weight), momentum, variance)


def head_step_kernel(
    scale_ref, p_ref, own_ref, g_ref, w_ref, m_ref, v_ref, w_out, m_out, v_out
):
    left = jnp.where(own_ref[0] > 0.0, p_ref[...], jnp.zeros_like(p_ref))
    grad = jnp.dot(left, g_ref[...], preferred_element_type=f32) * scale_ref[0, 0]
    w_out[0], m_out[0], v_out[0] = adamw(w_ref[0], m_ref[0], v_ref[0], grad, rates[5])


def loss_kernel(total, part_ref, proj_ref, act_ref, legal_ref, own_ref, g_ref, loss_ref, l_ref):
    logits = jnp.sum(part_ref[...].astype(f32), axis=0)
    for a in range(ACTIONS):
        l_ref[a] = logits[:, a * ATOMS : (a + 1) * ATOMS]
    l = l_ref[...]
    count = l.shape[1]
    proj = proj_ref[...]
    own = own_ref[...]
    top = jnp.max(l, axis=2, keepdims=True)
    e = jnp.exp(l - top)
    s = jnp.sum(e, axis=2, keepdims=True)
    p = e / s
    logp = l - top - jnp.log(s)
    z = -10.0 + 20.0 * lax.broadcasted_iota(jnp.int32, (1, 1, ATOMS), 2).astype(f32) / (ATOMS - 1)
    q = jnp.sum(p * z, axis=2, keepdims=True)
    action = lax.broadcasted_iota(jnp.int32, (ACTIONS, count, 1), 0)
    hot = (action == act_ref[...][None]).astype(f32)
    legal = legal_ref[...]
    masked = jnp.where(legal > 0.0, q, -1e30)
    best = jnp.max(masked, axis=0, keepdims=True)
    ex = jnp.where(legal > 0.0, jnp.exp(masked - best), 0.0)
    tot = jnp.sum(ex, axis=0, keepdims=True)
    taken = jnp.sum(hot * logp, axis=0)
    cross = -jnp.sum(proj * taken, axis=1, keepdims=True)
    picked = jnp.sum(hot * q, axis=0)
    loss = cross + 0.05 * (best[0] + jnp.log(tot[0]) - picked)
    loss_ref[...] = loss * own
    mass = jnp.sum(proj, axis=1, keepdims=True)
    grad = hot * (p * mass[None] - proj[None]) + (0.05 * (ex / tot - hot)) * (p * (z - q))
    grad = grad * (own * (1.0 / total))[None]
    g_ref[...] = jnp.concatenate([grad[a] for a in range(ACTIONS)], axis=1).astype(bf16)


def flip(value, axis, size, bit):
    return lax.ppermute(value, axis, [(i, i ^ bit) for i in range(size)])


def bits_of(size):
    return [1 << b for b in range(size.bit_length() - 1)]


def scatter_chan(keep, send, size):
    for bit in bits_of(size):
        got = flip(send, "chan", size, bit)
        if keep.shape[0] == 1:
            return keep[0], got[0]
        total = keep + got.astype(f32)
        pairs = total.reshape(total.shape[0] // 2, 2, *total.shape[1:])
        keep, send = pairs[:, 0], pairs[:, 1].astype(bf16)


def gather_chan(own, size):
    chunks = {0: own}
    for bit in reversed(bits_of(size)):
        for k in list(chunks):
            chunks[k ^ bit] = flip(chunks[k], "chan", size, bit)
    return [chunks[k] for k in range(size)]


def scatter_dp(value, size):
    me = lax.axis_index("dp")
    keep = value
    for bit in bits_of(size):
        half = keep.shape[0] // 2
        low, high = keep[:half], keep[half:]
        upper = (me & bit) > 0
        send = jnp.where(upper, low, high).astype(bf16)
        keep = jnp.where(upper, high, low).astype(f32) + flip(send, "dp", size, bit).astype(f32)
    return keep


def gather_dp(value, size):
    me = lax.axis_index("dp")
    whole = value.astype(bf16)
    for bit in reversed(bits_of(size)):
        got = flip(whole, "dp", size, bit)
        upper = (me & bit) > 0
        whole = jnp.concatenate(
            [jnp.where(upper, got, whole), jnp.where(upper, whole, got)], axis=0
        )
    return whole


def sum_all(value, sizes):
    for axis, size in sizes:
        for bit in bits_of(size):
            value = value + flip(value, axis, size, bit)
    return value


def swap_chunks(value, axis, size):
    me = lax.axis_index("chan")
    width = value.shape[axis] // size
    return jnp.concatenate(
        [
            lax.dynamic_slice_in_dim(value, (me ^ k) * width, width, axis=axis)
            for k in range(size)
        ],
        axis=axis,
    )


def conv_weights(weight, neck):
    size = NECK // GROUPS
    taps = weight.astype(bf16).reshape(LAYERS, neck, TAPS, size).transpose(0, 2, 3, 1)
    wide = jnp.tile(taps, (1, 1, neck // size, 1))
    place = np.arange(neck) // size
    same = jnp.asarray(place[:, None] == place[None, :])
    wide = jnp.where(same, wide, jnp.zeros_like(wide))
    back = wide[:, ::-1].swapaxes(2, 3)
    return (
        wide.reshape(LAYERS, TAPS * neck, neck),
        back.reshape(LAYERS, TAPS * neck, neck),
    )


def body(
    obs_now,
    obs_next,
    games,
    actions,
    next_actions,
    legal,
    done,
    proj_index,
    proj_frac,
    weight_in,
    weight_mid,
    weight_out,
    bottle_gains,
    stream_gains,
    weight_head,
    first_in,
    first_mid,
    first_out,
    first_bottle,
    first_stream,
    first_head,
    second_in,
    second_mid,
    second_out,
    second_bottle,
    second_stream,
    second_head,
    target_in,
    target_mid,
    target_out,
    target_bottle,
    target_stream,
    target_head,
):
    n_chan, n_dp = lax.axis_size("chan"), lax.axis_size("dp")
    chan_at, dp_at = lax.axis_index("chan"), lax.axis_index("dp")
    width = obs_now.shape[1]
    neck = weight_mid.shape[1]
    images = obs_now.shape[0] // PIX
    rows = images * SLOT
    half = n_chan // 2
    big = 2 * rows * width * NECK
    table = jnp.asarray(shift_matrices(), bf16)

    def front(obs, w_first):
        return call(
            front_kernel,
            (
                shape((rows, width), bf16),
                shape((half, rows, neck), f32),
                shape((half, rows, neck), bf16),
            ),
            flops=big,
        )(obs, w_first)

    def bottle(own, got, gains, w_conv, save):
        held = (
            (shape((rows, neck), bf16), pltpu.VMEM((rows, neck), bf16)),
            (shape((rows, neck), f32), pltpu.VMEM((rows, neck), f32)),
            (shape((rows, neck), f32), pltpu.VMEM((rows, neck), f32)),
            (shape((4, images, neck), f32), pltpu.VMEM((4, images, neck), f32)),
        )
        scratch = [pltpu.VMEM((images, neck), f32), pltpu.VMEM((rows, TAPS * neck), bf16)]
        outs = [shape((rows, neck), bf16)]
        if save:
            outs += [h[0] for h in held]
        else:
            scratch = [h[1] for h in held] + scratch
        return call(functools.partial(bottle_kernel, save), tuple(outs), scratch, flops=big)(
            own, got, gains, w_conv, table
        )

    def third(chunks, stream, w_last, gains, w_first, save):
        last = w_first is None
        held = (
            (shape((rows, width), f32), pltpu.VMEM((rows, width), f32)),
            (shape((2, images, width), f32), pltpu.VMEM((2, images, width), f32)),
        )
        scratch = [pltpu.VMEM((images, width), f32)]
        if last:
            outs = [shape((images, width), f32)]
        else:
            outs = [
                shape((rows, width), f32),
                shape((rows, width), bf16),
                shape((half, rows, neck), f32),
                shape((half, rows, neck), bf16),
            ]
        if save:
            outs += [h[0] for h in held]
        else:
            scratch = [h[1] for h in held] + scratch
        args = [*chunks, stream, w_last, gains] + ([] if last else [w_first])
        return call(
            functools.partial(third_kernel, n_chan, last, save), tuple(outs), scratch, flops=2 * big
        )(*args)

    def torso(obs, w_first, w_conv, w_last, bottles, outers, save):
        x, keep, send = front(obs, w_first[0])
        stream, low = x, x
        kept = []
        for layer in range(LAYERS):
            own, got = scatter_chan(keep, send, n_chan)
            two, *inner = bottle(own, got, bottles[layer], w_conv[layer], save)
            chunks = gather_chan(two, n_chan)
            last = layer == LAYERS - 1
            out = third(
                chunks,
                stream,
                w_last[layer],
                outers[layer],
                None if last else w_first[layer + 1],
                save,
            )
            kept.append((stream, low, inner, chunks, out[-2:]))
            if last:
                return out[0], kept
            stream, low, keep, send = out[:4]

    def relative(w_first, w_last):
        return (
            [swap_chunks(w_first[layer], 1, n_chan).astype(bf16) for layer in range(LAYERS)],
            [swap_chunks(w_last[layer], 0, n_chan).astype(bf16) for layer in range(LAYERS)],
        )

    on_in, on_out = relative(weight_in, weight_out)
    on_mid, on_back = conv_weights(weight_mid, neck)
    tg_in, tg_out = relative(target_in, target_out)
    tg_mid, _ = conv_weights(target_mid, neck)
    pooled_next, _ = torso(
        obs_next, tg_in, tg_mid, tg_out, target_bottle, target_stream, False
    )
    pooled_now, kept = torso(
        obs_now, on_in, on_mid, on_out, bottle_gains, stream_gains, True
    )

    local_games, shard, outputs = weight_head.shape
    count = actions.shape[0]
    total = count * n_dp
    owner = (
        games[:, None] == chan_at * local_games + jnp.arange(local_games)[None, :]
    ).astype(f32)
    own_cols = owner.T[:, :, None]
    own_rows = owner.T[:, None, :]
    mine = jnp.sum(lax.dynamic_slice_in_dim(owner, dp_at * count, count, 0), axis=1, keepdims=True)

    def head_call(kernel, outs, acc, flops, *args):
        left, own, weights = args
        return pl.pallas_call(
            kernel,
            grid=(local_games,),
            in_specs=[
                pl.BlockSpec(left.shape, lambda g: (0, 0)),
                pl.BlockSpec((1, total, 1), lambda g: (g, 0, 0)),
                pl.BlockSpec((1, shard, outputs), lambda g: (g, 0, 0)),
            ],
            out_specs=pl.BlockSpec(outs.shape, lambda g: (0, 0, 0)),
            out_shape=outs,
            scratch_shapes=[pltpu.VMEM(acc, f32)],
            compiler_params=pltpu.CompilerParams(vmem_limit_bytes=48 * 1024 * 1024),
            cost_estimate=pl.CostEstimate(
                flops=flops, bytes_accessed=weights.size * 4, transcendentals=0
            ),
        )(*args)

    head_flops = 2 * total * shard * outputs * local_games

    def columns(pooled):
        full = lax.all_gather(pooled.astype(bf16), "chan", axis=1, tiled=True)
        return lax.all_to_all(full, "dp", split_axis=1, concat_axis=0, tiled=True)

    def logits_parts(cols, weights):
        part = head_call(
            head_kernel,
            shape((n_dp, count, outputs), bf16),
            (total, outputs),
            head_flops,
            cols,
            own_cols,
            weights,
        )
        return lax.all_to_all(part, "dp", split_axis=0, concat_axis=0, tiled=True)

    parts_next = logits_parts(columns(pooled_next), target_head)
    logits_next = jnp.sum(parts_next.astype(f32), axis=0).reshape(count, ACTIONS, ATOMS)
    range_a = jnp.arange(ACTIONS)
    chosen = jnp.sum(
        jnp.where((range_a[None, :] == next_actions[:, None])[:, :, None], logits_next, 0.0), axis=1
    )
    chosen = jax.nn.softmax(chosen, axis=-1)
    source = jnp.where(done[:, None] > 0, 1.0 / ATOMS, chosen)
    atoms = jnp.arange(ATOMS)
    lower = jnp.where(proj_index[:, :, None] == atoms[None, None, :], proj_frac[:, :, None], 0.0)
    upper = jnp.where(
        proj_index[:, :, None] + 1 == atoms[None, None, :], 1.0 - proj_frac[:, :, None], 0.0
    )
    projected = jnp.sum(source[:, :, None] * (lower + upper), axis=1)

    cols_now = columns(pooled_now)
    parts_now = logits_parts(cols_now, weight_head)
    grad_rows, losses = call(
        functools.partial(loss_kernel, total),
        (shape((count, outputs), bf16), shape((count, 1), f32)),
        [pltpu.VMEM((ACTIONS, count, ATOMS), f32)],
    )(
        parts_now,
        projected,
        actions[:, None],
        legal.astype(f32).T[:, :, None],
        mine,
    )
    spread = jnp.broadcast_to(grad_rows[None], (n_dp, count, outputs))
    all_grad = lax.all_to_all(spread, "dp", split_axis=0, concat_axis=0, tiled=True)
    all_grad = all_grad.reshape(total, outputs)
    d_cols = head_call(
        head_back_kernel,
        shape((n_dp, count, shard), bf16),
        (total, shard),
        head_flops,
        all_grad,
        own_cols,
        weight_head,
    )
    d_rows = lax.all_to_all(d_cols, "dp", split_axis=0, concat_axis=0, tiled=True)
    d_rows = d_rows.transpose(1, 0, 2).reshape(count, n_chan, width).transpose(1, 0, 2)
    upstream = lax.all_to_all(d_rows, "chan", split_axis=0, concat_axis=0, tiled=True)

    same = jnp.dot(owner, owner.T, precision=highest)
    inner_p = lax.dot_general(cols_now, cols_now, NT, preferred_element_type=f32)
    inner_g = lax.dot_general(all_grad, all_grad, NT, preferred_element_type=f32)
    squares = jnp.sum(same * inner_p * inner_g)

    reduced = []
    chain = None
    for layer in reversed(range(LAYERS)):
        stream, low, (one, a1, a2, stats), chunks, (a3, stats3) = kept[layer]
        top = layer == LAYERS - 1
        lead = [upstream] if top else [d_stream, *whole, on_in[layer + 1]]
        dv_out = layer > 0
        outs = [
            shape((half, rows, neck), f32),
            shape((half, rows, neck), bf16),
            shape((rows, width), bf16),
            shape((2, width), f32),
        ]
        scratch = [pltpu.VMEM((images, width), f32), pltpu.VMEM((images, width), f32)]
        if dv_out:
            outs.append(shape((rows, width), f32))
        else:
            scratch.insert(0, pltpu.VMEM((rows, width), f32))
        keep, send, da3, d_outer, *rest = call(
            functools.partial(outer_back_kernel, n_chan, top), tuple(outs), scratch, flops=2 * big
        )(*lead, stream, a3, stats3, stream_gains[layer], on_out[layer])
        if dv_out:
            d_stream = rest[0]
        own, got = scatter_chan(keep, send, n_chan)
        d_last = call(
            functools.partial(left_grad_kernel, n_chan), shape((NECK, width), bf16), flops=big
        )(*chunks, da3)
        da1, da2, d_bottle = call(
            bottle_back_kernel,
            (
                shape((rows, neck), bf16),
                shape((rows, neck), bf16),
                shape((4, neck), f32),
            ),
            [
                pltpu.VMEM((rows, neck), f32),
                pltpu.VMEM((images, neck), f32),
                pltpu.VMEM((images, neck), f32),
                pltpu.VMEM((rows, TAPS * neck), bf16),
            ],
            flops=big,
        )(own, got, a1, a2, stats, bottle_gains[layer], on_back[layer], table)
        whole = gather_chan(da1, n_chan)
        d_conv = call(
            conv_grad_kernel,
            shape((NECK // GROUPS, TAPS * neck), f32),
            [pltpu.VMEM((neck, TAPS * neck), f32), pltpu.VMEM((rows, TAPS * neck), bf16)],
            flops=big,
        )(one, da2, table)
        d_first = call(
            functools.partial(right_grad_kernel, n_chan), shape((width, NECK), bf16), flops=big
        )(low, *whole)
        flat = jnp.concatenate(
            [d_conv.reshape(-1), d_outer.reshape(-1), d_bottle.reshape(-1)]
        ).astype(bf16)
        flat = jnp.pad(flat, (0, 64 * 512 - flat.shape[0])).reshape(64, 512)
        tail = jnp.concatenate([d_first.reshape(-1, 512), flat], axis=0)
        part_last = scatter_dp(d_last.reshape(-1, 512), n_dp)
        part_tail = scatter_dp(tail, n_dp)
        squares = squares + jnp.sum(part_last * part_last) + jnp.sum(part_tail * part_tail)
        reduced.insert(0, (part_last, part_tail))

    scalars = jnp.stack([squares, jnp.sum(losses)])
    scalars = jnp.pad(scalars, (0, 126)).reshape(1, 128)
    scalars = sum_all(scalars, (("chan", n_chan), ("dp", n_dp)))
    gradient_norm = jnp.sqrt(scalars[0, 0])
    loss_sum = scalars[0, 1]
    scale = jnp.minimum(1.0, 0.01 / (gradient_norm + 1e-06))

    block = pl.BlockSpec((1, shard, outputs), lambda g: (g, 0, 0))
    head_out = pl.pallas_call(
        head_step_kernel,
        grid=(local_games,),
        in_specs=[
            pl.BlockSpec(memory_space=pltpu.SMEM),
            pl.BlockSpec((shard, total), lambda g: (0, 0)),
            pl.BlockSpec((1, 1, total), lambda g: (g, 0, 0)),
            pl.BlockSpec((total, outputs), lambda g: (0, 0)),
            block,
            block,
            block,
        ],
        out_specs=[block, block, block],
        out_shape=[shape(weight_head.shape, f32)] * 3,
        compiler_params=pltpu.CompilerParams(vmem_limit_bytes=48 * 1024 * 1024),
        cost_estimate=pl.CostEstimate(
            flops=head_flops, bytes_accessed=weight_head.size * 24, transcendentals=0
        ),
    )(
        scale.reshape(1, 1),
        cols_now.T,
        own_rows,
        all_grad,
        weight_head,
        first_head,
        second_head,
    )

    grads = [[], [], [], [], []]
    for part_last, part_tail in reduced:
        last = gather_dp(part_last, n_dp).reshape(NECK, width).astype(f32)
        tail = gather_dp(part_tail, n_dp)
        split = tail.shape[0] - 64
        first = tail[:split].reshape(width, NECK).astype(f32)
        flat = tail[split:].reshape(-1).astype(f32)
        grads[0].append(swap_chunks(first, 1, n_chan))
        grads[2].append(swap_chunks(last, 0, n_chan))
        size = NECK // GROUPS
        ends = np.cumsum([size * TAPS * neck, 2 * width, 4 * neck])
        conv = flat[: ends[0]].reshape(size, TAPS, neck)[:, ::-1].transpose(2, 1, 0)
        grads[1].append(conv.reshape(neck, TAPS * size))
        grads[4].append(flat[ends[0] : ends[1]].reshape(2, width))
        grads[3].append(flat[ends[1] : ends[2]].reshape(4, neck))
    params = (weight_in, weight_mid, weight_out, bottle_gains, stream_gains)
    firsts = (first_in, first_mid, first_out, first_bottle, first_stream)
    seconds = (second_in, second_mid, second_out, second_bottle, second_stream)
    result = []
    for weight, first, second, grad, rate in zip(params, firsts, seconds, grads, rates):
        result.extend(adamw(weight, first, second, jnp.stack(grad) * scale, rate))
    return (*result, *head_out, gradient_norm, loss_sum)


def solution(mesh):
    rows = P("dp", "chan")
    third = P(None, None, "chan")
    second = P(None, "chan", None)
    heads = P("chan", "dp", None)
    torso = (second, second, third, third, third, heads)
    placed = (
        rows,
        rows,
        P(),
        P("dp"),
        P("dp"),
        P("dp", None),
        P("dp"),
        P("dp", None),
        P("dp", None),
        *torso,
        *torso,
        *torso,
        *torso,
    )
    outs = tuple(spec for spec in torso for _ in range(3)) + (P(), P())
    return jax.shard_map(body, mesh=mesh, in_specs=placed, out_specs=outs, check_vma=False)
```

```python
import functools

import jax
import jax.numpy as jnp
from jax import lax
from jax.experimental import pallas as pl
from jax.experimental.pallas import tpu as pltpu
from jax.sharding import PartitionSpec as P

WIDTH = 2048
NECK = 512
GROUPS = 32
LAYERS = 2
ACTIONS = 18
ATOMS = 51
MAP = 11
PIX = 121
STEP = 10
SLOT = 128
TAPS = 9
EPS = 1e-05
VMEM = 20 * 1024 * 1024
WIDE = 44 * 1024 * 1024

bf16 = jnp.bfloat16
f32 = jnp.float32
highest = lax.Precision.HIGHEST
rates = (0.02, 0.08, 0.02, 0.5, 0.5, 0.02)

NT = (((1,), (1,)), ((), ()))
TN = (((0,), (0,)), ((), ()))


WHOLE = pl.BlockSpec(memory_space=pltpu.VMEM)
SCALARS = pl.BlockSpec(memory_space=pltpu.SMEM)
DISTANT = pl.BlockSpec(memory_space=pltpu.HBM)


def call(kernel, ins, outs, scratch, flops, moves, limit=VMEM):
    return pl.pallas_call(
        kernel,
        in_specs=[spec for spec, _ in ins],
        out_specs=tuple(spec for spec, _ in outs),
        out_shape=tuple(
            pltpu.HBM(out.shape, out.dtype) if spec is DISTANT else out for spec, out in outs
        ),
        scratch_shapes=[*scratch, pltpu.SemaphoreType.DMA((moves,))],
        compiler_params=pltpu.CompilerParams(vmem_limit_bytes=limit),
        cost_estimate=pl.CostEstimate(
            flops=flops, bytes_accessed=12 * 1024 * 1024, transcendentals=0
        ),
    )(
        *(
            pltpu.with_memory_space_constraint(array, pltpu.HBM) if spec is DISTANT else array
            for spec, array in ins
        )
    )


def shape(dims, dtype):
    return jax.ShapeDtypeStruct(dims, dtype)


class Moves:
    def __init__(self, sems):
        self.sems, self.count = sems, 0

    def __call__(self, source, target):
        copy = pltpu.make_async_copy(source, target, self.sems.at[self.count])
        self.count += 1
        copy.start()
        return copy


def rows_of(i, count=SLOT):
    return slice(i * count, (i + 1) * count)


def pixel_mask():
    return (lax.broadcasted_iota(jnp.int32, (SLOT, 1), 0) < PIX).astype(f32)


def same_group(width, size):
    bits = size.bit_length() - 1
    row = lax.shift_right_logical(lax.broadcasted_iota(jnp.int32, (width, width), 0), bits)
    col = lax.shift_right_logical(lax.broadcasted_iota(jnp.int32, (width, width), 1), bits)
    return row == col


def group_mix(sums, size):
    count, width = sums.shape
    tile = min(width, 128)
    parts = width // tile
    tall = jnp.concatenate([sums[:, p * tile : (p + 1) * tile] for p in range(parts)], axis=0)
    matrix = jnp.where(same_group(tile, size), 1.0 / (size * PIX), 0.0).astype(f32)
    mixed = jnp.dot(tall, matrix, precision=highest, preferred_element_type=f32)
    return jnp.concatenate([mixed[p * count : (p + 1) * count] for p in range(parts)], axis=1)


def sigmoid(v):
    return 1.0 / (1.0 + jnp.exp(-v))


def tiles_of(width):
    tile = min(width, 128)
    return [slice(p * tile, (p + 1) * tile) for p in range(width // tile)]


def to_column(row):
    n = row.shape[1]
    diagonal = lax.broadcasted_iota(jnp.int32, (n, n), 0) == lax.broadcasted_iota(
        jnp.int32, (n, n), 1
    )
    return jnp.sum(jnp.where(diagonal, row, 0.0), axis=1, keepdims=True)


def split_store(product, rows, keep_refs, send_refs, neck):
    for j in range(len(keep_refs)):
        send_refs[j][rows, :] = product[:, (2 * j + 1) * neck : (2 * j + 2) * neck].astype(bf16)
        keep_refs[j][rows, :] = product[:, 2 * j * neck : (2 * j + 1) * neck]


def own_order_columns(me, w_ref, neck):
    if neck % 128:
        return w_ref[...].astype(bf16)
    picks = [
        w_ref[:, pl.ds(pl.multiple_of((me ^ k) * neck, neck), neck)].astype(bf16)
        for k in range(w_ref.shape[1] // neck)
    ]
    return jnp.concatenate(picks, axis=1)


def own_order_rows(me, w_ref, neck):
    picks = [
        w_ref[pl.ds(pl.multiple_of((me ^ k) * neck, neck), neck), :].astype(bf16)
        for k in range(w_ref.shape[0] // neck)
    ]
    return jnp.concatenate(picks, axis=0)


def tap_weights(mid_ref):
    size = NECK // GROUPS
    neck = mid_ref.shape[1]
    same = same_group(neck, size)
    mid = mid_ref[...].astype(f32)
    return [
        jnp.where(
            same,
            jnp.concatenate([mid[t * size : (t + 1) * size]] * (neck // size), axis=0),
            0.0,
        ).astype(bf16)
        for t in range(TAPS)
    ]


def shift_table():
    place = lax.broadcasted_iota(jnp.int32, (SLOT, SLOT), 0)
    at = lax.broadcasted_iota(jnp.int32, (SLOT, SLOT), 1)
    line = lax.shift_right_logical(place * 373, 12)
    column = place - line * MAP
    tables = []
    for tap in range(TAPS):
        down, right = tap // 3 - 1, tap % 3 - 1
        inside = (line + down >= 0) & (line + down < MAP) & (place < PIX)
        inside = inside & (column + right >= 0) & (column + right < MAP)
        tables.append(jnp.where(inside & (at == place + (down * MAP + right)), 1.0, 0.0))
    return jnp.concatenate(tables, axis=0).astype(bf16)


def convolve(source, images, cols_ref):
    table = shift_table()
    for i in range(images):
        here = rows_of(i)
        wide = jnp.dot(table, source[here, :], preferred_element_type=f32).astype(bf16)
        cols_ref[here, :] = jnp.concatenate([wide[rows_of(t)] for t in range(TAPS)], axis=1)


def add_terms(term_refs):
    total = term_refs[0][...]
    for term_ref in term_refs[1:]:
        total = total + term_ref[...].astype(f32)
    return total


def padded_image(obs_ref, i):
    start = i * PIX
    base = start // 16 * 16
    length = min(144, obs_ref.shape[0] - base)
    place = lax.broadcasted_iota(jnp.int32, (SLOT, length), 0)
    at = lax.broadcasted_iota(jnp.int32, (SLOT, length), 1)
    pick = ((at == place + (start - base)) & (place < PIX)).astype(bf16)
    image = jnp.dot(pick, obs_ref[base : base + length, :], preferred_element_type=f32)
    return image.astype(bf16)


def front_kernel(parts, me_ref, obs_hbm, w_hbm, *refs):
    half = parts // 2
    keep_refs, send_refs, (obs_ref, w_ref, sems) = refs[:half], refs[half:parts], refs[parts:]
    move = Moves(sems)
    obs_in = move(obs_hbm, obs_ref)
    w_in = move(w_hbm.at[0], w_ref)
    rows = obs_ref.shape[0]
    neck = keep_refs[0].shape[1]
    w_in.wait()
    weight = own_order_columns(me_ref[0], w_ref, neck)
    obs_in.wait()
    for i in range(rows // PIX):
        image = padded_image(obs_ref, i)
        got = jnp.dot(image, weight, preferred_element_type=f32)
        split_store(got, rows_of(i), keep_refs, send_refs, neck)


def bottle_kernel(layer, terms, save, *refs):
    term_refs, (gain_hbm, mid_hbm), refs = refs[:terms], refs[terms : terms + 2], refs[terms + 2 :]
    two_ref, refs = refs[0], refs[1:]
    saved, refs = (refs[:4], refs[4:]) if save else ((), refs)
    one_ref, a1_ref, a2_ref, stat_ref, sum_ref, cols_ref, gain_ref, mid_ref, sems = refs
    move = Moves(sems)
    gain_in = move(gain_hbm.at[layer], gain_ref)
    mid_in = move(mid_hbm.at[layer], mid_ref)
    rows, neck = a1_ref.shape
    images = rows // SLOT
    size = NECK // GROUPS
    mask = pixel_mask()
    out = []

    def norm(value_ref, at, out_ref):
        for i in range(images):
            sum_ref[i : i + 1, :] = jnp.sum(value_ref[rows_of(i), :], axis=0, keepdims=True)
        mean = group_mix(sum_ref[...], size)
        for i in range(images):
            center = (value_ref[rows_of(i), :] - mean[i : i + 1]) * mask
            sum_ref[i : i + 1, :] = jnp.sum(center * center, axis=0, keepdims=True)
        scale = lax.rsqrt(group_mix(sum_ref[...], size) + EPS)
        stat_ref[at, :, :] = mean
        stat_ref[at + 1, :, :] = scale
        for i in range(images):
            here = rows_of(i)
            v = (value_ref[here, :] - mean[i : i + 1]) * scale[i : i + 1]
            v = v * gain_ref[at : at + 1, :] + gain_ref[at + 1 : at + 2, :]
            out_ref[here, :] = (v * sigmoid(v) * mask).astype(bf16)

    a1_ref[...] = add_terms(term_refs)
    if save:
        out.append(move(a1_ref, saved[1]))
    gain_in.wait()
    norm(a1_ref, 0, one_ref)
    if save:
        out.append(move(one_ref, saved[0]))
    convolve(one_ref, images, cols_ref)
    mid_in.wait()
    weight = jnp.concatenate(tap_weights(mid_ref), axis=0)
    for i in range(images // 2):
        here = rows_of(i, 2 * SLOT)
        a2_ref[here, :] = jnp.dot(cols_ref[here, :], weight, preferred_element_type=f32)
    if save:
        out.append(move(a2_ref, saved[2]))
    norm(a2_ref, 2, two_ref)
    if save:
        out.append(move(stat_ref, saved[3]))
    for copy in out:
        copy.wait()


def third_kernel(layer, parts, last, save, me_ref, *refs):
    chunks, (x_hbm, w3_hbm, gain_hbm, extra_ref), refs = (
        refs[:parts],
        refs[parts : parts + 4],
        refs[parts + 4 :],
    )
    half = parts // 2
    if last:
        pool_ref, refs = refs[0], refs[1:]
    else:
        y_hbm, keep_refs, send_refs = refs[0], refs[1 : 1 + half], refs[1 + half : 1 + parts]
        refs = refs[1 + parts :]
    saved, refs = (refs[: 2 if last else 3], refs[2 if last else 3 :]) if save else ((), refs)
    a3_ref, stat_ref, sum_ref, x_ref, w3_ref, gain_ref, *refs, sems = refs
    move = Moves(sems)
    w3_in = move(w3_hbm.at[layer], w3_ref)
    gain_in = move(gain_hbm.at[layer], gain_ref)
    x_in = move(x_hbm, x_ref)
    if not last:
        y_ref, low_ref, w1_ref = refs
        w1_in = move(extra_ref.at[layer + 1], w1_ref)
    rows, width = a3_ref.shape
    neck = chunks[0].shape[1]
    images = rows // SLOT
    size = WIDTH // GROUPS
    tiles = tiles_of(width)
    mask = pixel_mask()
    out = []
    w3_in.wait()
    third_weight = own_order_rows(me_ref[0], w3_ref, neck)
    for i in range(images // 2):
        here = rows_of(i, 2 * SLOT)
        left = jnp.concatenate([c[here, :] for c in chunks], axis=1)
        a3_ref[here, :] = jnp.dot(left, third_weight, preferred_element_type=f32)
    if save:
        out.append(move(a3_ref, saved[0]))
    for i in range(images):
        for t in tiles:
            sum_ref[i : i + 1, t] = jnp.sum(a3_ref[rows_of(i), t], axis=0, keepdims=True)
    stat_ref[0, :, :] = group_mix(sum_ref[...], size)
    for i in range(images):
        for t in tiles:
            center = (a3_ref[rows_of(i), t] - stat_ref[0, i : i + 1, t]) * mask
            sum_ref[i : i + 1, t] = jnp.sum(center * center, axis=0, keepdims=True)
    stat_ref[1, :, :] = lax.rsqrt(group_mix(sum_ref[...], size) + EPS)
    if save:
        out.append(move(stat_ref, saved[1]))
    gain_in.wait()
    x_in.wait()
    if not last:
        w1_in.wait()
        first_weight = own_order_columns(me_ref[0], w1_ref, neck)
    for i in range(images):
        here = rows_of(i)
        if layer == 0:
            low_ref[here, :] = padded_image(x_ref, i)
        for t in tiles:
            x = low_ref[here, t].astype(f32) if layer == 0 else x_ref[here, t]
            v = (a3_ref[here, t] - stat_ref[0, i : i + 1, t]) * stat_ref[1, i : i + 1, t]
            v = x + (v * gain_ref[0:1, t] + gain_ref[1:2, t])
            y = v * sigmoid(v) * mask
            if last:
                sum_ref[i : i + 1, t] = jnp.sum(y, axis=0, keepdims=True) * (1.0 / PIX)
            else:
                y_ref[here, t] = y
                low_ref[here, t] = y.astype(bf16)
        if not last and i % 2:
            both = rows_of(i // 2, 2 * SLOT)
            out.append(move(y_ref.at[both], y_hbm.at[both]))
            got = jnp.dot(low_ref[both, :], first_weight, preferred_element_type=f32)
            split_store(got, both, keep_refs, send_refs, neck)
    if last:
        shard = pool_ref.shape[3]
        for e in range(width // shard):
            pool_ref[e, 0] = sum_ref[:, e * shard : (e + 1) * shard].astype(bf16)
            pool_ref[e, 1] = extra_ref[e, 0]
    elif save:
        out.append(move(low_ref, saved[2]))
    for copy in out:
        copy.wait()


def outer_back_kernel(layer, parts, top, me_ref, *refs):
    half = parts // 2
    if top:
        up_ref, refs = refs[0], refs[1:]
    else:
        up_hbm, chunks, w1_hbm = refs[0], refs[1 : 1 + parts], refs[1 + parts]
        refs = refs[2 + parts :]
    x_hbm, a3_hbm, stat_hbm, gain_hbm, w3_hbm = refs[:5]
    keep_refs, send_refs, refs = refs[5 : 5 + half], refs[5 + half : 5 + parts], refs[5 + parts :]
    da3_hbm, dgain_hbm, refs = refs[0], refs[1], refs[2:]
    if layer > 0:
        dv_hbm, refs = refs[0], refs[1:]
    x_ref, a3_ref, stat_ref, gain_ref, w3_ref, da3_ref, dgain_ref, dv_ref, p_ref, q_ref = refs[:10]
    *refs, sems = refs[10:]
    move = Moves(sems)
    if not top:
        up_ref, w1_ref = refs
        w1_in = move(w1_hbm.at[layer + 1], w1_ref)
        up_in = move(up_hbm, up_ref)
    early = [
        move(stat_hbm, stat_ref),
        move(gain_hbm.at[layer], gain_ref),
        move(a3_hbm, a3_ref),
        move(x_hbm, x_ref),
    ]
    w3_in = move(w3_hbm.at[layer], w3_ref)
    rows, width = a3_ref.shape
    neck = keep_refs[0].shape[1]
    images = rows // SLOT
    size = WIDTH // GROUPS
    tiles = tiles_of(width)
    mask = pixel_mask()
    out = []
    if top:
        pooled = jnp.sum(up_ref[...].astype(f32), axis=0) * (1.0 / PIX)
        p_ref[...] = jnp.concatenate([pooled[e] for e in range(pooled.shape[0])], axis=1)
    else:
        w1_in.wait()
        first_weight = own_order_columns(me_ref[0], w1_ref, neck)
        up_in.wait()
        for i in range(images // 2):
            here = rows_of(i, 2 * SLOT)
            left = jnp.concatenate([c[here, :] for c in chunks], axis=1)
            dv_ref[here, :] = up_ref[here, :] + lax.dot_general(
                left, first_weight, NT, preferred_element_type=f32
            )
    for copy in early:
        copy.wait()
    for i in range(images):
        here, one = rows_of(i), slice(i, i + 1)
        if layer == 0:
            da3_ref[here, :] = padded_image(x_ref, i)
        for t in tiles:
            x = da3_ref[here, t].astype(f32) if layer == 0 else x_ref[here, t]
            hat = (a3_ref[here, t] - stat_ref[0, one, t]) * stat_ref[1, one, t]
            v = x + (hat * gain_ref[0:1, t] + gain_ref[1:2, t])
            s = sigmoid(v)
            slope = s * (1.0 + v * (1.0 - s)) * mask
            dv = slope * (p_ref[one, t] if top else dv_ref[here, t])
            dv_ref[here, t] = dv
            q_ref[one, t] = jnp.sum(dv * hat, axis=0, keepdims=True)
            p_ref[one, t] = jnp.sum(dv, axis=0, keepdims=True)
    if layer > 0:
        out.append(move(dv_ref, dv_hbm))
    dgain_ref[0:1, :] = jnp.sum(q_ref[...], axis=0, keepdims=True)
    dgain_ref[1:2, :] = jnp.sum(p_ref[...], axis=0, keepdims=True)
    out.append(move(dgain_ref, dgain_hbm))
    p_ref[...] = group_mix(p_ref[...] * gain_ref[0:1, :], size)
    q_ref[...] = group_mix(q_ref[...] * gain_ref[0:1, :], size)
    w3_in.wait()
    third_weight = own_order_rows(me_ref[0], w3_ref, neck)
    for i in range(images):
        here, one = rows_of(i), slice(i, i + 1)
        for t in tiles:
            scale = stat_ref[1, one, t]
            hat = (a3_ref[here, t] - stat_ref[0, one, t]) * scale
            d = dv_ref[here, t] * gain_ref[0:1, t] - p_ref[one, t] - hat * q_ref[one, t]
            da3_ref[here, t] = (d * scale * mask).astype(bf16)
        if i % 2:
            both = rows_of(i // 2, 2 * SLOT)
            got = lax.dot_general(da3_ref[both, :], third_weight, NT, preferred_element_type=f32)
            split_store(got, both, keep_refs, send_refs, neck)
    out.append(move(da3_ref, da3_hbm))
    for copy in out:
        copy.wait()


def bottle_back_kernel(layer, terms, *refs):
    term_refs = refs[:terms]
    a1_hbm, a2_hbm, stat_hbm, gain_hbm, mid_hbm = refs[terms : terms + 5]
    da1_ref, da2_hbm, dgain_hbm = refs[terms + 5 : terms + 8]
    a1_ref, a2_ref, stat_ref, gain_ref, mid_ref = refs[terms + 8 : terms + 13]
    da2_ref, dgain_ref, work_ref, p_ref, q_ref, cols_ref, sems = refs[terms + 13 :]
    move = Moves(sems)
    early = [
        move(stat_hbm, stat_ref),
        move(gain_hbm.at[layer], gain_ref),
        move(a2_hbm, a2_ref),
    ]
    a1_in = move(a1_hbm, a1_ref)
    mid_in = move(mid_hbm.at[layer], mid_ref)
    rows, neck = a1_ref.shape
    images = rows // SLOT
    size = NECK // GROUPS
    mask = pixel_mask()

    def back(value_ref, at, out_ref):
        gain = gain_ref[at : at + 1, :]
        bias = gain_ref[at + 1 : at + 2, :]
        for i in range(images):
            here, one = rows_of(i), slice(i, i + 1)
            hat = (value_ref[here, :] - stat_ref[at, one, :]) * stat_ref[at + 1, one, :]
            v = hat * gain + bias
            s = sigmoid(v)
            dv = work_ref[here, :] * (s * (1.0 + v * (1.0 - s)) * mask)
            work_ref[here, :] = dv
            q_ref[one, :] = jnp.sum(dv * hat, axis=0, keepdims=True)
            p_ref[one, :] = jnp.sum(dv, axis=0, keepdims=True)
        dgain_ref[at : at + 1, :] = jnp.sum(q_ref[...], axis=0, keepdims=True)
        dgain_ref[at + 1 : at + 2, :] = jnp.sum(p_ref[...], axis=0, keepdims=True)
        mixed_p = group_mix(p_ref[...] * gain, size)
        mixed_q = group_mix(q_ref[...] * gain, size)
        for i in range(images):
            here, one = rows_of(i), slice(i, i + 1)
            scale = stat_ref[at + 1, one, :]
            hat = (value_ref[here, :] - stat_ref[at, one, :]) * scale
            d = work_ref[here, :] * gain - mixed_p[one] - hat * mixed_q[one]
            out_ref[here, :] = (d * scale * mask).astype(bf16)

    work_ref[...] = add_terms(term_refs)
    for copy in early:
        copy.wait()
    back(a2_ref, 2, da2_ref)
    out = [move(da2_ref, da2_hbm)]
    convolve(da2_ref, images, cols_ref)
    mid_in.wait()
    weight = jnp.concatenate(tap_weights(mid_ref)[::-1], axis=1)
    for i in range(images // 2):
        here = rows_of(i, 2 * SLOT)
        work_ref[here, :] = lax.dot_general(
            cols_ref[here, :], weight, NT, preferred_element_type=f32
        )
    a1_in.wait()
    back(a1_ref, 0, da1_ref)
    out.append(move(dgain_ref, dgain_hbm))
    for copy in out:
        copy.wait()


def small_grad_kernel(
    one_hbm,
    da2_hbm,
    bottle_hbm,
    outer_hbm,
    out_hbm,
    one_ref,
    da2_ref,
    bottle_ref,
    outer_ref,
    out_ref,
    acc_ref,
    cols_ref,
    sems,
):
    move = Moves(sems)
    da2_in = move(da2_hbm, da2_ref)
    early = [move(one_hbm, one_ref), move(bottle_hbm, bottle_ref), move(outer_hbm, outer_ref)]
    rows, neck = one_ref.shape
    size = NECK // GROUPS
    da2_in.wait()
    convolve(da2_ref, rows // SLOT, cols_ref)
    for copy in early:
        copy.wait()
    acc_ref[...] = lax.dot_general(one_ref[...], cols_ref[...], TN, preferred_element_type=f32)
    same = same_group(neck, size)
    fold = (
        lax.broadcasted_iota(jnp.int32, (size, neck), 0)
        == (lax.broadcasted_iota(jnp.int32, (size, neck), 1) & (size - 1))
    ).astype(bf16)
    out_ref[...] = jnp.zeros_like(out_ref)
    for t in range(TAPS):
        part = jnp.where(same, acc_ref[:, t * neck : (t + 1) * neck], 0.0).astype(bf16)
        to = TAPS - 1 - t
        rows_at = slice(to % 3 * size, (to % 3 + 1) * size)
        out_ref[rows_at, to // 3 * neck : (to // 3 + 1) * neck] = jnp.dot(
            fold, part, preferred_element_type=f32
        ).astype(bf16)
    out_ref[0:4, 3 * neck : 4 * neck] = bottle_ref[...].astype(bf16)
    out_ref[48:50, 0 : outer_ref.shape[1]] = outer_ref[...].astype(bf16)
    move(out_ref, out_hbm).wait()


def last_grad_kernel(parts, *refs):
    hbm, out_hbm, refs = refs[: parts + 1], refs[parts + 1], refs[parts + 2 :]
    vmem, out_ref, sems = refs[: parts + 1], refs[parts + 1], refs[parts + 2]
    move = Moves(sems)
    da3_in = move(hbm[parts], vmem[parts])
    ins = [move(source, target) for source, target in zip(hbm[:parts], vmem[:parts])]
    neck = vmem[0].shape[1]
    da3_in.wait()
    out = []
    for k in range(parts):
        ins[k].wait()
        at = slice(k * neck, (k + 1) * neck)
        out_ref[at, :] = lax.dot_general(
            vmem[k][...], vmem[parts][...], TN, preferred_element_type=f32
        ).astype(bf16)
        out.append(move(out_ref.at[at], out_hbm.at[at]))
    for copy in out:
        copy.wait()


def first_grad_kernel(layer, parts, *refs):
    hbm, out_hbm, refs = refs[: parts + 2], refs[parts + 2], refs[parts + 3 :]
    vmem, (right_ref, out_ref, *wide, sems) = refs[: parts + 1], refs[parts + 1 :]
    move = Moves(sems)
    ins = [move(source, target) for source, target in zip(hbm[: parts + 1], vmem)]
    neck, width = vmem[1].shape[1], vmem[0].shape[1]
    small = move(hbm[parts + 1], out_ref.at[width : width + 64])
    for k in range(parts):
        ins[k + 1].wait()
        right_ref[:, k * neck : (k + 1) * neck] = vmem[k + 1][...]
    ins[0].wait()
    left_ref = vmem[0]
    if layer == 0:
        left_ref = wide[0]
        for i in range(left_ref.shape[0] // SLOT):
            left_ref[rows_of(i), :] = padded_image(vmem[0], i)
    small.wait()
    out = [move(out_ref.at[width : width + 64], out_hbm.at[width : width + 64])]
    for t in tiles_of(width):
        out_ref[t, :] = lax.dot_general(
            left_ref[:, t], right_ref[...], TN, preferred_element_type=f32
        ).astype(bf16)
        out.append(move(out_ref.at[t], out_hbm.at[t]))
    for copy in out:
        copy.wait()


def head_kernel(me_ref, games_ref, p_ref, w_hbm, target_hbm, out_ref, now_hbm, *refs):
    now_ref, later_ref, w_ref, target_ref, acc_ref, sems = refs
    move = Moves(sems)
    count = w_hbm.shape[0]
    ins = [
        (move(w_hbm.at[g], w_ref.at[g]), move(target_hbm.at[g], target_ref.at[g]))
        for g in range(count)
    ]
    for at, cols_ref in enumerate((now_ref, later_ref)):
        cols_ref[...] = p_ref[:, at].astype(f32).reshape(cols_ref.shape).astype(bf16)
    out = move(now_ref, now_hbm)
    base = me_ref[0] * count
    acc_ref[...] = jnp.zeros_like(acc_ref)
    total, outputs = games_ref.shape[1], w_hbm.shape[1]
    for g in range(count):
        own = games_ref[...] == base + g
        for at, (cols, weight) in enumerate(((now_ref, w_ref), (later_ref, target_ref))):
            ins[g][at].wait()
            scores = lax.dot_general(
                weight[g].astype(bf16), cols[...], NT, preferred_element_type=f32
            )
            acc_ref[at, 0:outputs, 0:total] += jnp.where(own, scores, 0.0)
    parts, _, rows, _ = out_ref.shape
    for at in range(2):
        logits = acc_ref[at].T[0:total, 0:outputs]
        out_ref[:, at] = logits.reshape(parts, rows, outputs).astype(out_ref.dtype)
    out.wait()


def head_back_kernel(
    me_ref, games_ref, spread_ref, now_hbm, w_hbm, out_ref, g_hbm, square_hbm, *refs
):
    now_ref, g_ref, square_ref, w_ref, acc_ref, sems = refs
    move = Moves(sems)
    count = w_hbm.shape[0]
    ins = [move(w_hbm.at[g], w_ref.at[g]) for g in range(count)]
    now_in = move(now_hbm, now_ref)
    g_ref[...] = spread_ref[...].astype(f32).reshape(g_ref.shape).astype(bf16)
    out = [move(g_ref, g_hbm)]
    row = games_ref[...].astype(f32)
    game = to_column(row)
    base = me_ref[0] * count
    now_in.wait()
    inner_p = lax.dot_general(now_ref[...], now_ref[...], NT, preferred_element_type=f32)
    inner_g = lax.dot_general(g_ref[...], g_ref[...], NT, preferred_element_type=f32)
    low = base.astype(f32)
    pair = (game == row) & (row >= low) & (row < low + count)
    square_ref[...] = jnp.sum(jnp.where(pair, inner_p * inner_g, 0.0), axis=0, keepdims=True)
    out.append(move(square_ref, square_hbm))
    acc_ref[...] = jnp.zeros_like(acc_ref)
    for g in range(count):
        grad = jnp.where(game == low + g, g_ref[...], jnp.zeros_like(g_ref))
        ins[g].wait()
        acc_ref[...] += jnp.dot(grad, w_ref[g].astype(bf16), preferred_element_type=f32)
    out_ref[...] = acc_ref[...].reshape(out_ref.shape).astype(out_ref.dtype)
    for copy in out:
        copy.wait()


def adamw(weight, first, second, grad, rate):
    momentum = 0.9 * first + 0.1 * grad
    variance = 0.999 * second + 0.001 * grad * grad
    root = jnp.sqrt(variance * (1.0 / (1.0 - 0.999**STEP))) + 1e-08
    scaled = (momentum * (1.0 / (1.0 - 0.9**STEP))) / root
    return (weight - rate * (scaled + 0.1 * weight), momentum, variance)


def head_step_kernel(
    me_ref, scale_ref, games_ref, p_ref, g_ref, w_hbm, m_hbm, v_hbm, w_out, m_out, v_out, *refs
):
    old, new, sems = refs[:3], refs[3:6], refs[6]
    move = Moves(sems)
    count = w_hbm.shape[0]
    slots = new[0].shape[0]
    base = me_ref[0] * count
    ins = [
        [move(source.at[g], ref.at[g]) for source, ref in zip((w_hbm, m_hbm, v_hbm), old)]
        for g in range(count)
    ]
    outs = []
    for g in range(count):
        left = jnp.where(games_ref[...] == base + g, g_ref[...], jnp.zeros_like(g_ref))
        grad = jnp.dot(left, p_ref[...], preferred_element_type=f32) * scale_ref[0, 0]
        for copy in ins[g]:
            copy.wait()
        if g >= slots:
            for copy in outs[g - slots]:
                copy.wait()
        made = adamw(*(ref[g] for ref in old), grad, rates[5])
        for ref, value in zip(new, made):
            ref[g % slots] = value
        outs.append(
            [
                move(ref.at[g % slots], target.at[g])
                for ref, target in zip(new, (w_out, m_out, v_out))
            ]
        )
    for group in outs[-slots:]:
        for copy in group:
            copy.wait()


def torso_step_kernel(parts, me_ref, scale_ref, *refs):
    grads_hbm, refs = refs[: 2 * LAYERS], refs[2 * LAYERS :]
    old_hbm, new_hbm, refs = refs[:15], refs[15:30], refs[30:]
    first_refs, last_refs, refs = refs[:LAYERS], refs[LAYERS : 2 * LAYERS], refs[2 * LAYERS :]
    old, new, sems = refs[:15], refs[15:30], refs[30]
    move = Moves(sems)
    grads_in = [move(a, b) for a, b in zip(grads_hbm, (*first_refs, *last_refs))]
    ins = [move(old_hbm[k], old[k]) for k in range(15)]
    for copy in grads_in:
        copy.wait()
    me, scale = me_ref[0], scale_ref[0, 0]
    width = first_refs[0].shape[0] - 64
    size = NECK // GROUPS
    neck = NECK // parts
    outs = []

    def step(which, at, grad):
        k = 3 * which
        made = adamw(*(ref[at] for ref in old[k : k + 3]), grad.astype(f32) * scale, rates[which])
        for ref, value in zip(new[k : k + 3], made):
            ref[at] = value

    for copy in ins[3:6] + ins[9:15]:
        copy.wait()
    for layer in range(LAYERS):
        small = first_refs[layer]
        for k in range(3):
            taps = slice(k * 3 * size, (k + 1) * 3 * size)
            step(
                1, (layer, taps), small[width : width + 3 * size, k * neck : (k + 1) * neck]
            )
        step(3, (layer,), small[width : width + 16, 3 * neck : 4 * neck][0:4])
        step(4, (layer,), small[width + 48 : width + 64, 0:width][0:2])
    for k in (*range(3, 6), *range(9, 15)):
        outs.append(move(new[k], new_hbm[k]))
    for which, grad_refs in ((0, first_refs), (2, last_refs)):
        for copy in ins[3 * which : 3 * which + 3]:
            copy.wait()
        for layer in range(LAYERS):
            for q in range(parts):
                chunk = slice(q * neck, (q + 1) * neck)
                from_ = pl.ds(pl.multiple_of((me ^ q) * neck, neck), neck)
                if which:
                    step(which, (layer, chunk), grad_refs[layer][from_, :])
                elif neck % 128:
                    step(which, (layer, slice(None), chunk), grad_refs[layer][0:width, chunk])
                else:
                    step(which, (layer, slice(None), chunk), grad_refs[layer][0:width, from_])
            for k in range(3 * which, 3 * which + 3):
                outs.append(move(new[k].at[layer], new_hbm[k].at[layer]))
    for copy in outs:
        copy.wait()


def loss_kernel(total, me_ref, *refs):
    part_ref, hbm, (g_ref, loss_hbm), refs = refs[0], refs[1:8], refs[8:10], refs[10:]
    vmem, (loss_ref, l_ref, sems) = refs[:7], refs[7:]
    move = Moves(sems)
    for copy in [move(source, target) for source, target in zip(hbm, vmem)]:
        copy.wait()
    act_row, next_row, done_row, game_row, legal, index, share = (ref[...] for ref in vmem)
    act, later_act, done, game = (
        to_column(row.astype(f32)) for row in (act_row, next_row, done_row, game_row)
    )
    count = act.shape[0]
    first = me_ref[1].astype(f32)
    own = ((game >= first) & (game < first + me_ref[2].astype(f32))).astype(f32)
    later = jnp.sum(part_ref[:, 1].astype(f32), axis=0)
    chosen = jnp.zeros((count, ATOMS), f32)
    for a in range(ACTIONS):
        chosen = jnp.where(later_act == a, later[:, a * ATOMS : (a + 1) * ATOMS], chosen)
    source = jnp.exp(chosen - jnp.max(chosen, axis=1, keepdims=True))
    source = source / jnp.sum(source, axis=1, keepdims=True)
    source = jnp.where(done > 0.0, 1.0 / ATOMS, source)
    atom = lax.broadcasted_iota(jnp.int32, (count, ATOMS), 1)
    lower, upper = source * share, source * (1.0 - share)
    proj = jnp.zeros((count, ATOMS), f32)
    for j in range(ATOMS):
        gap = atom - index[:, j : j + 1]
        proj = proj + jnp.where(
            gap == 0, lower[:, j : j + 1], jnp.where(gap == 1, upper[:, j : j + 1], 0.0)
        )
    logits = jnp.sum(part_ref[:, 0].astype(f32), axis=0)
    for a in range(ACTIONS):
        l_ref[a] = logits[:, a * ATOMS : (a + 1) * ATOMS]
    l = l_ref[...]
    top = jnp.max(l, axis=2, keepdims=True)
    e = jnp.exp(l - top)
    s = jnp.sum(e, axis=2, keepdims=True)
    p = e / s
    logp = l - top - jnp.log(s)
    z = -10.0 + 20.0 * lax.broadcasted_iota(jnp.int32, (1, 1, ATOMS), 2).astype(f32) / (ATOMS - 1)
    q = jnp.sum(p * z, axis=2, keepdims=True)
    action = lax.broadcasted_iota(jnp.int32, (ACTIONS, count, 1), 0).astype(f32)
    hot = (action == act[None]).astype(f32)
    allowed = jnp.concatenate([legal[:, a : a + 1][None] for a in range(ACTIONS)], axis=0) > 0
    masked = jnp.where(allowed, q, -1e30)
    best = jnp.max(masked, axis=0, keepdims=True)
    ex = jnp.where(allowed, jnp.exp(masked - best), 0.0)
    tot = jnp.sum(ex, axis=0, keepdims=True)
    taken = jnp.sum(hot * logp, axis=0)
    cross = -jnp.sum(proj * taken, axis=1, keepdims=True)
    picked = jnp.sum(hot * q, axis=0)
    loss = cross + 0.05 * (best[0] + jnp.log(tot[0]) - picked)
    loss_ref[...] = jnp.broadcast_to(loss * own, loss_ref.shape)
    mass = jnp.sum(proj, axis=1, keepdims=True)
    grad = hot * (p * mass[None] - proj[None]) + (0.05 * (ex / tot - hot)) * (p * (z - q))
    grad = grad * (own * (1.0 / total))[None]
    flat = jnp.concatenate([grad[a] for a in range(ACTIONS)], axis=1).astype(bf16)
    for k in range(g_ref.shape[0]):
        g_ref[k] = flat
    move(loss_ref, loss_hbm).wait()


def flip(value, axis, size, bit):
    return lax.ppermute(value, axis, [(i, i ^ bit) for i in range(size)])


def bits_of(size):
    return [1 << b for b in range(size.bit_length() - 1)]


def after(value, *tokens):
    return lax.optimization_barrier((value, *tokens))[0]


def after_all(token, *values):
    return lax.optimization_barrier((*values, token))[:-1]


def scatter_chan(keeps, sends, size):
    half = size // 2
    terms = {j: [keeps[j]] for j in range(half)}
    for j in reversed(range(half)):
        terms[j].append(flip(sends[j], "chan", size, 1))
    sent = []
    for bit in bits_of(size)[1:]:
        step = bit // 2
        for j in sorted(terms, reverse=True):
            if j & step:
                whole, *rest = terms.pop(j)
                for term in rest:
                    whole = whole + term.astype(f32)
                sent.append(whole.astype(bf16))
                terms[j - step].append(flip(sent[-1], "chan", size, bit))
    return terms[0], sent[-1]


def gather_chan(own, size, *hold):
    chunks = {0: own}
    for bit in reversed(bits_of(size)):
        for k in list(chunks):
            value = after(chunks[k], *hold) if k else own
            chunks[k ^ bit] = flip(value, "chan", size, bit)
    return [chunks[k] for k in range(size)]


class Spread:
    def __init__(self, value, size):
        self.value = value.reshape(size, value.shape[0] // size, value.shape[1])
        self.size = size
        self.left = bits_of(size)
        self.me = lax.axis_index("dp")

    def send(self):
        bit = self.left.pop(0)
        pieces, *rest = self.value.shape
        paired = self.value.reshape(pieces // 2, 2, *rest)
        mine = ((self.me & bit) > 0).astype(jnp.int32)
        part = lambda at: lax.dynamic_index_in_dim(paired, at, 1, keepdims=False)
        self.keep = part(mine).astype(f32)
        self.sent = part(1 - mine).astype(bf16)
        self.got = flip(self.sent, "dp", self.size, bit)
        return self

    def add(self, *hold):
        got = after(self.got, *hold) if hold else self.got
        self.value = self.keep + got.astype(f32)
        self.sent = None
        if self.left:
            self.send()
        return self

    def finish(self, *hold):
        self.add(*hold)
        while self.sent is not None:
            self.add()
        return self


class Collect:
    def __init__(self, value, size, *hold):
        self.size, self.left = size, bits_of(size)
        self.me = lax.axis_index("dp")
        self.value = value.astype(bf16)
        self.send(*hold)

    def send(self, *hold):
        self.bit = self.left.pop()
        self.sent = after(self.value, *hold) if hold else self.value
        self.got = flip(self.sent, "dp", self.size, self.bit)

    def join(self, *hold):
        got = after(self.got, *hold) if hold else self.got
        upper = (self.me & self.bit) > 0
        pair = jnp.stack(
            [jnp.where(upper, got, self.value), jnp.where(upper, self.value, got)], axis=1
        )
        self.value = pair.reshape(2 * got.shape[0], *got.shape[1:])
        if self.left:
            self.send()
        return self

    def finish(self, *hold):
        while self.left:
            self.join(*hold)
        return self.join(*hold).value


def sum_all(value, sizes):
    for axis, size in sizes:
        for bit in bits_of(size):
            value = value + flip(value, axis, size, bit)
    return value


def swap_chunks(value, axis, size):
    me = lax.axis_index("chan")
    width = value.shape[axis] // size
    return jnp.concatenate(
        [
            lax.dynamic_slice_in_dim(value, (me ^ k) * width, width, axis=axis)
            for k in range(size)
        ],
        axis=axis,
    )


def body(
    obs_now,
    obs_next,
    games,
    actions,
    next_actions,
    legal,
    done,
    proj_index,
    proj_frac,
    weight_in,
    weight_mid,
    weight_out,
    bottle_gains,
    stream_gains,
    weight_head,
    first_in,
    first_mid,
    first_out,
    first_bottle,
    first_stream,
    first_head,
    second_in,
    second_mid,
    second_out,
    second_bottle,
    second_stream,
    second_head,
    target_in,
    target_mid,
    target_out,
    target_bottle,
    target_stream,
    target_head,
):
    n_chan, n_dp = lax.axis_size("chan"), lax.axis_size("dp")
    chan_at, dp_at = lax.axis_index("chan"), lax.axis_index("dp")
    width = obs_now.shape[1]
    neck = weight_mid.shape[1]
    images = obs_now.shape[0] // PIX
    rows = images * SLOT
    half = n_chan // 2
    big = 2 * rows * width * NECK
    local_games, shard, outputs = weight_head.shape
    count = actions.shape[0]
    total = count * n_dp
    me = jnp.stack([chan_at, chan_at * local_games, local_games]).astype(jnp.int32)
    turn = lambda array: array.swapaxes(1, 2)
    wide = shape((rows, width), f32)
    wide_low = shape((rows, width), bf16)
    slim = shape((rows, neck), f32)
    slim_low = shape((rows, neck), bf16)
    split_outs = [(WHOLE, slim)] * half + [(WHOLE, slim_low)] * half
    weights = shape((width, NECK), f32)

    def scratch(*shapes):
        return [pltpu.VMEM(s.shape, s.dtype) for s in shapes]

    def like(array):
        return shape(array.shape[1:], array.dtype)

    def here(*arrays):
        return [(WHOLE, array) for array in arrays]

    def far(*arrays):
        return [(DISTANT, array) for array in arrays]

    def columns(weight):
        return weight if neck % 128 == 0 else swap_chunks(weight, 2, n_chan)

    def front(obs, nets):
        return call(
            functools.partial(front_kernel, n_chan),
            [(SCALARS, me), *far(obs, nets[0])],
            split_outs,
            scratch(obs, like(nets[0])),
            big,
            2,
        )

    def bottle(layer, terms, nets, save):
        stats = shape((4, images, neck), f32)
        outs = [(WHOLE, slim_low)]
        if save:
            outs += far(slim_low, slim, slim, stats)
        return call(
            functools.partial(bottle_kernel, layer, len(terms), save),
            [*here(*terms), *far(nets[3], nets[1])],
            outs,
            scratch(
                slim_low,
                slim,
                slim,
                stats,
                shape((images, neck), f32),
                shape((rows, TAPS * neck), bf16),
                like(nets[3]),
                like(nets[1]),
            ),
            big,
            6 if save else 2,
        )

    def third(layer, chunks, stream, nets, save, other=None):
        last = layer == LAYERS - 1
        stats = shape((2, images, width), f32)
        keep = scratch(
            wide,
            stats,
            shape((images, width), f32),
            stream,
            like(nets[2]),
            like(nets[4]),
        )
        if last:
            outs = [(WHOLE, shape((width // shard, 2, images, shard), bf16))]
            extra = (WHOLE, other)
        else:
            outs = [(DISTANT, wide), *split_outs]
            extra = (DISTANT, nets[0])
            keep += scratch(wide, wide_low, like(nets[0]))
        if save:
            outs += far(wide, stats) if last else far(wide, stats, wide_low)
        return call(
            functools.partial(third_kernel, layer, n_chan, last, save),
            [(SCALARS, me), *here(*chunks), *far(stream, nets[2], nets[4]), extra],
            outs,
            keep,
            2 * big,
            (3 if last else 4 + images // 2) + (2 + (not last)) * save,
        )

    online = (columns(weight_in), turn(weight_mid), weight_out, bottle_gains, stream_gains)
    target = (columns(target_in), turn(target_mid), target_out, target_bottle, target_stream)

    stream_n, stream_o, low_o = obs_next, obs_now, obs_now
    split_n = front(obs_next, target)
    terms_n, sent_n = scatter_chan(split_n[:half], split_n[half:], n_chan)
    split_o = front(after(obs_now, split_n[0]), online)
    terms_o, sent_o = scatter_chan(split_o[:half], split_o[half:], n_chan)
    kept = []
    for layer in range(LAYERS):
        terms_n[-1] = after(terms_n[-1], sent_o)
        (two_n,) = bottle(layer, terms_n, target, False)
        terms_o[-1] = after(terms_o[-1], two_n)
        two_o, *inner = bottle(layer, terms_o, online, True)
        chunks_n = gather_chan(two_n, n_chan, two_o)
        if layer < LAYERS - 1:
            stream_n, *split_n = third(layer, chunks_n, stream_n, target, False)
            terms_n, sent_n = scatter_chan(split_n[:half], split_n[half:], n_chan)
            chunks_o = gather_chan(two_o, n_chan, split_n[0])
            chunks_o[0] = after(chunks_o[0], sent_n)
            got = third(layer, chunks_o, stream_o, online, True)
            kept.append((stream_o, low_o, inner, chunks_o, got[1 + n_chan : 3 + n_chan]))
            stream_o, low_o, split_o = got[0], got[-1], list(got[1 : 1 + n_chan])
            split_o[half:] = [after(part, terms_n[-1]) for part in split_o[half:]]
            terms_o, sent_o = scatter_chan(split_o[:half], split_o[half:], n_chan)
        else:
            empty = jnp.zeros((width // shard, 2, images, shard), bf16)
            (pooled,) = third(layer, chunks_n, stream_n, target, False, empty)
            chunks_o = gather_chan(two_o, n_chan, pooled)
            pooled, *saved = third(layer, chunks_o, stream_o, online, True, pooled)
            kept.append((stream_o, low_o, inner, chunks_o, saved))

    row = games.reshape(1, total)
    mine = lax.dynamic_slice_in_dim(row, dp_at * count, count, 1)
    heads_online, heads_target = turn(weight_head), turn(target_head)
    head_flops = 2 * total * shard * outputs * local_games
    cols_shape = shape((total, shard), bf16)
    grad_shape = shape((total, outputs), bf16)

    pooled = lax.all_gather(pooled, "chan", axis=0, tiled=True)
    cols = lax.all_to_all(pooled, "dp", split_axis=0, concat_axis=0, tiled=True)
    parts, cols_now = call(
        head_kernel,
        [(SCALARS, me), *here(row, cols), *far(heads_online, heads_target)],
        [(WHOLE, shape((n_dp, 2, count, outputs), bf16)), (DISTANT, cols_shape)],
        scratch(
            cols_shape,
            cols_shape,
            heads_online,
            heads_target,
            shape((2, -(-outputs // 128) * 128, max(total, 128)), f32),
        ),
        2 * head_flops,
        2 * local_games + 1,
        WIDE,
    )
    parts = lax.all_to_all(parts, "dp", split_axis=0, concat_axis=0, tiled=True)
    facts = (
        actions.reshape(1, count),
        next_actions.reshape(1, count),
        done.reshape(1, count),
        mine,
        legal,
        proj_index,
        proj_frac,
    )
    losses_shape = shape((count, 128), f32)
    spread, losses = call(
        functools.partial(loss_kernel, total),
        [(SCALARS, me), (WHOLE, parts), *far(*facts)],
        [(WHOLE, shape((n_dp, count, outputs), bf16)), (DISTANT, losses_shape)],
        scratch(*facts, losses_shape, shape((ACTIONS, count, ATOMS), f32)),
        big,
        8,
    )
    spread = lax.all_to_all(spread, "dp", split_axis=0, concat_axis=0, tiled=True)
    d_cols, all_grad, square_head = call(
        head_back_kernel,
        [(SCALARS, me), *here(row, spread), *far(cols_now, heads_online)],
        [
            (WHOLE, shape((n_dp, count, shard), bf16)),
            *far(grad_shape, shape((1, total), f32)),
        ],
        scratch(
            cols_shape,
            grad_shape,
            shape((1, total), f32),
            heads_online,
            shape((total, shard), f32),
        ),
        head_flops,
        local_games + 3,
        WIDE,
    )
    d_rows = lax.all_to_all(d_cols, "dp", split_axis=0, concat_axis=0, tiled=True)
    d_rows = d_rows.reshape(n_chan, n_dp // n_chan, count, shard)
    upstream = lax.all_to_all(d_rows, "chan", split_axis=0, concat_axis=0, tiled=True)

    def outer_back(layer, lead):
        stream, _, _, _, (a3, stats3) = kept[layer]
        gains = shape((2, width), f32)
        outs = [*split_outs, *far(wide_low, gains)]
        if layer > 0:
            outs += far(wide)
        keep = scratch(
            stream,
            wide,
            stats3,
            like(stream_gains),
            like(weight_out),
            wide_low,
            gains,
            wide,
            shape((images, width), f32),
            shape((images, width), f32),
        )
        top = layer == LAYERS - 1
        if not top:
            keep += scratch(wide, like(online[0]))
        return call(
            functools.partial(outer_back_kernel, layer, n_chan, top),
            [(SCALARS, me), *lead, *far(stream, a3, stats3, stream_gains, weight_out)],
            outs,
            keep,
            2 * big,
            7 + (layer > 0) + 2 * (not top),
        )

    def bottle_back(layer, terms):
        _, _, (_, a1, a2, stats), _, _ = kept[layer]
        gains = shape((4, neck), f32)
        sums_shape = shape((images, neck), f32)
        return call(
            functools.partial(bottle_back_kernel, layer, len(terms)),
            [*here(*terms), *far(a1, a2, stats, bottle_gains, online[1])],
            [(WHOLE, slim_low), *far(slim_low, gains)],
            scratch(
                slim,
                slim,
                stats,
                like(bottle_gains),
                like(online[1]),
                slim_low,
                gains,
                slim,
                sums_shape,
                sums_shape,
                shape((rows, TAPS * neck), bf16),
            ),
            big,
            7,
        )

    def small_grad(layer, da2, d_bottle, d_outer):
        ins = (kept[layer][2][0], da2, d_bottle, d_outer)
        out = shape((64, NECK), bf16)
        (got,) = call(
            small_grad_kernel,
            far(*ins),
            far(out),
            scratch(
                *ins,
                out,
                shape((neck, TAPS * neck), f32),
                shape((rows, TAPS * neck), bf16),
            ),
            big,
            5,
        )
        return got

    def last_grad_of(layer, da3):
        ins = (*kept[layer][3], da3)
        out = shape((NECK, width), bf16)
        (got,) = call(
            functools.partial(last_grad_kernel, n_chan),
            far(*ins),
            far(out),
            scratch(*ins, out),
            big,
            2 * n_chan + 1,
        )
        return got.reshape(-1, NECK)

    def first_grad_of(layer, chunks, small):
        ins = (kept[layer][1], *chunks)
        out = shape((width + 64, NECK), bf16)
        (got,) = call(
            functools.partial(first_grad_kernel, layer, n_chan),
            far(*ins, small),
            far(out),
            scratch(*ins, shape((rows, NECK), bf16), out, *([] if layer else [wide_low])),
            big,
            n_chan + 3 + max(width // 128, 1),
        )
        return got

    lead = here(upstream)
    above = None
    for layer in reversed(range(LAYERS)):
        got = outer_back(layer, lead)
        da3, d_outer, *rest = got[n_chan:]
        terms, sent = scatter_chan(got[:half], got[half:n_chan], n_chan)
        last = Spread(last_grad_of(layer, after(da3, sent)), n_dp).send()
        hold = [last.sent]
        if above:
            first = Spread(first_grad_of(layer + 1, chunks, after(small, last.sent)), n_dp).send()
            above.finish(first.sent)
            top_last = Collect(above.value, n_dp)
            hold = [first.sent, top_last.sent]
        terms[-1] = after(terms[-1], *hold)
        da1, da2, d_bottle = bottle_back(layer, terms)
        last.add(da1)
        hold = [last.sent]
        if above:
            first.add(last.sent)
            top_last.join(first.sent)
            hold = [first.sent, top_last.sent]
        small = small_grad(layer, after(da2, *hold), d_bottle, d_outer)
        last.add(small)
        hold = [last.sent]
        if above:
            first.add(last.sent)
            hold = [first.sent]
        chunks = gather_chan(da1, n_chan, *hold)
        if layer:
            above = last
            lead = [*far(rest[0]), *here(*chunks), *far(online[0])]
    final = Spread(after(first_grad_of(0, chunks, small), *hold), n_dp).send()
    last.finish(final.sent)
    first.finish(final.sent)
    most = [s.value[0].astype(bf16) for s in (last, first)]
    most = Collect(jnp.concatenate(most, axis=0)[None], n_dp)
    top_last.join(most.sent)
    squares = jnp.sum(square_head)
    for s in (above, last, first):
        squares = squares + jnp.sum(s.value * s.value)
    final.add(squares)
    most.join(final.sent)
    final.add(most.sent)
    most.join(final.sent)
    final.finish(most.sent)
    squares = squares + jnp.sum(final.value * final.value)
    below = Collect(final.value, n_dp, squares)

    scalars = jnp.stack([squares, jnp.sum(losses[:, 0])])
    scalars = jnp.pad(scalars, (0, 126)).reshape(1, 128)
    scalars = sum_all(scalars, (("chan", n_chan),))
    for bit in (*bits_of(n_dp)[1:], 1):
        scalars = scalars + flip(scalars, "dp", n_dp, bit)
        if below.left and bit < 4:
            below.join(scalars)
    scalars = after(scalars, below.sent)
    gradient_norm = jnp.sqrt(scalars[0, 0])
    loss_sum = scalars[0, 1]
    scale = jnp.minimum(1.0, 0.01 / (gradient_norm + 1e-06))

    head_shape = shape((local_games, outputs, shard), f32)
    head_out = call(
        head_step_kernel,
        [
            (SCALARS, me),
            (SCALARS, scale.reshape(1, 1)),
            *here(row, cols_now, all_grad.T),
            *far(heads_online, turn(first_head), turn(second_head)),
        ],
        far(head_shape, head_shape, head_shape),
        scratch(*[head_shape] * 3, *[shape((3, outputs, shard), f32)] * 3),
        head_flops,
        6 * local_games,
        WIDE,
    )
    piece = last.value.shape[1]
    most = most.finish(head_out[0])
    firsts = [below.finish(head_out[0]), most[:, piece:]]
    firsts = [g.reshape(-1, NECK) for g in firsts]
    lasts = [most[:, :piece], top_last.finish(head_out[0])]
    lasts = [g.reshape(NECK, width) for g in lasts]
    if neck % 128:
        firsts = [
            jnp.concatenate([swap_chunks(g[:width], 1, n_chan), g[width:]], axis=0) for g in firsts
        ]
    olds = (
        (weight_in, first_in, second_in),
        tuple(map(turn, (weight_mid, first_mid, second_mid))),
        (weight_out, first_out, second_out),
        (bottle_gains, first_bottle, second_bottle),
        (stream_gains, first_stream, second_stream),
    )
    olds = [array for group in olds for array in group]
    news = [shape(array.shape, f32) for array in olds]
    result = call(
        functools.partial(torso_step_kernel, n_chan),
        [(SCALARS, me), (SCALARS, scale.reshape(1, 1)), *far(*after_all(head_out[0], *firsts, *lasts), *olds)],
        far(*news),
        scratch(*firsts, *[shape((NECK, width), bf16)] * LAYERS, *news, *news),
        big,
        15 + 2 * LAYERS + 9 + 6 * LAYERS,
        WIDE,
    )
    result = list(result)
    result[3:6] = map(turn, result[3:6])
    return (*result, *map(turn, head_out), gradient_norm, loss_sum)


def solution(mesh):
    rows = P("dp", "chan")
    third = P(None, None, "chan")
    second = P(None, "chan", None)
    heads = P("chan", "dp", None)
    torso = (second, second, third, third, third, heads)
    placed = (
        rows,
        rows,
        P(),
        P("dp"),
        P("dp"),
        P("dp", None),
        P("dp"),
        P("dp", None),
        P("dp", None),
        *torso,
        *torso,
        *torso,
        *torso,
    )
    outs = tuple(spec for spec in torso for _ in range(3)) + (P(), P())
    return jax.shard_map(body, mesh=mesh, in_specs=placed, out_specs=outs, check_vma=False)
```

```python
import functools

import jax
import jax.numpy as jnp
from jax import lax
from jax.experimental import pallas as pl
from jax.experimental.pallas import tpu as pltpu
from jax.sharding import PartitionSpec as P

WIDTH = 2048
NECK = 512
GROUPS = 32
LAYERS = 2
ACTIONS = 18
ATOMS = 51
MAP = 11
PIX = 121
STEP = 10
SLOT = 128
TAPS = 9
EPS = 1e-05
SMALL = 128
VMEM = 20 * 1024 * 1024
WIDE = 44 * 1024 * 1024

bf16 = jnp.bfloat16
f32 = jnp.float32
highest = lax.Precision.HIGHEST
rates = (0.02, 0.08, 0.02, 0.5, 0.5, 0.02)

NT = (((1,), (1,)), ((), ()))
TN = (((0,), (0,)), ((), ()))


WHOLE = pl.BlockSpec(memory_space=pltpu.VMEM)
SCALARS = pl.BlockSpec(memory_space=pltpu.SMEM)
DISTANT = pl.BlockSpec(memory_space=pltpu.HBM)


def call(kernel, ins, outs, scratch, flops, moves, limit=VMEM, aliases=()):
    return pl.pallas_call(
        kernel,
        in_specs=[spec for spec, _ in ins],
        out_specs=tuple(spec for spec, _ in outs),
        out_shape=tuple(
            pltpu.HBM(out.shape, out.dtype) if spec is DISTANT else out for spec, out in outs
        ),
        scratch_shapes=[*scratch, pltpu.SemaphoreType.DMA((moves,))],
        input_output_aliases=dict(aliases),
        compiler_params=pltpu.CompilerParams(vmem_limit_bytes=limit),
        cost_estimate=pl.CostEstimate(
            flops=flops, bytes_accessed=12 * 1024 * 1024, transcendentals=0
        ),
    )(
        *(
            pltpu.with_memory_space_constraint(array, pltpu.HBM) if spec is DISTANT else array
            for spec, array in ins
        )
    )


def shape(dims, dtype):
    return jax.ShapeDtypeStruct(dims, dtype)


class Moves:
    def __init__(self, sems):
        self.sems, self.count = sems, 0

    def __call__(self, source, target):
        copy = pltpu.make_async_copy(source, target, self.sems.at[self.count])
        self.count += 1
        copy.start()
        return copy


def rows_of(i, count=SLOT):
    return slice(i * count, (i + 1) * count)


def pixel_mask():
    return (lax.broadcasted_iota(jnp.int32, (SLOT, 1), 0) < PIX).astype(f32)


def same_group(width, size):
    bits = size.bit_length() - 1
    row = lax.shift_right_logical(lax.broadcasted_iota(jnp.int32, (width, width), 0), bits)
    col = lax.shift_right_logical(lax.broadcasted_iota(jnp.int32, (width, width), 1), bits)
    return row == col


def group_mix(sums, size):
    count, width = sums.shape
    tile = min(width, 128)
    parts = width // tile
    tall = jnp.concatenate([sums[:, p * tile : (p + 1) * tile] for p in range(parts)], axis=0)
    matrix = jnp.where(same_group(tile, size), 1.0 / (size * PIX), 0.0).astype(f32)
    mixed = jnp.dot(tall, matrix, precision=highest, preferred_element_type=f32)
    return jnp.concatenate([mixed[p * count : (p + 1) * count] for p in range(parts)], axis=1)


def sigmoid(v):
    return 1.0 / (1.0 + jnp.exp(-v))


def tiles_of(width):
    tile = min(width, 128)
    return [slice(p * tile, (p + 1) * tile) for p in range(width // tile)]


def to_column(row):
    n = row.shape[1]
    diagonal = lax.broadcasted_iota(jnp.int32, (n, n), 0) == lax.broadcasted_iota(
        jnp.int32, (n, n), 1
    )
    return jnp.sum(jnp.where(diagonal, row, 0.0), axis=1, keepdims=True)


def split_store(product, rows, keep_refs, send_refs, neck):
    for j in range(len(keep_refs)):
        send_refs[j][rows, :] = product[:, (2 * j + 1) * neck : (2 * j + 2) * neck].astype(bf16)
        keep_refs[j][rows, :] = product[:, 2 * j * neck : (2 * j + 1) * neck]


def own_order_columns(me, w_ref, neck):
    if neck % 128:
        return w_ref[...].astype(bf16)
    picks = [
        w_ref[:, pl.ds(pl.multiple_of((me ^ k) * neck, neck), neck)].astype(bf16)
        for k in range(w_ref.shape[1] // neck)
    ]
    return jnp.concatenate(picks, axis=1)


def own_order_rows(me, w_ref, neck):
    picks = [
        w_ref[pl.ds(pl.multiple_of((me ^ k) * neck, neck), neck), :].astype(bf16)
        for k in range(w_ref.shape[0] // neck)
    ]
    return jnp.concatenate(picks, axis=0)


def tap_weights(mid_ref):
    size = NECK // GROUPS
    neck = mid_ref.shape[1]
    same = same_group(neck, size)
    mid = mid_ref[...].astype(f32)
    return [
        jnp.where(
            same,
            jnp.concatenate([mid[t * size : (t + 1) * size]] * (neck // size), axis=0),
            0.0,
        ).astype(bf16)
        for t in range(TAPS)
    ]


def shift_table():
    place = lax.broadcasted_iota(jnp.int32, (SLOT, SLOT), 0)
    at = lax.broadcasted_iota(jnp.int32, (SLOT, SLOT), 1)
    line = lax.shift_right_logical(place * 373, 12)
    column = place - line * MAP
    tables = []
    for tap in range(TAPS):
        down, right = tap // 3 - 1, tap % 3 - 1
        inside = (line + down >= 0) & (line + down < MAP) & (place < PIX)
        inside = inside & (column + right >= 0) & (column + right < MAP)
        tables.append(jnp.where(inside & (at == place + (down * MAP + right)), 1.0, 0.0))
    return jnp.concatenate(tables, axis=0).astype(bf16)


def convolve(source, images, cols_ref):
    table = shift_table()
    for i in range(images):
        here = rows_of(i)
        wide = jnp.dot(table, source[here, :], preferred_element_type=f32).astype(bf16)
        cols_ref[here, :] = jnp.concatenate([wide[rows_of(t)] for t in range(TAPS)], axis=1)


def add_terms(term_refs):
    total = term_refs[0][...]
    for term_ref in term_refs[1:]:
        total = total + term_ref[...].astype(f32)
    return total


def padded_image(obs_ref, i):
    start = i * PIX
    base = start // 16 * 16
    length = min(144, obs_ref.shape[0] - base)
    place = lax.broadcasted_iota(jnp.int32, (SLOT, length), 0)
    at = lax.broadcasted_iota(jnp.int32, (SLOT, length), 1)
    pick = ((at == place + (start - base)) & (place < PIX)).astype(bf16)
    image = jnp.dot(pick, obs_ref[base : base + length, :], preferred_element_type=f32)
    return image.astype(bf16)


def front_kernel(parts, me_ref, obs_hbm, w_hbm, *refs):
    half = parts // 2
    keep_refs, send_refs, (obs_ref, w_ref, sems) = refs[:half], refs[half:parts], refs[parts:]
    move = Moves(sems)
    obs_in = move(obs_hbm, obs_ref)
    w_in = move(w_hbm.at[0], w_ref)
    rows = obs_ref.shape[0]
    neck = keep_refs[0].shape[1]
    w_in.wait()
    weight = own_order_columns(me_ref[0], w_ref, neck)
    obs_in.wait()
    for i in range(rows // PIX):
        image = padded_image(obs_ref, i)
        got = jnp.dot(image, weight, preferred_element_type=f32)
        split_store(got, rows_of(i), keep_refs, send_refs, neck)


def bottle_kernel(layer, terms, save, *refs):
    term_refs, (gain_hbm, mid_hbm), refs = refs[:terms], refs[terms : terms + 2], refs[terms + 2 :]
    two_ref, refs = refs[0], refs[1:]
    saved, refs = (refs[:4], refs[4:]) if save else ((), refs)
    one_ref, a1_ref, a2_ref, stat_ref, sum_ref, cols_ref, gain_ref, mid_ref, sems = refs
    move = Moves(sems)
    gain_in = move(gain_hbm.at[layer], gain_ref)
    mid_in = move(mid_hbm.at[layer], mid_ref)
    rows, neck = a1_ref.shape
    images = rows // SLOT
    size = NECK // GROUPS
    mask = pixel_mask()
    out = []

    def norm(value_ref, at, out_ref):
        for i in range(images):
            sum_ref[i : i + 1, :] = jnp.sum(value_ref[rows_of(i), :], axis=0, keepdims=True)
        mean = group_mix(sum_ref[...], size)
        for i in range(images):
            center = (value_ref[rows_of(i), :] - mean[i : i + 1]) * mask
            sum_ref[i : i + 1, :] = jnp.sum(center * center, axis=0, keepdims=True)
        scale = lax.rsqrt(group_mix(sum_ref[...], size) + EPS)
        stat_ref[at, :, :] = mean
        stat_ref[at + 1, :, :] = scale
        for i in range(images):
            here = rows_of(i)
            v = (value_ref[here, :] - mean[i : i + 1]) * scale[i : i + 1]
            v = v * gain_ref[at : at + 1, :] + gain_ref[at + 1 : at + 2, :]
            out_ref[here, :] = (v * sigmoid(v) * mask).astype(bf16)

    a1_ref[...] = add_terms(term_refs)
    if save:
        out.append(move(a1_ref, saved[1]))
    gain_in.wait()
    norm(a1_ref, 0, one_ref)
    if save:
        out.append(move(one_ref, saved[0]))
    convolve(one_ref, images, cols_ref)
    mid_in.wait()
    weight = jnp.concatenate(tap_weights(mid_ref), axis=0)
    for i in range(images // 2):
        here = rows_of(i, 2 * SLOT)
        a2_ref[here, :] = jnp.dot(cols_ref[here, :], weight, preferred_element_type=f32)
    if save:
        out.append(move(a2_ref, saved[2]))
    norm(a2_ref, 2, two_ref)
    if save:
        out.append(move(stat_ref, saved[3]))
    for copy in out:
        copy.wait()


def third_kernel(layer, parts, last, save, me_ref, *refs):
    chunks, (x_hbm, w3_hbm, gain_hbm, extra_ref), refs = (
        refs[:parts],
        refs[parts : parts + 4],
        refs[parts + 4 :],
    )
    half = parts // 2
    if last:
        pool_ref, refs = refs[0], refs[1:]
    else:
        y_hbm, keep_refs, send_refs = refs[0], refs[1 : 1 + half], refs[1 + half : 1 + parts]
        refs = refs[1 + parts :]
    saved, refs = (refs[: 2 if last else 3], refs[2 if last else 3 :]) if save else ((), refs)
    a3_ref, stat_ref, sum_ref, x_ref, w3_ref, gain_ref, *refs, sems = refs
    move = Moves(sems)
    w3_in = move(w3_hbm.at[layer], w3_ref)
    gain_in = move(gain_hbm.at[layer], gain_ref)
    x_in = move(x_hbm, x_ref)
    if not last:
        y_ref, low_ref, w1_ref = refs
        w1_in = move(extra_ref.at[layer + 1], w1_ref)
    rows, width = a3_ref.shape
    neck = chunks[0].shape[1]
    images = rows // SLOT
    size = WIDTH // GROUPS
    tiles = tiles_of(width)
    mask = pixel_mask()
    out = []
    w3_in.wait()
    third_weight = own_order_rows(me_ref[0], w3_ref, neck)
    for i in range(images // 2):
        here = rows_of(i, 2 * SLOT)
        left = jnp.concatenate([c[here, :] for c in chunks], axis=1)
        a3_ref[here, :] = jnp.dot(left, third_weight, preferred_element_type=f32)
    if save:
        out.append(move(a3_ref, saved[0]))
    for i in range(images):
        for t in tiles:
            sum_ref[i : i + 1, t] = jnp.sum(a3_ref[rows_of(i), t], axis=0, keepdims=True)
    stat_ref[0, :, :] = group_mix(sum_ref[...], size)
    for i in range(images):
        for t in tiles:
            center = (a3_ref[rows_of(i), t] - stat_ref[0, i : i + 1, t]) * mask
            sum_ref[i : i + 1, t] = jnp.sum(center * center, axis=0, keepdims=True)
    stat_ref[1, :, :] = lax.rsqrt(group_mix(sum_ref[...], size) + EPS)
    if save:
        out.append(move(stat_ref, saved[1]))
    gain_in.wait()
    x_in.wait()
    if not last:
        w1_in.wait()
        first_weight = own_order_columns(me_ref[0], w1_ref, neck)
    for i in range(images):
        here = rows_of(i)
        if layer == 0:
            low_ref[here, :] = padded_image(x_ref, i)
        for t in tiles:
            x = low_ref[here, t].astype(f32) if layer == 0 else x_ref[here, t]
            v = (a3_ref[here, t] - stat_ref[0, i : i + 1, t]) * stat_ref[1, i : i + 1, t]
            v = x + (v * gain_ref[0:1, t] + gain_ref[1:2, t])
            y = v * sigmoid(v) * mask
            if last:
                sum_ref[i : i + 1, t] = jnp.sum(y, axis=0, keepdims=True) * (1.0 / PIX)
            else:
                y_ref[here, t] = y
                low_ref[here, t] = y.astype(bf16)
        if not last and i % 2:
            both = rows_of(i // 2, 2 * SLOT)
            out.append(move(y_ref.at[both], y_hbm.at[both]))
            got = jnp.dot(low_ref[both, :], first_weight, preferred_element_type=f32)
            split_store(got, both, keep_refs, send_refs, neck)
    if last:
        shard = pool_ref.shape[3]
        for e in range(width // shard):
            pool_ref[e, 0] = sum_ref[:, e * shard : (e + 1) * shard].astype(bf16)
            pool_ref[e, 1] = extra_ref[e, 0]
    elif save:
        out.append(move(low_ref, saved[2]))
    for copy in out:
        copy.wait()


def outer_back_kernel(layer, parts, top, me_ref, *refs):
    half = parts // 2
    if top:
        up_ref, refs = refs[0], refs[1:]
    else:
        up_hbm, chunks, w1_hbm = refs[0], refs[1 : 1 + parts], refs[1 + parts]
        refs = refs[2 + parts :]
    x_hbm, a3_hbm, stat_hbm, gain_hbm, w3_hbm = refs[:5]
    keep_refs, send_refs, refs = refs[5 : 5 + half], refs[5 + half : 5 + parts], refs[5 + parts :]
    da3_hbm, dgain_hbm, refs = refs[0], refs[1], refs[2:]
    if layer > 0:
        dv_hbm, refs = refs[0], refs[1:]
    x_ref, a3_ref, stat_ref, gain_ref, w3_ref, da3_ref, dgain_ref, dv_ref, p_ref, q_ref = refs[:10]
    *refs, sems = refs[10:]
    move = Moves(sems)
    if not top:
        up_ref, w1_ref = refs
        w1_in = move(w1_hbm.at[layer + 1], w1_ref)
        up_in = move(up_hbm, up_ref)
    early = [
        move(stat_hbm, stat_ref),
        move(gain_hbm.at[layer], gain_ref),
        move(a3_hbm, a3_ref),
        move(x_hbm, x_ref),
    ]
    w3_in = move(w3_hbm.at[layer], w3_ref)
    rows, width = a3_ref.shape
    neck = keep_refs[0].shape[1]
    images = rows // SLOT
    size = WIDTH // GROUPS
    tiles = tiles_of(width)
    mask = pixel_mask()
    out = []
    if top:
        pooled = jnp.sum(up_ref[...].astype(f32), axis=0) * (1.0 / PIX)
        p_ref[...] = jnp.concatenate([pooled[e] for e in range(pooled.shape[0])], axis=1)
    else:
        w1_in.wait()
        first_weight = own_order_columns(me_ref[0], w1_ref, neck)
        up_in.wait()
        for i in range(images // 2):
            here = rows_of(i, 2 * SLOT)
            left = jnp.concatenate([c[here, :] for c in chunks], axis=1)
            dv_ref[here, :] = up_ref[here, :] + lax.dot_general(
                left, first_weight, NT, preferred_element_type=f32
            )
    for copy in early:
        copy.wait()
    for i in range(images):
        here, one = rows_of(i), slice(i, i + 1)
        if layer == 0:
            da3_ref[here, :] = padded_image(x_ref, i)
        for t in tiles:
            x = da3_ref[here, t].astype(f32) if layer == 0 else x_ref[here, t]
            hat = (a3_ref[here, t] - stat_ref[0, one, t]) * stat_ref[1, one, t]
            v = x + (hat * gain_ref[0:1, t] + gain_ref[1:2, t])
            s = sigmoid(v)
            slope = s * (1.0 + v * (1.0 - s)) * mask
            dv = slope * (p_ref[one, t] if top else dv_ref[here, t])
            dv_ref[here, t] = dv
            q_ref[one, t] = jnp.sum(dv * hat, axis=0, keepdims=True)
            p_ref[one, t] = jnp.sum(dv, axis=0, keepdims=True)
    if layer > 0:
        out.append(move(dv_ref, dv_hbm))
    dgain_ref[0:1, :] = jnp.sum(q_ref[...], axis=0, keepdims=True)
    dgain_ref[1:2, :] = jnp.sum(p_ref[...], axis=0, keepdims=True)
    out.append(move(dgain_ref, dgain_hbm))
    p_ref[...] = group_mix(p_ref[...] * gain_ref[0:1, :], size)
    q_ref[...] = group_mix(q_ref[...] * gain_ref[0:1, :], size)
    w3_in.wait()
    third_weight = own_order_rows(me_ref[0], w3_ref, neck)
    for i in range(images):
        here, one = rows_of(i), slice(i, i + 1)
        for t in tiles:
            scale = stat_ref[1, one, t]
            hat = (a3_ref[here, t] - stat_ref[0, one, t]) * scale
            d = dv_ref[here, t] * gain_ref[0:1, t] - p_ref[one, t] - hat * q_ref[one, t]
            da3_ref[here, t] = (d * scale * mask).astype(bf16)
        if i % 2:
            both = rows_of(i // 2, 2 * SLOT)
            got = lax.dot_general(da3_ref[both, :], third_weight, NT, preferred_element_type=f32)
            split_store(got, both, keep_refs, send_refs, neck)
    out.append(move(da3_ref, da3_hbm))
    for copy in out:
        copy.wait()


def bottle_back_kernel(layer, terms, *refs):
    term_refs = refs[:terms]
    a1_hbm, a2_hbm, stat_hbm, gain_hbm, mid_hbm = refs[terms : terms + 5]
    da1_ref, da2_hbm, dgain_hbm = refs[terms + 5 : terms + 8]
    a1_ref, a2_ref, stat_ref, gain_ref, mid_ref = refs[terms + 8 : terms + 13]
    da2_ref, dgain_ref, work_ref, p_ref, q_ref, cols_ref, sems = refs[terms + 13 :]
    move = Moves(sems)
    early = [
        move(stat_hbm, stat_ref),
        move(gain_hbm.at[layer], gain_ref),
        move(a2_hbm, a2_ref),
    ]
    a1_in = move(a1_hbm, a1_ref)
    mid_in = move(mid_hbm.at[layer], mid_ref)
    rows, neck = a1_ref.shape
    images = rows // SLOT
    size = NECK // GROUPS
    mask = pixel_mask()

    def back(value_ref, at, out_ref):
        gain = gain_ref[at : at + 1, :]
        bias = gain_ref[at + 1 : at + 2, :]
        for i in range(images):
            here, one = rows_of(i), slice(i, i + 1)
            hat = (value_ref[here, :] - stat_ref[at, one, :]) * stat_ref[at + 1, one, :]
            v = hat * gain + bias
            s = sigmoid(v)
            dv = work_ref[here, :] * (s * (1.0 + v * (1.0 - s)) * mask)
            work_ref[here, :] = dv
            q_ref[one, :] = jnp.sum(dv * hat, axis=0, keepdims=True)
            p_ref[one, :] = jnp.sum(dv, axis=0, keepdims=True)
        dgain_ref[at : at + 1, :] = jnp.sum(q_ref[...], axis=0, keepdims=True)
        dgain_ref[at + 1 : at + 2, :] = jnp.sum(p_ref[...], axis=0, keepdims=True)
        mixed_p = group_mix(p_ref[...] * gain, size)
        mixed_q = group_mix(q_ref[...] * gain, size)
        for i in range(images):
            here, one = rows_of(i), slice(i, i + 1)
            scale = stat_ref[at + 1, one, :]
            hat = (value_ref[here, :] - stat_ref[at, one, :]) * scale
            d = work_ref[here, :] * gain - mixed_p[one] - hat * mixed_q[one]
            out_ref[here, :] = (d * scale * mask).astype(bf16)

    work_ref[...] = add_terms(term_refs)
    for copy in early:
        copy.wait()
    back(a2_ref, 2, da2_ref)
    out = [move(da2_ref, da2_hbm)]
    convolve(da2_ref, images, cols_ref)
    mid_in.wait()
    weight = jnp.concatenate(tap_weights(mid_ref)[::-1], axis=1)
    for i in range(images // 2):
        here = rows_of(i, 2 * SLOT)
        work_ref[here, :] = lax.dot_general(
            cols_ref[here, :], weight, NT, preferred_element_type=f32
        )
    a1_in.wait()
    back(a1_ref, 0, da1_ref)
    out.append(move(dgain_ref, dgain_hbm))
    for copy in out:
        copy.wait()


def small_grad_kernel(
    one_hbm,
    da2_hbm,
    bottle_hbm,
    outer_hbm,
    out_hbm,
    one_ref,
    da2_ref,
    bottle_ref,
    outer_ref,
    out_ref,
    acc_ref,
    cols_ref,
    sems,
):
    move = Moves(sems)
    da2_in = move(da2_hbm, da2_ref)
    early = [move(one_hbm, one_ref), move(bottle_hbm, bottle_ref), move(outer_hbm, outer_ref)]
    rows, neck = one_ref.shape
    size = NECK // GROUPS
    da2_in.wait()
    convolve(da2_ref, rows // SLOT, cols_ref)
    for copy in early:
        copy.wait()
    acc_ref[...] = lax.dot_general(one_ref[...], cols_ref[...], TN, preferred_element_type=f32)
    same = same_group(neck, size)
    fold = (
        lax.broadcasted_iota(jnp.int32, (size, neck), 0)
        == (lax.broadcasted_iota(jnp.int32, (size, neck), 1) & (size - 1))
    ).astype(bf16)
    out_ref[...] = jnp.zeros_like(out_ref)
    for t in range(TAPS):
        part = jnp.where(same, acc_ref[:, t * neck : (t + 1) * neck], 0.0).astype(bf16)
        to = TAPS - 1 - t
        rows_at = slice(to % 3 * size, (to % 3 + 1) * size)
        out_ref[rows_at, to // 3 * neck : (to // 3 + 1) * neck] = jnp.dot(
            fold, part, preferred_element_type=f32
        ).astype(bf16)
    out_ref[0:4, 3 * neck : 4 * neck] = bottle_ref[...].astype(bf16)
    out_ref[48:50, 0 : outer_ref.shape[1]] = outer_ref[...].astype(bf16)
    move(out_ref, out_hbm).wait()


def last_grad(chunk_refs, right_ref, out_ref):
    neck = chunk_refs[0].shape[1]
    for k, chunk_ref in enumerate(chunk_refs):
        out_ref[k * neck : (k + 1) * neck, :] = lax.dot_general(
            chunk_ref[...], right_ref[...], TN, preferred_element_type=f32
        ).astype(bf16)


def first_grad(layer, x_ref, chunk_refs, right_ref, padded_ref, out_ref):
    neck = chunk_refs[0].shape[1]
    for k, chunk_ref in enumerate(chunk_refs):
        right_ref[:, k * neck : (k + 1) * neck] = chunk_ref[...]
    left_ref = x_ref
    if layer == 0:
        left_ref = padded_ref
        for i in range(padded_ref.shape[0] // SLOT):
            padded_ref[rows_of(i), :] = padded_image(x_ref, i)
    for t in tiles_of(x_ref.shape[1]):
        out_ref[t, :] = lax.dot_general(
            left_ref[:, t], right_ref[...], TN, preferred_element_type=f32
        ).astype(bf16)


def grad_kernel(layers, near, pieces, parts, me_ref, *refs):
    many = parts + 1
    count = (layers[0] is not None) * many + (layers[1] is not None) * (many + 1)
    hbm, (keep_hbm, send_hbm), refs = refs[:count], refs[count : count + 2], refs[count + 2 :]
    *refs, sems = refs
    move = Moves(sems)
    outs = []

    def give(out_ref, at):
        size = out_ref.shape[0] // pieces
        for j in range(pieces // 2):
            for target, bit in ((send_hbm, 1 - me_ref[3]), (keep_hbm, me_ref[3])):
                start = pl.multiple_of((2 * j + bit) * size, 16)
                outs.append(
                    move(out_ref.at[pl.ds(start, size), :], target.at[j, at : at + size, :])
                )

    jobs = []
    if layers[0] is not None:
        held, out_ref, refs = refs[:many], refs[many], refs[many + 1 :]
        jobs.append((0, held, out_ref, [move(a, b) for a, b in zip(hbm[:many], held)]))
        hbm = hbm[many:]
    if layers[1] is not None:
        held, right_ref, padded_ref, out_ref = refs[:-3], *refs[-3:]
        width = held[0].shape[1]
        ins = [move(a, b) for a, b in zip(hbm[:many], held)]
        if near:
            held = [held[0], *hbm[1:many]]
        ins.append(move(hbm[many], out_ref.at[width : width + SMALL]))
        jobs.append((1, held, out_ref, ins))
    at = 0
    for which, held, out_ref, ins in jobs:
        for copy in ins:
            copy.wait()
        if which:
            first_grad(layers[1], held[0], held[1:], right_ref, padded_ref, out_ref)
        else:
            last_grad(held[:parts], held[parts], out_ref)
        give(out_ref, at)
        at += out_ref.shape[0] // pieces
    for copy in outs:
        copy.wait()


def head_kernel(me_ref, games_ref, p_ref, w_hbm, target_hbm, out_ref, now_hbm, *refs):
    now_ref, later_ref, w_ref, target_ref, own_ref, acc_ref, sems = refs
    move = Moves(sems)
    count = w_hbm.shape[0]
    ins = [
        [move(source.at[g], target.at[g]) for g in range(count)]
        for source, target in ((w_hbm, w_ref), (target_hbm, target_ref))
    ]
    for at, cols_ref in enumerate((now_ref, later_ref)):
        cols_ref[...] = p_ref[:, at].astype(f32).reshape(cols_ref.shape).astype(bf16)
    out = move(now_ref, now_hbm)
    total, outputs = games_ref.shape[1], w_hbm.shape[1]
    game = to_column(games_ref[...].astype(f32))
    base = (me_ref[0] * count).astype(f32)
    acc_ref[...] = jnp.zeros_like(acc_ref)
    parts, _, rows, _ = out_ref.shape
    for at, (cols, weight) in enumerate(((now_ref, w_ref), (later_ref, target_ref))):
        for g in range(count):
            own_ref[g] = jnp.where(game == base + g, cols[...], jnp.zeros_like(cols))
        for copy in ins[at]:
            copy.wait()
        for start in range(0, outputs, 128):
            here = slice(start, min(start + 128, outputs))
            scores = None
            for g in range(count):
                part = lax.dot_general(
                    weight[g, here, :].astype(bf16), own_ref[g], NT, preferred_element_type=f32
                )
                scores = part if scores is None else scores + part
            acc_ref[here, 0:total] = scores
        logits = acc_ref[...].T[0:total, 0:outputs]
        out_ref[:, at] = logits.reshape(parts, rows, outputs).astype(out_ref.dtype)
    out.wait()


def head_back_kernel(
    me_ref, games_ref, spread_ref, now_hbm, w_hbm, out_ref, g_hbm, square_hbm, *refs
):
    now_ref, g_ref, square_ref, w_ref, acc_ref, sems = refs
    move = Moves(sems)
    count = w_hbm.shape[0]
    ins = [move(w_hbm.at[g], w_ref.at[g]) for g in range(count)]
    now_in = move(now_hbm, now_ref)
    g_ref[...] = spread_ref[...].astype(f32).reshape(g_ref.shape).astype(bf16)
    out = [move(g_ref, g_hbm)]
    row = games_ref[...].astype(f32)
    game = to_column(row)
    base = me_ref[0] * count
    now_in.wait()
    inner_p = lax.dot_general(now_ref[...], now_ref[...], NT, preferred_element_type=f32)
    inner_g = lax.dot_general(g_ref[...], g_ref[...], NT, preferred_element_type=f32)
    low = base.astype(f32)
    pair = (game == row) & (row >= low) & (row < low + count)
    square_ref[...] = jnp.sum(jnp.where(pair, inner_p * inner_g, 0.0), axis=0, keepdims=True)
    out.append(move(square_ref, square_hbm))
    acc_ref[...] = jnp.zeros_like(acc_ref)
    for g in range(count):
        grad = jnp.where(game == low + g, g_ref[...], jnp.zeros_like(g_ref))
        ins[g].wait()
        acc_ref[...] += jnp.dot(grad, w_ref[g].astype(bf16), preferred_element_type=f32)
    out_ref[...] = acc_ref[...].reshape(out_ref.shape).astype(out_ref.dtype)
    for copy in out:
        copy.wait()


def adamw(weight, first, second, grad, rate):
    momentum = 0.9 * first + 0.1 * grad
    variance = 0.999 * second + 0.001 * grad * grad
    root = jnp.sqrt(variance * (1.0 / (1.0 - 0.999**STEP))) + 1e-08
    scaled = (momentum * (1.0 / (1.0 - 0.9**STEP))) / root
    return (weight - rate * (scaled + 0.1 * weight), momentum, variance)


def head_step_kernel(games, me_ref, scale_ref, games_ref, p_ref, g_ref, *refs):
    (w_hbm, m_hbm, v_hbm), (w_out, m_out, v_out, *refs) = refs[:3], refs[-10:]
    old, new, sems = refs[:3], refs[3:6], refs[6]
    move = Moves(sems)
    slots = new[0].shape[0]
    base = me_ref[0] * w_hbm.shape[0]
    ins = [
        [move(source.at[g], ref.at[k]) for source, ref in zip((w_hbm, m_hbm, v_hbm), old)]
        for k, g in enumerate(games)
    ]
    outs = []
    for k, g in enumerate(games):
        left = jnp.where(games_ref[...] == base + g, g_ref[...], jnp.zeros_like(g_ref))
        grad = jnp.dot(left, p_ref[...], preferred_element_type=f32) * scale_ref[0, 0]
        for copy in ins[k]:
            copy.wait()
        if k >= slots:
            for copy in outs[k - slots]:
                copy.wait()
        made = adamw(*(ref[k] for ref in old), grad, rates[5])
        for ref, value in zip(new, made):
            ref[k % slots] = value
        outs.append(
            [
                move(ref.at[k % slots], target.at[g])
                for ref, target in zip(new, (w_out, m_out, v_out))
            ]
        )
    for group in outs[-slots:]:
        for copy in group:
            copy.wait()


def bring(move, source_hbm, target_ref, at, size):
    if not size:
        return [move(source_hbm, target_ref)]
    return [
        move(source_hbm.at[d, at : at + size, :], target_ref.at[d * size : (d + 1) * size, :])
        for d in range(source_hbm.shape[0])
    ]


def step_part(refs, at, grad, scale, rate):
    made = adamw(*(ref[at] for ref in refs), grad.astype(f32) * scale, rate)
    for ref, value in zip(refs, made):
        ref[at] = value


def last_step_kernel(parts, cuts, me_ref, scale_ref, *refs):
    grads_hbm, old_hbm, new_hbm = refs[:LAYERS], refs[LAYERS : LAYERS + 3], refs[LAYERS + 3 : LAYERS + 6]
    grads, held, sems = refs[LAYERS + 6 : -4], refs[-4:-1], refs[-1]
    move = Moves(sems)
    ins = []
    for layer in range(LAYERS):
        ins.append(bring(move, grads_hbm[layer], grads[layer], *cuts[layer]))
        ins[-1] += [move(a.at[layer], b.at[layer]) for a, b in zip(old_hbm, held)]
    me, scale = me_ref[0], scale_ref[0, 0]
    neck = NECK // parts
    outs = []
    for layer in range(LAYERS):
        for copy in ins[layer]:
            copy.wait()
        for q in range(parts):
            chunk = slice(q * neck, (q + 1) * neck)
            from_ = pl.ds(pl.multiple_of((me ^ q) * neck, neck), neck)
            step_part(held, (layer, chunk), grads[layer][from_, :], scale, rates[2])
        outs += [move(a.at[layer], b.at[layer]) for a, b in zip(held, new_hbm)]
    for copy in outs:
        copy.wait()


def first_step_kernel(parts, cuts, me_ref, scale_ref, *refs):
    grads_hbm, refs = refs[:LAYERS], refs[LAYERS:]
    old_hbm, new_hbm, refs = refs[:12], refs[12:24], refs[24:]
    grads, held, sems = refs[:LAYERS], refs[LAYERS : LAYERS + 12], refs[-1]
    move = Moves(sems)
    grads_in = []
    for layer in range(LAYERS):
        grads_in += bring(move, grads_hbm[layer], grads[layer], *cuts[layer])
    ins = [move(old_hbm[k], held[k]) for k in range(3, 12)]
    wide = [[move(old_hbm[k].at[layer], held[k].at[layer]) for k in range(3)] for layer in range(LAYERS)]
    me, scale = me_ref[0], scale_ref[0, 0]
    width = grads[0].shape[0] - SMALL
    size = NECK // GROUPS
    neck = NECK // parts
    for copy in (*grads_in, *ins):
        copy.wait()
    for layer in range(LAYERS):
        small = grads[layer]
        for k in range(3):
            taps = slice(k * 3 * size, (k + 1) * 3 * size)
            grad = small[width : width + 3 * size, k * neck : (k + 1) * neck]
            step_part(held[3:6], (layer, taps), grad, scale, rates[1])
        grad = small[width : width + 16, 3 * neck : 4 * neck][0:4]
        step_part(held[6:9], (layer,), grad, scale, rates[3])
        grad = small[width + 48 : width + 64, 0:width][0:2]
        step_part(held[9:12], (layer,), grad, scale, rates[4])
    outs = [move(held[k], new_hbm[k]) for k in range(3, 12)]
    for layer in range(LAYERS):
        for copy in wide[layer]:
            copy.wait()
        for q in range(parts):
            chunk = slice(q * neck, (q + 1) * neck)
            from_ = chunk if neck % 128 else pl.ds(pl.multiple_of((me ^ q) * neck, neck), neck)
            grad = grads[layer][0:width, from_]
            step_part(held[:3], (layer, slice(None), chunk), grad, scale, rates[0])
        outs += [move(held[k].at[layer], new_hbm[k].at[layer]) for k in range(3)]
    for copy in outs:
        copy.wait()


def loss_kernel(total, me_ref, *refs):
    part_ref, hbm, (g_ref, loss_hbm), refs = refs[0], refs[1:8], refs[8:10], refs[10:]
    vmem, (loss_ref, l_ref, sems) = refs[:7], refs[7:]
    move = Moves(sems)
    for copy in [move(source, target) for source, target in zip(hbm, vmem)]:
        copy.wait()
    act_row, next_row, done_row, game_row, legal, index, share = (ref[...] for ref in vmem)
    act, later_act, done, game = (
        to_column(row.astype(f32)) for row in (act_row, next_row, done_row, game_row)
    )
    count = act.shape[0]
    first = me_ref[1].astype(f32)
    own = ((game >= first) & (game < first + me_ref[2].astype(f32))).astype(f32)
    later = jnp.sum(part_ref[:, 1].astype(f32), axis=0)
    chosen = jnp.zeros((count, ATOMS), f32)
    for a in range(ACTIONS):
        chosen = jnp.where(later_act == a, later[:, a * ATOMS : (a + 1) * ATOMS], chosen)
    source = jnp.exp(chosen - jnp.max(chosen, axis=1, keepdims=True))
    source = source / jnp.sum(source, axis=1, keepdims=True)
    source = jnp.where(done > 0.0, 1.0 / ATOMS, source)
    atom = lax.broadcasted_iota(jnp.int32, (count, ATOMS), 1)
    lower, upper = source * share, source * (1.0 - share)
    proj = jnp.zeros((count, ATOMS), f32)
    for j in range(ATOMS):
        gap = atom - index[:, j : j + 1]
        proj = proj + jnp.where(
            gap == 0, lower[:, j : j + 1], jnp.where(gap == 1, upper[:, j : j + 1], 0.0)
        )
    logits = jnp.sum(part_ref[:, 0].astype(f32), axis=0)
    for a in range(ACTIONS):
        l_ref[a] = logits[:, a * ATOMS : (a + 1) * ATOMS]
    l = l_ref[...]
    top = jnp.max(l, axis=2, keepdims=True)
    e = jnp.exp(l - top)
    s = jnp.sum(e, axis=2, keepdims=True)
    p = e / s
    logp = l - top - jnp.log(s)
    z = -10.0 + 20.0 * lax.broadcasted_iota(jnp.int32, (1, 1, ATOMS), 2).astype(f32) / (ATOMS - 1)
    q = jnp.sum(p * z, axis=2, keepdims=True)
    action = lax.broadcasted_iota(jnp.int32, (ACTIONS, count, 1), 0).astype(f32)
    hot = (action == act[None]).astype(f32)
    allowed = jnp.concatenate([legal[:, a : a + 1][None] for a in range(ACTIONS)], axis=0) > 0
    masked = jnp.where(allowed, q, -1e30)
    best = jnp.max(masked, axis=0, keepdims=True)
    ex = jnp.where(allowed, jnp.exp(masked - best), 0.0)
    tot = jnp.sum(ex, axis=0, keepdims=True)
    taken = jnp.sum(hot * logp, axis=0)
    cross = -jnp.sum(proj * taken, axis=1, keepdims=True)
    picked = jnp.sum(hot * q, axis=0)
    loss = cross + 0.05 * (best[0] + jnp.log(tot[0]) - picked)
    loss_ref[...] = jnp.broadcast_to(loss * own, loss_ref.shape)
    mass = jnp.sum(proj, axis=1, keepdims=True)
    grad = hot * (p * mass[None] - proj[None]) + (0.05 * (ex / tot - hot)) * (p * (z - q))
    grad = grad * (own * (1.0 / total))[None]
    flat = jnp.concatenate([grad[a] for a in range(ACTIONS)], axis=1).astype(bf16)
    for k in range(g_ref.shape[0]):
        g_ref[k] = flat
    move(loss_ref, loss_hbm).wait()


def flip(value, axis, size, bit):
    return lax.ppermute(value, axis, [(i, i ^ bit) for i in range(size)])


def bits_of(size):
    return [1 << b for b in range(size.bit_length() - 1)]


def after(value, *tokens):
    return lax.optimization_barrier((value, *tokens))[0]


def after_all(token, *values):
    return lax.optimization_barrier((*values, token))[:-1]


def scatter_chan(keeps, sends, size):
    half = size // 2
    terms = {j: [keeps[j]] for j in range(half)}
    for j in reversed(range(half)):
        terms[j].append(flip(sends[j], "chan", size, 1))
    sent = []
    for bit in bits_of(size)[1:]:
        step = bit // 2
        for j in sorted(terms, reverse=True):
            if j & step:
                whole, *rest = terms.pop(j)
                for term in rest:
                    whole = whole + term.astype(f32)
                sent.append(whole.astype(bf16))
                terms[j - step].append(flip(sent[-1], "chan", size, bit))
    return terms[0], sent[-1]


def gather_chan(own, size, *hold):
    chunks = {0: own}
    for bit in reversed(bits_of(size)):
        for k in list(chunks):
            value = after(chunks[k], *hold) if k else own
            chunks[k ^ bit] = flip(value, "chan", size, bit)
    return [chunks[k] for k in range(size)]


class Spread:
    def __init__(self, value, size):
        self.value, self.size = value, size
        self.left = bits_of(size)
        self.me = lax.axis_index("dp")

    def begin(self, keep, send):
        self.keep, self.sent = keep.astype(f32), send
        self.got = flip(send, "dp", self.size, self.left.pop(0))
        return self

    def send(self):
        bit = self.left.pop(0)
        pieces, *rest = self.value.shape
        paired = self.value.reshape(pieces // 2, 2, *rest)
        mine = ((self.me & bit) > 0).astype(jnp.int32)
        part = lambda at: lax.dynamic_index_in_dim(paired, at, 1, keepdims=False)
        self.keep = part(mine).astype(f32)
        self.sent = part(1 - mine).astype(bf16)
        self.got = flip(self.sent, "dp", self.size, bit)
        return self

    def add(self, *hold):
        got = after(self.got, *hold) if hold else self.got
        self.value = self.keep + got.astype(f32)
        self.sent = None
        if self.left:
            self.send()
        return self

    def finish(self, *hold):
        self.add(*hold)
        while self.sent is not None:
            self.add()
        return self


class Collect:
    def __init__(self, value, size, *hold):
        self.size, self.left = size, bits_of(size)
        self.me = lax.axis_index("dp")
        self.value = value.astype(bf16)
        self.send(*hold)

    def send(self, *hold):
        self.bit = self.left.pop()
        self.sent = after(self.value, *hold) if hold else self.value
        self.got = flip(self.sent, "dp", self.size, self.bit)

    def join(self, *hold):
        got = after(self.got, *hold) if hold else self.got
        upper = (self.me & self.bit) > 0
        pair = jnp.stack(
            [jnp.where(upper, got, self.value), jnp.where(upper, self.value, got)], axis=1
        )
        self.value = pair.reshape(2 * got.shape[0], *got.shape[1:])
        if self.left:
            self.send()
        return self

    def finish(self, *hold):
        while self.left:
            self.join(*hold)
        return self.join(*hold).value


def sum_all(value, sizes):
    for axis, size in sizes:
        for bit in bits_of(size):
            value = value + flip(value, axis, size, bit)
    return value


def swap_chunks(value, axis, size):
    me = lax.axis_index("chan")
    width = value.shape[axis] // size
    return jnp.concatenate(
        [
            lax.dynamic_slice_in_dim(value, (me ^ k) * width, width, axis=axis)
            for k in range(size)
        ],
        axis=axis,
    )


def body(
    obs_now,
    obs_next,
    games,
    actions,
    next_actions,
    legal,
    done,
    proj_index,
    proj_frac,
    weight_in,
    weight_mid,
    weight_out,
    bottle_gains,
    stream_gains,
    weight_head,
    first_in,
    first_mid,
    first_out,
    first_bottle,
    first_stream,
    first_head,
    second_in,
    second_mid,
    second_out,
    second_bottle,
    second_stream,
    second_head,
    target_in,
    target_mid,
    target_out,
    target_bottle,
    target_stream,
    target_head,
):
    n_chan, n_dp = lax.axis_size("chan"), lax.axis_size("dp")
    chan_at, dp_at = lax.axis_index("chan"), lax.axis_index("dp")
    width = obs_now.shape[1]
    neck = weight_mid.shape[1]
    images = obs_now.shape[0] // PIX
    rows = images * SLOT
    half = n_chan // 2
    big = 2 * rows * width * NECK
    local_games, shard, outputs = weight_head.shape
    count = actions.shape[0]
    total = count * n_dp
    me = jnp.stack([chan_at, chan_at * local_games, local_games, dp_at & 1]).astype(jnp.int32)
    turn = lambda array: array.swapaxes(1, 2)
    wide = shape((rows, width), f32)
    wide_low = shape((rows, width), bf16)
    slim = shape((rows, neck), f32)
    slim_low = shape((rows, neck), bf16)
    split_outs = [(WHOLE, slim)] * half + [(WHOLE, slim_low)] * half
    weights = shape((width, NECK), f32)

    def scratch(*shapes):
        return [pltpu.VMEM(s.shape, s.dtype) for s in shapes]

    def like(array):
        return shape(array.shape[1:], array.dtype)

    def here(*arrays):
        return [(WHOLE, array) for array in arrays]

    def far(*arrays):
        return [(DISTANT, array) for array in arrays]

    def columns(weight):
        return weight if neck % 128 == 0 else swap_chunks(weight, 2, n_chan)

    def front(obs, nets):
        return call(
            functools.partial(front_kernel, n_chan),
            [(SCALARS, me), *far(obs, nets[0])],
            split_outs,
            scratch(obs, like(nets[0])),
            big,
            2,
        )

    def bottle(layer, terms, nets, save):
        stats = shape((4, images, neck), f32)
        outs = [(WHOLE, slim_low)]
        if save:
            outs += far(slim_low, slim, slim, stats)
        return call(
            functools.partial(bottle_kernel, layer, len(terms), save),
            [*here(*terms), *far(nets[3], nets[1])],
            outs,
            scratch(
                slim_low,
                slim,
                slim,
                stats,
                shape((images, neck), f32),
                shape((rows, TAPS * neck), bf16),
                like(nets[3]),
                like(nets[1]),
            ),
            big,
            6 if save else 2,
        )

    def third(layer, chunks, stream, nets, save, other=None):
        last = layer == LAYERS - 1
        stats = shape((2, images, width), f32)
        keep = scratch(
            wide,
            stats,
            shape((images, width), f32),
            stream,
            like(nets[2]),
            like(nets[4]),
        )
        if last:
            outs = [(WHOLE, shape((width // shard, 2, images, shard), bf16))]
            extra = (WHOLE, other)
        else:
            outs = [(DISTANT, wide), *split_outs]
            extra = (DISTANT, nets[0])
            keep += scratch(wide, wide_low, like(nets[0]))
        if save:
            outs += far(wide, stats) if last else far(wide, stats, wide_low)
        return call(
            functools.partial(third_kernel, layer, n_chan, last, save),
            [(SCALARS, me), *here(*chunks), *far(stream, nets[2], nets[4]), extra],
            outs,
            keep,
            2 * big,
            (3 if last else 4 + images // 2) + (2 + (not last)) * save,
        )

    online = (columns(weight_in), turn(weight_mid), weight_out, bottle_gains, stream_gains)
    target = (columns(target_in), turn(target_mid), target_out, target_bottle, target_stream)

    stream_n, stream_o, low_o = obs_next, obs_now, obs_now
    split_n = front(obs_next, target)
    terms_n, sent_n = scatter_chan(split_n[:half], split_n[half:], n_chan)
    split_o = front(after(obs_now, split_n[0]), online)
    terms_o, sent_o = scatter_chan(split_o[:half], split_o[half:], n_chan)
    kept = []
    for layer in range(LAYERS):
        terms_n[-1] = after(terms_n[-1], sent_o)
        (two_n,) = bottle(layer, terms_n, target, False)
        terms_o[-1] = after(terms_o[-1], two_n)
        two_o, *inner = bottle(layer, terms_o, online, True)
        chunks_n = gather_chan(two_n, n_chan, two_o)
        if layer < LAYERS - 1:
            stream_n, *split_n = third(layer, chunks_n, stream_n, target, False)
            terms_n, sent_n = scatter_chan(split_n[:half], split_n[half:], n_chan)
            chunks_o = gather_chan(two_o, n_chan, split_n[0])
            chunks_o[0] = after(chunks_o[0], sent_n)
            got = third(layer, chunks_o, stream_o, online, True)
            kept.append((stream_o, low_o, inner, chunks_o, got[1 + n_chan : 3 + n_chan]))
            stream_o, low_o, split_o = got[0], got[-1], list(got[1 : 1 + n_chan])
            split_o[half:] = [after(part, terms_n[-1]) for part in split_o[half:]]
            terms_o, sent_o = scatter_chan(split_o[:half], split_o[half:], n_chan)
        else:
            empty = jnp.zeros((width // shard, 2, images, shard), bf16)
            (pooled,) = third(layer, chunks_n, stream_n, target, False, empty)
            chunks_o = gather_chan(two_o, n_chan, pooled)
            pooled, *saved = third(layer, chunks_o, stream_o, online, True, pooled)
            kept.append((stream_o, low_o, inner, chunks_o, saved))

    row = games.reshape(1, total)
    mine = lax.dynamic_slice_in_dim(row, dp_at * count, count, 1)
    heads_online, heads_target = turn(weight_head), turn(target_head)
    head_flops = 2 * total * shard * outputs * local_games
    cols_shape = shape((total, shard), bf16)
    grad_shape = shape((total, outputs), bf16)

    pooled = lax.all_gather(pooled, "chan", axis=0, tiled=True)
    cols = lax.all_to_all(pooled, "dp", split_axis=0, concat_axis=0, tiled=True)
    parts, cols_now = call(
        head_kernel,
        [(SCALARS, me), *here(row, cols), *far(heads_online, heads_target)],
        [(WHOLE, shape((n_dp, 2, count, outputs), bf16)), (DISTANT, cols_shape)],
        scratch(
            cols_shape,
            cols_shape,
            heads_online,
            heads_target,
            shape((local_games, total, shard), bf16),
            shape((-(-outputs // 128) * 128, max(total, 128)), f32),
        ),
        2 * head_flops,
        2 * local_games + 1,
        WIDE,
    )
    parts = lax.all_to_all(parts, "dp", split_axis=0, concat_axis=0, tiled=True)
    facts = (
        actions.reshape(1, count),
        next_actions.reshape(1, count),
        done.reshape(1, count),
        mine,
        legal,
        proj_index,
        proj_frac,
    )
    losses_shape = shape((count, 128), f32)
    spread, losses = call(
        functools.partial(loss_kernel, total),
        [(SCALARS, me), (WHOLE, parts), *far(*facts)],
        [(WHOLE, shape((n_dp, count, outputs), bf16)), (DISTANT, losses_shape)],
        scratch(*facts, losses_shape, shape((ACTIONS, count, ATOMS), f32)),
        big,
        8,
    )
    spread = lax.all_to_all(spread, "dp", split_axis=0, concat_axis=0, tiled=True)
    d_cols, all_grad, square_head = call(
        head_back_kernel,
        [(SCALARS, me), *here(row, spread), *far(cols_now, heads_online)],
        [
            (WHOLE, shape((n_dp, count, shard), bf16)),
            *far(grad_shape, shape((1, total), f32)),
        ],
        scratch(
            cols_shape,
            grad_shape,
            shape((1, total), f32),
            heads_online,
            shape((total, shard), f32),
        ),
        head_flops,
        local_games + 3,
        WIDE,
    )
    d_rows = lax.all_to_all(d_cols, "dp", split_axis=0, concat_axis=0, tiled=True)
    d_rows = d_rows.reshape(n_chan, n_dp // n_chan, count, shard)
    upstream = lax.all_to_all(d_rows, "chan", split_axis=0, concat_axis=0, tiled=True)

    def outer_back(layer, lead):
        stream, _, _, _, (a3, stats3) = kept[layer]
        gains = shape((2, width), f32)
        outs = [*split_outs, *far(wide_low, gains)]
        if layer > 0:
            outs += far(wide)
        keep = scratch(
            stream,
            wide,
            stats3,
            like(stream_gains),
            like(weight_out),
            wide_low,
            gains,
            wide,
            shape((images, width), f32),
            shape((images, width), f32),
        )
        top = layer == LAYERS - 1
        if not top:
            keep += scratch(wide, like(online[0]))
        return call(
            functools.partial(outer_back_kernel, layer, n_chan, top),
            [(SCALARS, me), *lead, *far(stream, a3, stats3, stream_gains, weight_out)],
            outs,
            keep,
            2 * big,
            7 + (layer > 0) + 2 * (not top),
        )

    def bottle_back(layer, terms):
        _, _, (_, a1, a2, stats), _, _ = kept[layer]
        gains = shape((4, neck), f32)
        sums_shape = shape((images, neck), f32)
        return call(
            functools.partial(bottle_back_kernel, layer, len(terms)),
            [*here(*terms), *far(a1, a2, stats, bottle_gains, online[1])],
            [(WHOLE, slim_low), *far(slim_low, gains)],
            scratch(
                slim,
                slim,
                stats,
                like(bottle_gains),
                like(online[1]),
                slim_low,
                gains,
                slim,
                sums_shape,
                sums_shape,
                shape((rows, TAPS * neck), bf16),
            ),
            big,
            7,
        )

    def small_grad(layer, da2, d_bottle, d_outer):
        ins = (kept[layer][2][0], da2, d_bottle, d_outer)
        out = shape((SMALL, NECK), bf16)
        (got,) = call(
            small_grad_kernel,
            far(*ins),
            far(out),
            scratch(
                *ins,
                out,
                shape((neck, TAPS * neck), f32),
                shape((rows, TAPS * neck), bf16),
            ),
            big,
            5,
        )
        return got

    whole_pieces = width == NECK and NECK // n_dp % 16 == 0 and (width + SMALL) // n_dp % 16 == 0

    def gradients(last_layer=None, da3=None, first_layer=None, grads=(), small=None):
        ins, keep, size = [], [], 0
        if last_layer is not None:
            ins += [*kept[last_layer][3], da3]
            keep += [*ins, shape((NECK, width), bf16)]
            size += NECK * width // NECK // n_dp
        near, placed = first_layer == 0, None
        if first_layer is not None:
            more = [kept[first_layer][1], *grads]
            ins += [*more, small]
            if near:
                placed = [*far(more[0]), *here(*grads), *far(small)]
                more = more[:1]
            keep += [*more, shape((rows, NECK), bf16), wide_low, shape((width + SMALL, NECK), bf16)]
            size += (width + SMALL) // n_dp
        pieces = n_dp if whole_pieces else 2
        out = shape((pieces // 2, size if whole_pieces else size * n_dp // 2, NECK), bf16)
        if whole_pieces:
            keep_part, send_part = call(
                functools.partial(grad_kernel, (last_layer, first_layer), near, n_dp, n_chan),
                [(SCALARS, me), *(placed or far(*ins))],
                far(out, out),
                scratch(*keep),
                2 * big,
                len(ins) + 4 * n_dp,
            )
            return Spread(None, n_dp).begin(keep_part, send_part)
        flat = []
        if last_layer is not None:
            left = jnp.concatenate(kept[last_layer][3], axis=1)
            got = lax.dot_general(left, da3, TN, preferred_element_type=f32).astype(bf16)
            flat.append(got.reshape(n_dp, -1, NECK))
        if first_layer is not None:
            left = kept[first_layer][1]
            if first_layer == 0:
                left = jnp.pad(left.reshape(images, PIX, width), ((0, 0), (0, SLOT - PIX), (0, 0)))
                left = left.reshape(rows, width)
            right = jnp.concatenate(grads, axis=1)
            got = lax.dot_general(left, right, TN, preferred_element_type=f32).astype(bf16)
            got = jnp.concatenate([got, small], axis=0)
            flat.append(got.reshape(n_dp, -1, NECK))
        return Spread(jnp.concatenate(flat, axis=1), n_dp).send()

    lead = here(upstream)
    above = None
    for layer in reversed(range(LAYERS)):
        got = outer_back(layer, lead)
        da3, d_outer, *rest = got[n_chan:]
        terms, sent = scatter_chan(got[:half], got[half:n_chan], n_chan)
        da3 = after(da3, sent)
        if layer:
            above = gradients(layer, da3)
            hold = above.sent
        else:
            most = gradients(layer, da3, layer + 1, chunks, small)
            hold = most.sent
        terms[-1] = after(terms[-1], hold)
        da1, da2, d_bottle = bottle_back(layer, terms)
        if layer:
            above.add(da1)
            small = small_grad(layer, after(da2, above.sent), d_bottle, d_outer)
            above.add(small)
            chunks = gather_chan(da1, n_chan, above.sent)
            lead = [*far(*rest), *here(*chunks), *far(online[0])]
        else:
            above.finish(da1)
            top_last = Collect(above.value, n_dp)
            small = small_grad(layer, after(da2, top_last.sent), d_bottle, d_outer)
            most.add(small)
            chunks = gather_chan(da1, n_chan, small)
    final = gradients(first_layer=0, grads=chunks, small=small)
    most.add(final.sent)
    top_last.join(most.sent)
    squares = jnp.sum(square_head) + jnp.sum(above.value * above.value)
    final.add(squares, top_last.sent)
    most.finish(final.sent)
    squares = squares + jnp.sum(most.value * most.value)
    bulk = Collect(most.value, n_dp, squares)
    top_last.join(bulk.sent)
    final.add(top_last.sent)
    bulk.join(final.sent)
    final.finish(bulk.sent)
    squares = squares + jnp.sum(final.value * final.value)
    below = Collect(final.value, n_dp, squares)

    scalars = jnp.stack([squares, jnp.sum(losses[:, 0])])
    scalars = jnp.pad(scalars, (0, 126)).reshape(1, 128)
    scalars = sum_all(scalars, (("chan", n_chan),))
    for bit in (1, *reversed(bits_of(n_dp)[1:])):
        scalars = scalars + flip(scalars, "dp", n_dp, bit)
    hold = []
    for c in (bulk, below):
        if c.left:
            c.join(scalars)
            hold.append(c.sent)
    scalars = after(scalars, *hold)
    gradient_norm = jnp.sqrt(scalars[0, 0])
    loss_sum = scalars[0, 1]
    scale = jnp.minimum(1.0, 0.01 / (gradient_norm + 1e-06))

    head_shape = shape((local_games, outputs, shard), f32)

    def head_step(first_game, last_game, scale, before):
        chosen = range(first_game, last_game)
        held = shape((len(chosen), outputs, shard), f32)
        aliases = [(8 + k, k) for k in range(3)] if before else ()
        return call(
            functools.partial(head_step_kernel, chosen),
            [
                (SCALARS, me),
                (SCALARS, scale.reshape(1, 1)),
                *here(row, cols_now, all_grad.T),
                *far(heads_online, turn(first_head), turn(second_head), *before),
            ],
            far(head_shape, head_shape, head_shape),
            scratch(*[held] * 3, *[shape((2, outputs, shard), f32)] * 3),
            head_flops,
            6 * len(chosen),
            WIDE,
            aliases,
        )

    head_out = head_step(0, local_games, scale, ())
    while below.left:
        below.join(head_out[0])
    piece = NECK * width // NECK // n_dp
    bulk = bulk.finish(head_out[0])
    lasts = [(bulk, 0, piece), (top_last.finish(head_out[0]), 0, piece)]
    if not whole_pieces:
        lasts = [(g[:, :piece].reshape(NECK, width), 0, 0) for g, _, _ in lasts]

    def torso_step(kernel, grads, olds, hold):
        news = [shape(array.shape, f32) for array in olds]
        moves = 2 * len(olds) + LAYERS * (n_dp + len(olds))
        arrays = after_all(hold, *[g for g, _, _ in grads])
        cuts = [(at, size) for _, at, size in grads]
        flat = [shape((g.shape[0] * size, NECK) if size else g.shape, bf16) for g, _, size in grads]
        return call(
            functools.partial(kernel, n_chan, cuts),
            [(SCALARS, me), (SCALARS, scale.reshape(1, 1)), *far(*arrays, *olds)],
            far(*news),
            scratch(*flat, *news),
            big,
            moves,
            WIDE,
        )

    result_out = torso_step(last_step_kernel, lasts, (weight_out, first_out, second_out), head_out[0])
    below = below.finish(result_out[0])
    firsts = [(below, 0, below.shape[1]), (bulk, piece, below.shape[1])]
    if not whole_pieces:
        firsts = [g[:, at:].reshape(-1, NECK) for g, at, _ in firsts]
        if neck % 128:
            firsts = [
                jnp.concatenate([swap_chunks(g[:width], 1, n_chan), g[width:]], axis=0)
                for g in firsts
            ]
        firsts = [(g, 0, 0) for g in firsts]
    olds = (
        (weight_in, first_in, second_in),
        tuple(map(turn, (weight_mid, first_mid, second_mid))),
        (bottle_gains, first_bottle, second_bottle),
        (stream_gains, first_stream, second_stream),
    )
    olds = [array for group in olds for array in group]
    result = list(torso_step(first_step_kernel, firsts, olds, result_out[0]))
    result[3:6] = map(turn, result[3:6])
    result[6:6] = result_out
    return (*result, *map(turn, head_out), gradient_norm, loss_sum)


def solution(mesh):
    rows = P("dp", "chan")
    third = P(None, None, "chan")
    second = P(None, "chan", None)
    heads = P("chan", "dp", None)
    torso = (second, second, third, third, third, heads)
    placed = (
        rows,
        rows,
        P(),
        P("dp"),
        P("dp"),
        P("dp", None),
        P("dp"),
        P("dp", None),
        P("dp", None),
        *torso,
        *torso,
        *torso,
        *torso,
    )
    outs = tuple(spec for spec in torso for _ in range(3)) + (P(), P())
    return jax.shard_map(body, mesh=mesh, in_specs=placed, out_specs=outs, check_vma=False)
```

```python
import functools

import jax
import jax.numpy as jnp
from jax import lax
from jax.experimental import pallas as pl
from jax.experimental.pallas import tpu as pltpu
from jax.sharding import PartitionSpec as P

WIDTH = 2048
NECK = 512
GROUPS = 32
LAYERS = 2
ACTIONS = 18
ATOMS = 51
MAP = 11
PIX = 121
STEP = 10
SLOT = 128
TAPS = 9
EPS = 1e-05
SMALL = 128
VMEM = 20 * 1024 * 1024
WIDE = 44 * 1024 * 1024

bf16 = jnp.bfloat16
f32 = jnp.float32
highest = lax.Precision.HIGHEST
rates = (0.02, 0.08, 0.02, 0.5, 0.5, 0.02)

NT = (((1,), (1,)), ((), ()))
TN = (((0,), (0,)), ((), ()))


WHOLE = pl.BlockSpec(memory_space=pltpu.VMEM)
SCALARS = pl.BlockSpec(memory_space=pltpu.SMEM)
DISTANT = pl.BlockSpec(memory_space=pltpu.HBM)


def call(kernel, ins, outs, scratch, flops, moves, limit=VMEM, aliases=()):
    return pl.pallas_call(
        kernel,
        in_specs=[spec for spec, _ in ins],
        out_specs=tuple(spec for spec, _ in outs),
        out_shape=tuple(
            pltpu.HBM(out.shape, out.dtype) if spec is DISTANT else out for spec, out in outs
        ),
        scratch_shapes=[*scratch, pltpu.SemaphoreType.DMA((moves,))],
        input_output_aliases=dict(aliases),
        compiler_params=pltpu.CompilerParams(vmem_limit_bytes=limit),
        cost_estimate=pl.CostEstimate(
            flops=flops, bytes_accessed=12 * 1024 * 1024, transcendentals=0
        ),
    )(
        *(
            pltpu.with_memory_space_constraint(array, pltpu.HBM) if spec is DISTANT else array
            for spec, array in ins
        )
    )


def shape(dims, dtype):
    return jax.ShapeDtypeStruct(dims, dtype)


class Moves:
    def __init__(self, sems):
        self.sems, self.count = sems, 0

    def __call__(self, source, target):
        copy = pltpu.make_async_copy(source, target, self.sems.at[self.count])
        self.count += 1
        copy.start()
        return copy


def rows_of(i, count=SLOT):
    return slice(i * count, (i + 1) * count)


def pixel_mask():
    return (lax.broadcasted_iota(jnp.int32, (SLOT, 1), 0) < PIX).astype(f32)


def same_group(width, size):
    bits = size.bit_length() - 1
    row = lax.shift_right_logical(lax.broadcasted_iota(jnp.int32, (width, width), 0), bits)
    col = lax.shift_right_logical(lax.broadcasted_iota(jnp.int32, (width, width), 1), bits)
    return row == col


def group_mix(sums, size):
    count, width = sums.shape
    tile = min(width, 128)
    parts = width // tile
    tall = jnp.concatenate([sums[:, p * tile : (p + 1) * tile] for p in range(parts)], axis=0)
    matrix = jnp.where(same_group(tile, size), 1.0 / (size * PIX), 0.0).astype(f32)
    mixed = jnp.dot(tall, matrix, precision=highest, preferred_element_type=f32)
    return jnp.concatenate([mixed[p * count : (p + 1) * count] for p in range(parts)], axis=1)


def sigmoid(v):
    return 1.0 / (1.0 + jnp.exp(-v))


def tiles_of(width):
    tile = min(width, 128)
    return [slice(p * tile, (p + 1) * tile) for p in range(width // tile)]


def to_column(row):
    n = row.shape[1]
    diagonal = lax.broadcasted_iota(jnp.int32, (n, n), 0) == lax.broadcasted_iota(
        jnp.int32, (n, n), 1
    )
    return jnp.sum(jnp.where(diagonal, row, 0.0), axis=1, keepdims=True)


def split_store(product, rows, keep_refs, send_refs, neck):
    for j in range(len(keep_refs)):
        send_refs[j][rows, :] = product[:, (2 * j + 1) * neck : (2 * j + 2) * neck].astype(bf16)
        keep_refs[j][rows, :] = product[:, 2 * j * neck : (2 * j + 1) * neck]


def own_order_columns(me, w_ref, neck):
    if neck % 128:
        return w_ref[...].astype(bf16)
    picks = [
        w_ref[:, pl.ds(pl.multiple_of((me ^ k) * neck, neck), neck)].astype(bf16)
        for k in range(w_ref.shape[1] // neck)
    ]
    return jnp.concatenate(picks, axis=1)


def own_order_rows(me, w_ref, neck):
    picks = [
        w_ref[pl.ds(pl.multiple_of((me ^ k) * neck, neck), neck), :].astype(bf16)
        for k in range(w_ref.shape[0] // neck)
    ]
    return jnp.concatenate(picks, axis=0)


def tap_weights(mid_ref):
    size = NECK // GROUPS
    neck = mid_ref.shape[1]
    same = same_group(neck, size)
    mid = mid_ref[...].astype(f32)
    return [
        jnp.where(
            same,
            jnp.concatenate([mid[t * size : (t + 1) * size]] * (neck // size), axis=0),
            0.0,
        ).astype(bf16)
        for t in range(TAPS)
    ]


def shift_table():
    place = lax.broadcasted_iota(jnp.int32, (SLOT, SLOT), 0)
    at = lax.broadcasted_iota(jnp.int32, (SLOT, SLOT), 1)
    line = lax.shift_right_logical(place * 373, 12)
    column = place - line * MAP
    tables = []
    for tap in range(TAPS):
        down, right = tap // 3 - 1, tap % 3 - 1
        inside = (line + down >= 0) & (line + down < MAP) & (place < PIX)
        inside = inside & (column + right >= 0) & (column + right < MAP)
        tables.append(jnp.where(inside & (at == place + (down * MAP + right)), 1.0, 0.0))
    return jnp.concatenate(tables, axis=0).astype(bf16)


def convolve(source, images, cols_ref):
    table = shift_table()
    for i in range(images):
        here = rows_of(i)
        wide = jnp.dot(table, source[here, :], preferred_element_type=f32).astype(bf16)
        cols_ref[here, :] = jnp.concatenate([wide[rows_of(t)] for t in range(TAPS)], axis=1)


def add_terms(term_refs):
    total = term_refs[0][...]
    for term_ref in term_refs[1:]:
        total = total + term_ref[...].astype(f32)
    return total


def padded_image(obs_ref, i):
    start = i * PIX
    base = start // 16 * 16
    length = min(144, obs_ref.shape[0] - base)
    place = lax.broadcasted_iota(jnp.int32, (SLOT, length), 0)
    at = lax.broadcasted_iota(jnp.int32, (SLOT, length), 1)
    pick = ((at == place + (start - base)) & (place < PIX)).astype(bf16)
    image = jnp.dot(pick, obs_ref[base : base + length, :], preferred_element_type=f32)
    return image.astype(bf16)


def front_kernel(parts, me_ref, obs_hbm, w_hbm, *refs):
    half = parts // 2
    keep_refs, send_refs, (obs_ref, w_ref, sems) = refs[:half], refs[half:parts], refs[parts:]
    move = Moves(sems)
    obs_in = move(obs_hbm, obs_ref)
    w_in = move(w_hbm.at[0], w_ref)
    rows = obs_ref.shape[0]
    neck = keep_refs[0].shape[1]
    w_in.wait()
    weight = own_order_columns(me_ref[0], w_ref, neck)
    obs_in.wait()
    for i in range(rows // PIX):
        image = padded_image(obs_ref, i)
        got = jnp.dot(image, weight, preferred_element_type=f32)
        split_store(got, rows_of(i), keep_refs, send_refs, neck)


def bottle_kernel(layer, terms, save, *refs):
    term_refs, (gain_hbm, mid_hbm), refs = refs[:terms], refs[terms : terms + 2], refs[terms + 2 :]
    two_ref, refs = refs[0], refs[1:]
    saved, refs = (refs[:4], refs[4:]) if save else ((), refs)
    one_ref, a1_ref, a2_ref, stat_ref, sum_ref, cols_ref, gain_ref, mid_ref, sems = refs
    move = Moves(sems)
    gain_in = move(gain_hbm.at[layer], gain_ref)
    mid_in = move(mid_hbm.at[layer], mid_ref)
    rows, neck = a1_ref.shape
    images = rows // SLOT
    size = NECK // GROUPS
    mask = pixel_mask()
    out = []

    def norm(value_ref, at, out_ref):
        for i in range(images):
            sum_ref[i : i + 1, :] = jnp.sum(value_ref[rows_of(i), :], axis=0, keepdims=True)
        mean = group_mix(sum_ref[...], size)
        for i in range(images):
            center = (value_ref[rows_of(i), :] - mean[i : i + 1]) * mask
            sum_ref[i : i + 1, :] = jnp.sum(center * center, axis=0, keepdims=True)
        scale = lax.rsqrt(group_mix(sum_ref[...], size) + EPS)
        stat_ref[at, :, :] = mean
        stat_ref[at + 1, :, :] = scale
        for i in range(images):
            here = rows_of(i)
            v = (value_ref[here, :] - mean[i : i + 1]) * scale[i : i + 1]
            v = v * gain_ref[at : at + 1, :] + gain_ref[at + 1 : at + 2, :]
            out_ref[here, :] = (v * sigmoid(v) * mask).astype(bf16)

    a1_ref[...] = add_terms(term_refs)
    if save:
        out.append(move(a1_ref, saved[1]))
    gain_in.wait()
    norm(a1_ref, 0, one_ref)
    if save:
        out.append(move(one_ref, saved[0]))
    convolve(one_ref, images, cols_ref)
    mid_in.wait()
    weight = jnp.concatenate(tap_weights(mid_ref), axis=0)
    for i in range(images // 2):
        here = rows_of(i, 2 * SLOT)
        a2_ref[here, :] = jnp.dot(cols_ref[here, :], weight, preferred_element_type=f32)
    if save:
        out.append(move(a2_ref, saved[2]))
    norm(a2_ref, 2, two_ref)
    if save:
        out.append(move(stat_ref, saved[3]))
    for copy in out:
        copy.wait()


def third_kernel(layer, parts, last, save, me_ref, *refs):
    chunks, (x_hbm, w3_hbm, gain_hbm, extra_ref), refs = (
        refs[:parts],
        refs[parts : parts + 4],
        refs[parts + 4 :],
    )
    half = parts // 2
    if last:
        pool_ref, refs = refs[0], refs[1:]
    else:
        y_hbm, keep_refs, send_refs = refs[0], refs[1 : 1 + half], refs[1 + half : 1 + parts]
        refs = refs[1 + parts :]
    saved, refs = (refs[: 2 if last else 3], refs[2 if last else 3 :]) if save else ((), refs)
    a3_ref, stat_ref, sum_ref, x_ref, w3_ref, gain_ref, *refs, sems = refs
    move = Moves(sems)
    w3_in = move(w3_hbm.at[layer], w3_ref)
    gain_in = move(gain_hbm.at[layer], gain_ref)
    x_in = move(x_hbm, x_ref)
    if not last:
        y_ref, low_ref, w1_ref = refs
        w1_in = move(extra_ref.at[layer + 1], w1_ref)
    rows, width = a3_ref.shape
    neck = chunks[0].shape[1]
    images = rows // SLOT
    size = WIDTH // GROUPS
    tiles = tiles_of(width)
    mask = pixel_mask()
    out = []
    w3_in.wait()
    third_weight = own_order_rows(me_ref[0], w3_ref, neck)
    for i in range(images // 2):
        here = rows_of(i, 2 * SLOT)
        left = jnp.concatenate([c[here, :] for c in chunks], axis=1)
        a3_ref[here, :] = jnp.dot(left, third_weight, preferred_element_type=f32)
    if save:
        out.append(move(a3_ref, saved[0]))
    for i in range(images):
        for t in tiles:
            sum_ref[i : i + 1, t] = jnp.sum(a3_ref[rows_of(i), t], axis=0, keepdims=True)
    stat_ref[0, :, :] = group_mix(sum_ref[...], size)
    for i in range(images):
        for t in tiles:
            center = (a3_ref[rows_of(i), t] - stat_ref[0, i : i + 1, t]) * mask
            sum_ref[i : i + 1, t] = jnp.sum(center * center, axis=0, keepdims=True)
    stat_ref[1, :, :] = lax.rsqrt(group_mix(sum_ref[...], size) + EPS)
    if save:
        out.append(move(stat_ref, saved[1]))
    gain_in.wait()
    x_in.wait()
    if not last:
        w1_in.wait()
        first_weight = own_order_columns(me_ref[0], w1_ref, neck)
    for i in range(images):
        here = rows_of(i)
        if layer == 0:
            low_ref[here, :] = padded_image(x_ref, i)
        for t in tiles:
            x = low_ref[here, t].astype(f32) if layer == 0 else x_ref[here, t]
            v = (a3_ref[here, t] - stat_ref[0, i : i + 1, t]) * stat_ref[1, i : i + 1, t]
            v = x + (v * gain_ref[0:1, t] + gain_ref[1:2, t])
            y = v * sigmoid(v) * mask
            if last:
                sum_ref[i : i + 1, t] = jnp.sum(y, axis=0, keepdims=True) * (1.0 / PIX)
            else:
                y_ref[here, t] = y
                low_ref[here, t] = y.astype(bf16)
        if not last and i % 2:
            both = rows_of(i // 2, 2 * SLOT)
            out.append(move(y_ref.at[both], y_hbm.at[both]))
            got = jnp.dot(low_ref[both, :], first_weight, preferred_element_type=f32)
            split_store(got, both, keep_refs, send_refs, neck)
    if last:
        shard = pool_ref.shape[3]
        for e in range(width // shard):
            pool_ref[e, 0] = sum_ref[:, e * shard : (e + 1) * shard].astype(bf16)
            pool_ref[e, 1] = extra_ref[e, 0]
    elif save:
        out.append(move(low_ref, saved[2]))
    for copy in out:
        copy.wait()


def outer_back_kernel(layer, parts, top, me_ref, *refs):
    half = parts // 2
    if top:
        up_ref, refs = refs[0], refs[1:]
    else:
        up_hbm, chunks, w1_hbm = refs[0], refs[1 : 1 + parts], refs[1 + parts]
        refs = refs[2 + parts :]
    x_hbm, a3_hbm, stat_hbm, gain_hbm, w3_hbm = refs[:5]
    keep_refs, send_refs, refs = refs[5 : 5 + half], refs[5 + half : 5 + parts], refs[5 + parts :]
    da3_hbm, dgain_hbm, refs = refs[0], refs[1], refs[2:]
    if layer > 0:
        dv_hbm, refs = refs[0], refs[1:]
    x_ref, a3_ref, stat_ref, gain_ref, w3_ref, da3_ref, dgain_ref, dv_ref, p_ref, q_ref = refs[:10]
    *refs, sems = refs[10:]
    move = Moves(sems)
    if not top:
        up_ref, w1_ref = refs
        w1_in = move(w1_hbm.at[layer + 1], w1_ref)
        up_in = move(up_hbm, up_ref)
    early = [
        move(stat_hbm, stat_ref),
        move(gain_hbm.at[layer], gain_ref),
        move(a3_hbm, a3_ref),
        move(x_hbm, x_ref),
    ]
    w3_in = move(w3_hbm.at[layer], w3_ref)
    rows, width = a3_ref.shape
    neck = keep_refs[0].shape[1]
    images = rows // SLOT
    size = WIDTH // GROUPS
    tiles = tiles_of(width)
    mask = pixel_mask()
    out = []
    if top:
        pooled = jnp.sum(up_ref[...].astype(f32), axis=0) * (1.0 / PIX)
        p_ref[...] = jnp.concatenate([pooled[e] for e in range(pooled.shape[0])], axis=1)
    else:
        w1_in.wait()
        first_weight = own_order_columns(me_ref[0], w1_ref, neck)
        up_in.wait()
        for i in range(images // 2):
            here = rows_of(i, 2 * SLOT)
            left = jnp.concatenate([c[here, :] for c in chunks], axis=1)
            dv_ref[here, :] = up_ref[here, :] + lax.dot_general(
                left, first_weight, NT, preferred_element_type=f32
            )
    for copy in early:
        copy.wait()
    for i in range(images):
        here, one = rows_of(i), slice(i, i + 1)
        if layer == 0:
            da3_ref[here, :] = padded_image(x_ref, i)
        for t in tiles:
            x = da3_ref[here, t].astype(f32) if layer == 0 else x_ref[here, t]
            hat = (a3_ref[here, t] - stat_ref[0, one, t]) * stat_ref[1, one, t]
            v = x + (hat * gain_ref[0:1, t] + gain_ref[1:2, t])
            s = sigmoid(v)
            slope = s * (1.0 + v * (1.0 - s)) * mask
            dv = slope * (p_ref[one, t] if top else dv_ref[here, t])
            dv_ref[here, t] = dv
            q_ref[one, t] = jnp.sum(dv * hat, axis=0, keepdims=True)
            p_ref[one, t] = jnp.sum(dv, axis=0, keepdims=True)
    if layer > 0:
        out.append(move(dv_ref, dv_hbm))
    dgain_ref[0:1, :] = jnp.sum(q_ref[...], axis=0, keepdims=True)
    dgain_ref[1:2, :] = jnp.sum(p_ref[...], axis=0, keepdims=True)
    out.append(move(dgain_ref, dgain_hbm))
    p_ref[...] = group_mix(p_ref[...] * gain_ref[0:1, :], size)
    q_ref[...] = group_mix(q_ref[...] * gain_ref[0:1, :], size)
    w3_in.wait()
    third_weight = own_order_rows(me_ref[0], w3_ref, neck)
    for i in range(images):
        here, one = rows_of(i), slice(i, i + 1)
        for t in tiles:
            scale = stat_ref[1, one, t]
            hat = (a3_ref[here, t] - stat_ref[0, one, t]) * scale
            d = dv_ref[here, t] * gain_ref[0:1, t] - p_ref[one, t] - hat * q_ref[one, t]
            da3_ref[here, t] = (d * scale * mask).astype(bf16)
        if i % 2:
            both = rows_of(i // 2, 2 * SLOT)
            got = lax.dot_general(da3_ref[both, :], third_weight, NT, preferred_element_type=f32)
            split_store(got, both, keep_refs, send_refs, neck)
    out.append(move(da3_ref, da3_hbm))
    for copy in out:
        copy.wait()


def bottle_back_kernel(layer, terms, *refs):
    term_refs = refs[:terms]
    a1_hbm, a2_hbm, stat_hbm, gain_hbm, mid_hbm = refs[terms : terms + 5]
    da1_ref, da2_hbm, dgain_hbm = refs[terms + 5 : terms + 8]
    a1_ref, a2_ref, stat_ref, gain_ref, mid_ref = refs[terms + 8 : terms + 13]
    da2_ref, dgain_ref, work_ref, p_ref, q_ref, cols_ref, sems = refs[terms + 13 :]
    move = Moves(sems)
    early = [
        move(stat_hbm, stat_ref),
        move(gain_hbm.at[layer], gain_ref),
        move(a2_hbm, a2_ref),
    ]
    a1_in = move(a1_hbm, a1_ref)
    mid_in = move(mid_hbm.at[layer], mid_ref)
    rows, neck = a1_ref.shape
    images = rows // SLOT
    size = NECK // GROUPS
    mask = pixel_mask()

    def back(value_ref, at, out_ref):
        gain = gain_ref[at : at + 1, :]
        bias = gain_ref[at + 1 : at + 2, :]
        for i in range(images):
            here, one = rows_of(i), slice(i, i + 1)
            hat = (value_ref[here, :] - stat_ref[at, one, :]) * stat_ref[at + 1, one, :]
            v = hat * gain + bias
            s = sigmoid(v)
            dv = work_ref[here, :] * (s * (1.0 + v * (1.0 - s)) * mask)
            work_ref[here, :] = dv
            q_ref[one, :] = jnp.sum(dv * hat, axis=0, keepdims=True)
            p_ref[one, :] = jnp.sum(dv, axis=0, keepdims=True)
        dgain_ref[at : at + 1, :] = jnp.sum(q_ref[...], axis=0, keepdims=True)
        dgain_ref[at + 1 : at + 2, :] = jnp.sum(p_ref[...], axis=0, keepdims=True)
        mixed_p = group_mix(p_ref[...] * gain, size)
        mixed_q = group_mix(q_ref[...] * gain, size)
        for i in range(images):
            here, one = rows_of(i), slice(i, i + 1)
            scale = stat_ref[at + 1, one, :]
            hat = (value_ref[here, :] - stat_ref[at, one, :]) * scale
            d = work_ref[here, :] * gain - mixed_p[one] - hat * mixed_q[one]
            out_ref[here, :] = (d * scale * mask).astype(bf16)

    work_ref[...] = add_terms(term_refs)
    for copy in early:
        copy.wait()
    back(a2_ref, 2, da2_ref)
    out = [move(da2_ref, da2_hbm)]
    convolve(da2_ref, images, cols_ref)
    mid_in.wait()
    weight = jnp.concatenate(tap_weights(mid_ref)[::-1], axis=1)
    for i in range(images // 2):
        here = rows_of(i, 2 * SLOT)
        work_ref[here, :] = lax.dot_general(
            cols_ref[here, :], weight, NT, preferred_element_type=f32
        )
    a1_in.wait()
    back(a1_ref, 0, da1_ref)
    out.append(move(dgain_ref, dgain_hbm))
    for copy in out:
        copy.wait()


def small_grad_kernel(
    one_hbm,
    da2_hbm,
    bottle_hbm,
    outer_hbm,
    out_hbm,
    one_ref,
    da2_ref,
    bottle_ref,
    outer_ref,
    out_ref,
    acc_ref,
    cols_ref,
    sems,
):
    move = Moves(sems)
    da2_in = move(da2_hbm, da2_ref)
    early = [move(one_hbm, one_ref), move(bottle_hbm, bottle_ref), move(outer_hbm, outer_ref)]
    rows, neck = one_ref.shape
    size = NECK // GROUPS
    da2_in.wait()
    convolve(da2_ref, rows // SLOT, cols_ref)
    for copy in early:
        copy.wait()
    acc_ref[...] = lax.dot_general(one_ref[...], cols_ref[...], TN, preferred_element_type=f32)
    same = same_group(neck, size)
    fold = (
        lax.broadcasted_iota(jnp.int32, (size, neck), 0)
        == (lax.broadcasted_iota(jnp.int32, (size, neck), 1) & (size - 1))
    ).astype(bf16)
    out_ref[...] = jnp.zeros_like(out_ref)
    for t in range(TAPS):
        part = jnp.where(same, acc_ref[:, t * neck : (t + 1) * neck], 0.0).astype(bf16)
        to = TAPS - 1 - t
        rows_at = slice(to % 3 * size, (to % 3 + 1) * size)
        out_ref[rows_at, to // 3 * neck : (to // 3 + 1) * neck] = jnp.dot(
            fold, part, preferred_element_type=f32
        ).astype(bf16)
    out_ref[0:4, 3 * neck : 4 * neck] = bottle_ref[...].astype(bf16)
    out_ref[48:50, 0 : outer_ref.shape[1]] = outer_ref[...].astype(bf16)
    move(out_ref, out_hbm).wait()


def last_grad(chunk_refs, right_ref, out_ref):
    neck = chunk_refs[0].shape[1]
    for k, chunk_ref in enumerate(chunk_refs):
        out_ref[k * neck : (k + 1) * neck, :] = lax.dot_general(
            chunk_ref[...], right_ref[...], TN, preferred_element_type=f32
        ).astype(bf16)


def first_grad(layer, x_ref, chunk_refs, right_ref, padded_ref, out_ref):
    neck = chunk_refs[0].shape[1]
    for k, chunk_ref in enumerate(chunk_refs):
        right_ref[:, k * neck : (k + 1) * neck] = chunk_ref[...]
    left_ref = x_ref
    if layer == 0:
        left_ref = padded_ref
        for i in range(padded_ref.shape[0] // SLOT):
            padded_ref[rows_of(i), :] = padded_image(x_ref, i)
    for t in tiles_of(x_ref.shape[1]):
        out_ref[t, :] = lax.dot_general(
            left_ref[:, t], right_ref[...], TN, preferred_element_type=f32
        ).astype(bf16)


def grad_kernel(layers, near, pieces, parts, me_ref, *refs):
    many = parts + 1
    count = (layers[0] is not None) * many + (layers[1] is not None) * (many + 1)
    hbm, (keep_hbm, send_hbm), refs = refs[:count], refs[count : count + 2], refs[count + 2 :]
    *refs, sems = refs
    move = Moves(sems)
    outs = []

    def give(out_ref, at):
        size = out_ref.shape[0] // pieces
        for j in range(pieces // 2):
            for target, bit in ((send_hbm, 1 - me_ref[3]), (keep_hbm, me_ref[3])):
                start = pl.multiple_of((2 * j + bit) * size, 16)
                outs.append(
                    move(out_ref.at[pl.ds(start, size), :], target.at[j, at : at + size, :])
                )

    jobs = []
    if layers[0] is not None:
        held, out_ref, refs = refs[:many], refs[many], refs[many + 1 :]
        jobs.append((0, held, out_ref, [move(a, b) for a, b in zip(hbm[:many], held)]))
        hbm = hbm[many:]
    if layers[1] is not None:
        held, right_ref, padded_ref, out_ref = refs[:-3], *refs[-3:]
        width = held[0].shape[1]
        ins = [move(a, b) for a, b in zip(hbm[:many], held)]
        if near:
            held = [held[0], *hbm[1:many]]
        ins.append(move(hbm[many], out_ref.at[width : width + SMALL]))
        jobs.append((1, held, out_ref, ins))
    at = 0
    for which, held, out_ref, ins in jobs:
        for copy in ins:
            copy.wait()
        if which:
            first_grad(layers[1], held[0], held[1:], right_ref, padded_ref, out_ref)
        else:
            last_grad(held[:parts], held[parts], out_ref)
        give(out_ref, at)
        at += out_ref.shape[0] // pieces
    for copy in outs:
        copy.wait()


def head_kernel(me_ref, games_ref, p_ref, w_hbm, target_hbm, out_ref, now_hbm, *refs):
    now_ref, later_ref, w_ref, target_ref, own_ref, acc_ref, sems = refs
    move = Moves(sems)
    count = w_hbm.shape[0]
    ins = [
        [move(source.at[g], target.at[g]) for g in range(count)]
        for source, target in ((w_hbm, w_ref), (target_hbm, target_ref))
    ]
    for at, cols_ref in enumerate((now_ref, later_ref)):
        cols_ref[...] = p_ref[:, at].astype(f32).reshape(cols_ref.shape).astype(bf16)
    out = move(now_ref, now_hbm)
    total, outputs = games_ref.shape[1], w_hbm.shape[1]
    game = to_column(games_ref[...].astype(f32))
    base = (me_ref[0] * count).astype(f32)
    acc_ref[...] = jnp.zeros_like(acc_ref)
    parts, _, rows, _ = out_ref.shape
    for at, (cols, weight) in enumerate(((now_ref, w_ref), (later_ref, target_ref))):
        for g in range(count):
            own_ref[g] = jnp.where(game == base + g, cols[...], jnp.zeros_like(cols))
        for copy in ins[at]:
            copy.wait()
        for start in range(0, outputs, 128):
            here = slice(start, min(start + 128, outputs))
            scores = None
            for g in range(count):
                part = lax.dot_general(
                    weight[g, here, :].astype(bf16), own_ref[g], NT, preferred_element_type=f32
                )
                scores = part if scores is None else scores + part
            acc_ref[here, 0:total] = scores
        logits = acc_ref[...].T[0:total, 0:outputs]
        out_ref[:, at] = logits.reshape(parts, rows, outputs).astype(out_ref.dtype)
    out.wait()


def head_back_kernel(
    me_ref, games_ref, spread_ref, now_hbm, w_hbm, out_ref, g_hbm, square_hbm, *refs
):
    now_ref, g_ref, square_ref, w_ref, acc_ref, sems = refs
    move = Moves(sems)
    count = w_hbm.shape[0]
    ins = [move(w_hbm.at[g], w_ref.at[g]) for g in range(count)]
    now_in = move(now_hbm, now_ref)
    g_ref[...] = spread_ref[...].astype(f32).reshape(g_ref.shape).astype(bf16)
    out = [move(g_ref, g_hbm)]
    row = games_ref[...].astype(f32)
    game = to_column(row)
    base = me_ref[0] * count
    now_in.wait()
    inner_p = lax.dot_general(now_ref[...], now_ref[...], NT, preferred_element_type=f32)
    inner_g = lax.dot_general(g_ref[...], g_ref[...], NT, preferred_element_type=f32)
    low = base.astype(f32)
    pair = (game == row) & (row >= low) & (row < low + count)
    square_ref[...] = jnp.sum(jnp.where(pair, inner_p * inner_g, 0.0), axis=0, keepdims=True)
    out.append(move(square_ref, square_hbm))
    acc_ref[...] = jnp.zeros_like(acc_ref)
    for g in range(count):
        grad = jnp.where(game == low + g, g_ref[...], jnp.zeros_like(g_ref))
        ins[g].wait()
        acc_ref[...] += jnp.dot(grad, w_ref[g].astype(bf16), preferred_element_type=f32)
    out_ref[...] = acc_ref[...].reshape(out_ref.shape).astype(out_ref.dtype)
    for copy in out:
        copy.wait()


def adamw(weight, first, second, grad, rate):
    momentum = 0.9 * first + 0.1 * grad
    variance = 0.999 * second + 0.001 * grad * grad
    root = jnp.sqrt(variance * (1.0 / (1.0 - 0.999**STEP))) + 1e-08
    scaled = (momentum * (1.0 / (1.0 - 0.9**STEP))) / root
    return (weight - rate * (scaled + 0.1 * weight), momentum, variance)


def head_step_kernel(games, me_ref, scale_ref, games_ref, p_ref, g_ref, *refs):
    (w_hbm, m_hbm, v_hbm), (w_out, m_out, v_out, *refs) = refs[:3], refs[-10:]
    old, new, sems = refs[:3], refs[3:6], refs[6]
    move = Moves(sems)
    slots = new[0].shape[0]
    base = me_ref[0] * w_hbm.shape[0]
    ins = [
        [move(source.at[g], ref.at[k]) for source, ref in zip((w_hbm, m_hbm, v_hbm), old)]
        for k, g in enumerate(games)
    ]
    outs = []
    for k, g in enumerate(games):
        left = jnp.where(games_ref[...] == base + g, g_ref[...], jnp.zeros_like(g_ref))
        grad = jnp.dot(left, p_ref[...], preferred_element_type=f32) * scale_ref[0, 0]
        for copy in ins[k]:
            copy.wait()
        if k >= slots:
            for copy in outs[k - slots]:
                copy.wait()
        made = adamw(*(ref[k] for ref in old), grad, rates[5])
        for ref, value in zip(new, made):
            ref[k % slots] = value
        outs.append(
            [
                move(ref.at[k % slots], target.at[g])
                for ref, target in zip(new, (w_out, m_out, v_out))
            ]
        )
    for group in outs[-slots:]:
        for copy in group:
            copy.wait()


def bring(move, source_hbm, target_ref, at, size):
    if not size:
        return [move(source_hbm, target_ref)]
    return [
        move(source_hbm.at[d, at : at + size, :], target_ref.at[d * size : (d + 1) * size, :])
        for d in range(source_hbm.shape[0])
    ]


def step_part(refs, at, grad, scale, rate):
    made = adamw(*(ref[at] for ref in refs), grad.astype(f32) * scale, rate)
    for ref, value in zip(refs, made):
        ref[at] = value


def last_step_kernel(parts, cuts, me_ref, scale_ref, *refs):
    grads_hbm, old_hbm, new_hbm = refs[:LAYERS], refs[LAYERS : LAYERS + 3], refs[LAYERS + 3 : LAYERS + 6]
    grads, held, sems = refs[LAYERS + 6 : -4], refs[-4:-1], refs[-1]
    move = Moves(sems)
    ins = []
    for layer in range(LAYERS):
        ins.append(bring(move, grads_hbm[layer], grads[layer], *cuts[layer]))
        ins[-1] += [move(a.at[layer], b.at[layer]) for a, b in zip(old_hbm, held)]
    me, scale = me_ref[0], scale_ref[0, 0]
    neck = NECK // parts
    outs = []
    for layer in range(LAYERS):
        for copy in ins[layer]:
            copy.wait()
        for q in range(parts):
            chunk = slice(q * neck, (q + 1) * neck)
            from_ = pl.ds(pl.multiple_of((me ^ q) * neck, neck), neck)
            step_part(held, (layer, chunk), grads[layer][from_, :], scale, rates[2])
        outs += [move(a.at[layer], b.at[layer]) for a, b in zip(held, new_hbm)]
    for copy in outs:
        copy.wait()


def first_step_kernel(parts, cuts, me_ref, scale_ref, *refs):
    grads_hbm, refs = refs[:LAYERS], refs[LAYERS:]
    old_hbm, new_hbm, refs = refs[:12], refs[12:24], refs[24:]
    grads, held, sems = refs[:LAYERS], refs[LAYERS : LAYERS + 12], refs[-1]
    move = Moves(sems)
    grads_in = []
    for layer in range(LAYERS):
        grads_in += bring(move, grads_hbm[layer], grads[layer], *cuts[layer])
    ins = [move(old_hbm[k], held[k]) for k in range(3, 12)]
    wide = [[move(old_hbm[k].at[layer], held[k].at[layer]) for k in range(3)] for layer in range(LAYERS)]
    me, scale = me_ref[0], scale_ref[0, 0]
    width = grads[0].shape[0] - SMALL
    size = NECK // GROUPS
    neck = NECK // parts
    for copy in (*grads_in, *ins):
        copy.wait()
    for layer in range(LAYERS):
        small = grads[layer]
        for k in range(3):
            taps = slice(k * 3 * size, (k + 1) * 3 * size)
            grad = small[width : width + 3 * size, k * neck : (k + 1) * neck]
            step_part(held[3:6], (layer, taps), grad, scale, rates[1])
        grad = small[width : width + 16, 3 * neck : 4 * neck][0:4]
        step_part(held[6:9], (layer,), grad, scale, rates[3])
        grad = small[width + 48 : width + 64, 0:width][0:2]
        step_part(held[9:12], (layer,), grad, scale, rates[4])
    outs = [move(held[k], new_hbm[k]) for k in range(3, 12)]
    for layer in range(LAYERS):
        for copy in wide[layer]:
            copy.wait()
        for q in range(parts):
            chunk = slice(q * neck, (q + 1) * neck)
            from_ = chunk if neck % 128 else pl.ds(pl.multiple_of((me ^ q) * neck, neck), neck)
            grad = grads[layer][0:width, from_]
            step_part(held[:3], (layer, slice(None), chunk), grad, scale, rates[0])
        outs += [move(held[k].at[layer], new_hbm[k].at[layer]) for k in range(3)]
    for copy in outs:
        copy.wait()


def loss_kernel(total, me_ref, *refs):
    part_ref, hbm, (g_ref, loss_hbm), refs = refs[0], refs[1:8], refs[8:10], refs[10:]
    vmem, (loss_ref, l_ref, sems) = refs[:7], refs[7:]
    move = Moves(sems)
    for copy in [move(source, target) for source, target in zip(hbm, vmem)]:
        copy.wait()
    act_row, next_row, done_row, game_row, legal, index, share = (ref[...] for ref in vmem)
    act, later_act, done, game = (
        to_column(row.astype(f32)) for row in (act_row, next_row, done_row, game_row)
    )
    count = act.shape[0]
    first = me_ref[1].astype(f32)
    own = ((game >= first) & (game < first + me_ref[2].astype(f32))).astype(f32)
    later = jnp.sum(part_ref[:, 1].astype(f32), axis=0)
    chosen = jnp.zeros((count, ATOMS), f32)
    for a in range(ACTIONS):
        chosen = jnp.where(later_act == a, later[:, a * ATOMS : (a + 1) * ATOMS], chosen)
    source = jnp.exp(chosen - jnp.max(chosen, axis=1, keepdims=True))
    source = source / jnp.sum(source, axis=1, keepdims=True)
    source = jnp.where(done > 0.0, 1.0 / ATOMS, source)
    atom = lax.broadcasted_iota(jnp.int32, (count, ATOMS), 1)
    lower, upper = source * share, source * (1.0 - share)
    proj = jnp.zeros((count, ATOMS), f32)
    for j in range(ATOMS):
        gap = atom - index[:, j : j + 1]
        proj = proj + jnp.where(
            gap == 0, lower[:, j : j + 1], jnp.where(gap == 1, upper[:, j : j + 1], 0.0)
        )
    logits = jnp.sum(part_ref[:, 0].astype(f32), axis=0)
    for a in range(ACTIONS):
        l_ref[a] = logits[:, a * ATOMS : (a + 1) * ATOMS]
    l = l_ref[...]
    top = jnp.max(l, axis=2, keepdims=True)
    e = jnp.exp(l - top)
    s = jnp.sum(e, axis=2, keepdims=True)
    p = e / s
    logp = l - top - jnp.log(s)
    z = -10.0 + 20.0 * lax.broadcasted_iota(jnp.int32, (1, 1, ATOMS), 2).astype(f32) / (ATOMS - 1)
    q = jnp.sum(p * z, axis=2, keepdims=True)
    action = lax.broadcasted_iota(jnp.int32, (ACTIONS, count, 1), 0).astype(f32)
    hot = (action == act[None]).astype(f32)
    allowed = jnp.concatenate([legal[:, a : a + 1][None] for a in range(ACTIONS)], axis=0) > 0
    masked = jnp.where(allowed, q, -1e30)
    best = jnp.max(masked, axis=0, keepdims=True)
    ex = jnp.where(allowed, jnp.exp(masked - best), 0.0)
    tot = jnp.sum(ex, axis=0, keepdims=True)
    taken = jnp.sum(hot * logp, axis=0)
    cross = -jnp.sum(proj * taken, axis=1, keepdims=True)
    picked = jnp.sum(hot * q, axis=0)
    loss = cross + 0.05 * (best[0] + jnp.log(tot[0]) - picked)
    loss_ref[...] = jnp.broadcast_to(loss * own, loss_ref.shape)
    mass = jnp.sum(proj, axis=1, keepdims=True)
    grad = hot * (p * mass[None] - proj[None]) + (0.05 * (ex / tot - hot)) * (p * (z - q))
    grad = grad * (own * (1.0 / total))[None]
    flat = jnp.concatenate([grad[a] for a in range(ACTIONS)], axis=1).astype(bf16)
    for k in range(g_ref.shape[0]):
        g_ref[k] = flat
    move(loss_ref, loss_hbm).wait()


def flip(value, axis, size, bit):
    return lax.ppermute(value, axis, [(i, i ^ bit) for i in range(size)])


def bits_of(size):
    return [1 << b for b in range(size.bit_length() - 1)]


def after(value, *tokens):
    return lax.optimization_barrier((value, *tokens))[0]


def after_all(token, *values):
    return lax.optimization_barrier((*values, token))[:-1]


def scatter_chan(keeps, sends, size):
    half = size // 2
    terms = {j: [keeps[j]] for j in range(half)}
    for j in reversed(range(half)):
        terms[j].append(flip(sends[j], "chan", size, 1))
    sent = []
    for bit in bits_of(size)[1:]:
        step = bit // 2
        for j in sorted(terms, reverse=True):
            if j & step:
                whole, *rest = terms.pop(j)
                for term in rest:
                    whole = whole + term.astype(f32)
                sent.append(whole.astype(bf16))
                terms[j - step].append(flip(sent[-1], "chan", size, bit))
    return terms[0], sent[-1]


def gather_chan(own, size, *hold):
    chunks = {0: own}
    for bit in reversed(bits_of(size)):
        for k in list(chunks):
            value = after(chunks[k], *hold) if k else own
            chunks[k ^ bit] = flip(value, "chan", size, bit)
    return [chunks[k] for k in range(size)]


class Spread:
    def __init__(self, value, size):
        self.value, self.size = value, size
        self.left = bits_of(size)
        self.me = lax.axis_index("dp")

    def begin(self, keep, send):
        self.keep, self.sent = keep.astype(f32), send
        self.got = flip(send, "dp", self.size, self.left.pop(0))
        return self

    def send(self):
        bit = self.left.pop(0)
        pieces, *rest = self.value.shape
        paired = self.value.reshape(pieces // 2, 2, *rest)
        mine = ((self.me & bit) > 0).astype(jnp.int32)
        part = lambda at: lax.dynamic_index_in_dim(paired, at, 1, keepdims=False)
        self.keep = part(mine).astype(f32)
        self.sent = part(1 - mine).astype(bf16)
        self.got = flip(self.sent, "dp", self.size, bit)
        return self

    def add(self, *hold):
        got = after(self.got, *hold) if hold else self.got
        self.value = self.keep + got.astype(f32)
        self.sent = None
        if self.left:
            self.send()
        return self

    def finish(self, *hold):
        self.add(*hold)
        while self.sent is not None:
            self.add()
        return self


class Collect:
    def __init__(self, value, size, *hold):
        self.size, self.left = size, bits_of(size)
        self.me = lax.axis_index("dp")
        self.value = value.astype(bf16)
        self.send(*hold)

    def send(self, *hold):
        self.bit = self.left.pop()
        self.sent = after(self.value, *hold) if hold else self.value
        self.got = flip(self.sent, "dp", self.size, self.bit)

    def join(self, *hold):
        got = after(self.got, *hold) if hold else self.got
        upper = (self.me & self.bit) > 0
        pair = jnp.stack(
            [jnp.where(upper, got, self.value), jnp.where(upper, self.value, got)], axis=1
        )
        self.value = pair.reshape(2 * got.shape[0], *got.shape[1:])
        if self.left:
            self.send()
        return self

    def finish(self, *hold):
        while self.left:
            self.join(*hold)
        return self.join(*hold).value


def sum_all(value, sizes):
    for axis, size in sizes:
        for bit in bits_of(size):
            value = value + flip(value, axis, size, bit)
    return value


def swap_chunks(value, axis, size):
    me = lax.axis_index("chan")
    width = value.shape[axis] // size
    return jnp.concatenate(
        [
            lax.dynamic_slice_in_dim(value, (me ^ k) * width, width, axis=axis)
            for k in range(size)
        ],
        axis=axis,
    )


def body(
    obs_now,
    obs_next,
    games,
    actions,
    next_actions,
    legal,
    done,
    proj_index,
    proj_frac,
    weight_in,
    weight_mid,
    weight_out,
    bottle_gains,
    stream_gains,
    weight_head,
    first_in,
    first_mid,
    first_out,
    first_bottle,
    first_stream,
    first_head,
    second_in,
    second_mid,
    second_out,
    second_bottle,
    second_stream,
    second_head,
    target_in,
    target_mid,
    target_out,
    target_bottle,
    target_stream,
    target_head,
):
    n_chan, n_dp = lax.axis_size("chan"), lax.axis_size("dp")
    chan_at, dp_at = lax.axis_index("chan"), lax.axis_index("dp")
    width = obs_now.shape[1]
    neck = weight_mid.shape[1]
    images = obs_now.shape[0] // PIX
    rows = images * SLOT
    half = n_chan // 2
    big = 2 * rows * width * NECK
    local_games, shard, outputs = weight_head.shape
    count = actions.shape[0]
    total = count * n_dp
    me = jnp.stack([chan_at, chan_at * local_games, local_games, dp_at & 1]).astype(jnp.int32)
    turn = lambda array: array.swapaxes(1, 2)
    wide = shape((rows, width), f32)
    wide_low = shape((rows, width), bf16)
    slim = shape((rows, neck), f32)
    slim_low = shape((rows, neck), bf16)
    split_outs = [(WHOLE, slim)] * half + [(WHOLE, slim_low)] * half
    weights = shape((width, NECK), f32)

    def scratch(*shapes):
        return [pltpu.VMEM(s.shape, s.dtype) for s in shapes]

    def like(array):
        return shape(array.shape[1:], array.dtype)

    def here(*arrays):
        return [(WHOLE, array) for array in arrays]

    def far(*arrays):
        return [(DISTANT, array) for array in arrays]

    def columns(weight):
        return weight if neck % 128 == 0 else swap_chunks(weight, 2, n_chan)

    def front(obs, nets):
        return call(
            functools.partial(front_kernel, n_chan),
            [(SCALARS, me), *far(obs, nets[0])],
            split_outs,
            scratch(obs, like(nets[0])),
            big,
            2,
        )

    def bottle(layer, terms, nets, save):
        stats = shape((4, images, neck), f32)
        outs = [(WHOLE, slim_low)]
        if save:
            outs += far(slim_low, slim, slim, stats)
        return call(
            functools.partial(bottle_kernel, layer, len(terms), save),
            [*here(*terms), *far(nets[3], nets[1])],
            outs,
            scratch(
                slim_low,
                slim,
                slim,
                stats,
                shape((images, neck), f32),
                shape((rows, TAPS * neck), bf16),
                like(nets[3]),
                like(nets[1]),
            ),
            big,
            6 if save else 2,
        )

    def third(layer, chunks, stream, nets, save, other=None):
        last = layer == LAYERS - 1
        stats = shape((2, images, width), f32)
        keep = scratch(
            wide,
            stats,
            shape((images, width), f32),
            stream,
            like(nets[2]),
            like(nets[4]),
        )
        if last:
            outs = [(WHOLE, shape((width // shard, 2, images, shard), bf16))]
            extra = (WHOLE, other)
        else:
            outs = [(DISTANT, wide), *split_outs]
            extra = (DISTANT, nets[0])
            keep += scratch(wide, wide_low, like(nets[0]))
        if save:
            outs += far(wide, stats) if last else far(wide, stats, wide_low)
        return call(
            functools.partial(third_kernel, layer, n_chan, last, save),
            [(SCALARS, me), *here(*chunks), *far(stream, nets[2], nets[4]), extra],
            outs,
            keep,
            2 * big,
            (3 if last else 4 + images // 2) + (2 + (not last)) * save,
        )

    online = (columns(weight_in), turn(weight_mid), weight_out, bottle_gains, stream_gains)
    target = (columns(target_in), turn(target_mid), target_out, target_bottle, target_stream)

    stream_n, stream_o, low_o = obs_next, obs_now, obs_now
    split_n = front(obs_next, target)
    terms_n, sent_n = scatter_chan(split_n[:half], split_n[half:], n_chan)
    split_o = front(after(obs_now, split_n[0]), online)
    terms_o, sent_o = scatter_chan(split_o[:half], split_o[half:], n_chan)
    kept = []
    for layer in range(LAYERS):
        terms_n[-1] = after(terms_n[-1], sent_o)
        (two_n,) = bottle(layer, terms_n, target, False)
        terms_o[-1] = after(terms_o[-1], two_n)
        two_o, *inner = bottle(layer, terms_o, online, True)
        chunks_n = gather_chan(two_n, n_chan, two_o)
        if layer < LAYERS - 1:
            stream_n, *split_n = third(layer, chunks_n, stream_n, target, False)
            terms_n, sent_n = scatter_chan(split_n[:half], split_n[half:], n_chan)
            chunks_o = gather_chan(two_o, n_chan, split_n[0])
            chunks_o[0] = after(chunks_o[0], sent_n)
            got = third(layer, chunks_o, stream_o, online, True)
            kept.append((stream_o, low_o, inner, chunks_o, got[1 + n_chan : 3 + n_chan]))
            stream_o, low_o, split_o = got[0], got[-1], list(got[1 : 1 + n_chan])
            split_o[half:] = [after(part, terms_n[-1]) for part in split_o[half:]]
            terms_o, sent_o = scatter_chan(split_o[:half], split_o[half:], n_chan)
        else:
            empty = jnp.zeros((width // shard, 2, images, shard), bf16)
            (pooled,) = third(layer, chunks_n, stream_n, target, False, empty)
            chunks_o = gather_chan(two_o, n_chan, pooled)
            pooled, *saved = third(layer, chunks_o, stream_o, online, True, pooled)
            kept.append((stream_o, low_o, inner, chunks_o, saved))

    row = games.reshape(1, total)
    mine = lax.dynamic_slice_in_dim(row, dp_at * count, count, 1)
    heads_online, heads_target = turn(weight_head), turn(target_head)
    head_flops = 2 * total * shard * outputs * local_games
    cols_shape = shape((total, shard), bf16)
    grad_shape = shape((total, outputs), bf16)

    pooled = lax.all_gather(pooled, "chan", axis=0, tiled=True)
    cols = lax.all_to_all(pooled, "dp", split_axis=0, concat_axis=0, tiled=True)
    parts, cols_now = call(
        head_kernel,
        [(SCALARS, me), *here(row, cols), *far(heads_online, heads_target)],
        [(WHOLE, shape((n_dp, 2, count, outputs), bf16)), (DISTANT, cols_shape)],
        scratch(
            cols_shape,
            cols_shape,
            heads_online,
            heads_target,
            shape((local_games, total, shard), bf16),
            shape((-(-outputs // 128) * 128, max(total, 128)), f32),
        ),
        2 * head_flops,
        2 * local_games + 1,
        WIDE,
    )
    parts = lax.all_to_all(parts, "dp", split_axis=0, concat_axis=0, tiled=True)
    facts = (
        actions.reshape(1, count),
        next_actions.reshape(1, count),
        done.reshape(1, count),
        mine,
        legal,
        proj_index,
        proj_frac,
    )
    losses_shape = shape((count, 128), f32)
    spread, losses = call(
        functools.partial(loss_kernel, total),
        [(SCALARS, me), (WHOLE, parts), *far(*facts)],
        [(WHOLE, shape((n_dp, count, outputs), bf16)), (DISTANT, losses_shape)],
        scratch(*facts, losses_shape, shape((ACTIONS, count, ATOMS), f32)),
        big,
        8,
    )
    spread = lax.all_to_all(spread, "dp", split_axis=0, concat_axis=0, tiled=True)
    d_cols, all_grad, square_head = call(
        head_back_kernel,
        [(SCALARS, me), *here(row, spread), *far(cols_now, heads_online)],
        [
            (WHOLE, shape((n_dp, count, shard), bf16)),
            *far(grad_shape, shape((1, total), f32)),
        ],
        scratch(
            cols_shape,
            grad_shape,
            shape((1, total), f32),
            heads_online,
            shape((total, shard), f32),
        ),
        head_flops,
        local_games + 3,
        WIDE,
    )
    d_rows = lax.all_to_all(d_cols, "dp", split_axis=0, concat_axis=0, tiled=True)
    d_rows = d_rows.reshape(n_chan, n_dp // n_chan, count, shard)
    upstream = lax.all_to_all(d_rows, "chan", split_axis=0, concat_axis=0, tiled=True)

    def outer_back(layer, lead):
        stream, _, _, _, (a3, stats3) = kept[layer]
        gains = shape((2, width), f32)
        outs = [*split_outs, *far(wide_low, gains)]
        if layer > 0:
            outs += far(wide)
        keep = scratch(
            stream,
            wide,
            stats3,
            like(stream_gains),
            like(weight_out),
            wide_low,
            gains,
            wide,
            shape((images, width), f32),
            shape((images, width), f32),
        )
        top = layer == LAYERS - 1
        if not top:
            keep += scratch(wide, like(online[0]))
        return call(
            functools.partial(outer_back_kernel, layer, n_chan, top),
            [(SCALARS, me), *lead, *far(stream, a3, stats3, stream_gains, weight_out)],
            outs,
            keep,
            2 * big,
            7 + (layer > 0) + 2 * (not top),
        )

    def bottle_back(layer, terms):
        _, _, (_, a1, a2, stats), _, _ = kept[layer]
        gains = shape((4, neck), f32)
        sums_shape = shape((images, neck), f32)
        return call(
            functools.partial(bottle_back_kernel, layer, len(terms)),
            [*here(*terms), *far(a1, a2, stats, bottle_gains, online[1])],
            [(WHOLE, slim_low), *far(slim_low, gains)],
            scratch(
                slim,
                slim,
                stats,
                like(bottle_gains),
                like(online[1]),
                slim_low,
                gains,
                slim,
                sums_shape,
                sums_shape,
                shape((rows, TAPS * neck), bf16),
            ),
            big,
            7,
        )

    def small_grad(layer, da2, d_bottle, d_outer):
        ins = (kept[layer][2][0], da2, d_bottle, d_outer)
        out = shape((SMALL, NECK), bf16)
        (got,) = call(
            small_grad_kernel,
            far(*ins),
            far(out),
            scratch(
                *ins,
                out,
                shape((neck, TAPS * neck), f32),
                shape((rows, TAPS * neck), bf16),
            ),
            big,
            5,
        )
        return got

    whole_pieces = width == NECK and NECK // n_dp % 16 == 0 and (width + SMALL) // n_dp % 16 == 0

    def gradients(last_layer=None, da3=None, first_layer=None, grads=(), small=None):
        ins, keep, size = [], [], 0
        if last_layer is not None:
            ins += [*kept[last_layer][3], da3]
            keep += [*ins, shape((NECK, width), bf16)]
            size += NECK * width // NECK // n_dp
        near, placed = first_layer == 0, None
        if first_layer is not None:
            more = [kept[first_layer][1], *grads]
            ins += [*more, small]
            if near:
                placed = [*far(more[0]), *here(*grads), *far(small)]
                more = more[:1]
            keep += [*more, shape((rows, NECK), bf16), wide_low, shape((width + SMALL, NECK), bf16)]
            size += (width + SMALL) // n_dp
        pieces = n_dp if whole_pieces else 2
        out = shape((pieces // 2, size if whole_pieces else size * n_dp // 2, NECK), bf16)
        if whole_pieces:
            keep_part, send_part = call(
                functools.partial(grad_kernel, (last_layer, first_layer), near, n_dp, n_chan),
                [(SCALARS, me), *(placed or far(*ins))],
                far(out, out),
                scratch(*keep),
                2 * big,
                len(ins) + 4 * n_dp,
            )
            return Spread(None, n_dp).begin(keep_part, send_part)
        flat = []
        if last_layer is not None:
            left = jnp.concatenate(kept[last_layer][3], axis=1)
            got = lax.dot_general(left, da3, TN, preferred_element_type=f32).astype(bf16)
            flat.append(got.reshape(n_dp, -1, NECK))
        if first_layer is not None:
            left = kept[first_layer][1]
            if first_layer == 0:
                left = jnp.pad(left.reshape(images, PIX, width), ((0, 0), (0, SLOT - PIX), (0, 0)))
                left = left.reshape(rows, width)
            right = jnp.concatenate(grads, axis=1)
            got = lax.dot_general(left, right, TN, preferred_element_type=f32).astype(bf16)
            got = jnp.concatenate([got, small], axis=0)
            flat.append(got.reshape(n_dp, -1, NECK))
        return Spread(jnp.concatenate(flat, axis=1), n_dp).send()

    lead = here(upstream)
    above = None
    for layer in reversed(range(LAYERS)):
        got = outer_back(layer, lead)
        da3, d_outer, *rest = got[n_chan:]
        terms, sent = scatter_chan(got[:half], got[half:n_chan], n_chan)
        da3 = after(da3, sent)
        if layer:
            above = gradients(layer, da3)
            hold = above.sent
        else:
            most = gradients(layer, da3, layer + 1, chunks, small)
            hold = most.sent
        terms[-1] = after(terms[-1], hold)
        da1, da2, d_bottle = bottle_back(layer, terms)
        if layer:
            above.add(da1)
            small = small_grad(layer, after(da2, above.sent), d_bottle, d_outer)
            above.add(small)
            chunks = gather_chan(da1, n_chan, above.sent)
            lead = [*far(*rest), *here(*chunks), *far(online[0])]
        else:
            above.finish(da1)
            top_last = Collect(above.value, n_dp)
            small = small_grad(layer, after(da2, top_last.sent), d_bottle, d_outer)
            chunks = gather_chan(da1, n_chan, small)
    final = gradients(first_layer=0, grads=chunks, small=small)
    most.add(final.sent)
    top_last.join(most.sent)
    square_head, top_value = after_all(most.sent, square_head, above.value)
    squares = jnp.sum(square_head) + jnp.sum(top_value * top_value)
    final.add(squares, top_last.sent)
    most.add(final.sent)
    top_last.join(most.sent)
    final.add(top_last.sent)
    most.finish(final.sent)
    squares = squares + jnp.sum(most.value * most.value)
    bulk = Collect(most.value, n_dp, squares)
    final.finish(bulk.sent)
    squares = squares + jnp.sum(final.value * final.value)
    below = Collect(final.value, n_dp, squares)
    bulk.join(below.sent)

    scalars = jnp.stack([squares, jnp.sum(losses[:, 0])])
    scalars = jnp.pad(scalars, (0, 126)).reshape(1, 128)
    scalars = sum_all(scalars, (("chan", n_chan),))
    for bit in (1, *reversed(bits_of(n_dp)[1:])):
        if bit == 2 and bulk.left:
            bulk.join(scalars)
            scalars = after(scalars, bulk.sent)
        scalars = scalars + flip(scalars, "dp", n_dp, bit)
    if below.left:
        below.join(scalars)
    scalars = after(scalars, below.sent)
    gradient_norm = jnp.sqrt(scalars[0, 0])
    loss_sum = scalars[0, 1]
    scale = jnp.minimum(1.0, 0.01 / (gradient_norm + 1e-06))

    head_shape = shape((local_games, outputs, shard), f32)

    def head_step(first_game, last_game, scale, before):
        chosen = range(first_game, last_game)
        held = shape((len(chosen), outputs, shard), f32)
        aliases = [(8 + k, k) for k in range(3)] if before else ()
        return call(
            functools.partial(head_step_kernel, chosen),
            [
                (SCALARS, me),
                (SCALARS, scale.reshape(1, 1)),
                *here(row, cols_now, all_grad.T),
                *far(heads_online, turn(first_head), turn(second_head), *before),
            ],
            far(head_shape, head_shape, head_shape),
            scratch(*[held] * 3, *[shape((2, outputs, shard), f32)] * 3),
            head_flops,
            6 * len(chosen),
            WIDE,
            aliases,
        )

    head_out = head_step(0, local_games, scale, ())
    while below.left:
        below.join(head_out[0])
    piece = NECK * width // NECK // n_dp
    bulk = bulk.finish(head_out[0])
    lasts = [(bulk, 0, piece), (top_last.finish(head_out[0]), 0, piece)]
    if not whole_pieces:
        lasts = [(g[:, :piece].reshape(NECK, width), 0, 0) for g, _, _ in lasts]

    def torso_step(kernel, grads, olds, hold):
        news = [shape(array.shape, f32) for array in olds]
        moves = 2 * len(olds) + LAYERS * (n_dp + len(olds))
        arrays = after_all(hold, *[g for g, _, _ in grads])
        cuts = [(at, size) for _, at, size in grads]
        flat = [shape((g.shape[0] * size, NECK) if size else g.shape, bf16) for g, _, size in grads]
        return call(
            functools.partial(kernel, n_chan, cuts),
            [(SCALARS, me), (SCALARS, scale.reshape(1, 1)), *far(*arrays, *olds)],
            far(*news),
            scratch(*flat, *news),
            big,
            moves,
            WIDE,
        )

    result_out = torso_step(last_step_kernel, lasts, (weight_out, first_out, second_out), head_out[0])
    below = below.finish(result_out[0])
    firsts = [(below, 0, below.shape[1]), (bulk, piece, below.shape[1])]
    if not whole_pieces:
        firsts = [g[:, at:].reshape(-1, NECK) for g, at, _ in firsts]
        if neck % 128:
            firsts = [
                jnp.concatenate([swap_chunks(g[:width], 1, n_chan), g[width:]], axis=0)
                for g in firsts
            ]
        firsts = [(g, 0, 0) for g in firsts]
    olds = (
        (weight_in, first_in, second_in),
        tuple(map(turn, (weight_mid, first_mid, second_mid))),
        (bottle_gains, first_bottle, second_bottle),
        (stream_gains, first_stream, second_stream),
    )
    olds = [array for group in olds for array in group]
    result = list(torso_step(first_step_kernel, firsts, olds, result_out[0]))
    result[3:6] = map(turn, result[3:6])
    result[6:6] = result_out
    return (*result, *map(turn, head_out), gradient_norm, loss_sum)


def solution(mesh):
    rows = P("dp", "chan")
    third = P(None, None, "chan")
    second = P(None, "chan", None)
    heads = P("chan", "dp", None)
    torso = (second, second, third, third, third, heads)
    placed = (
        rows,
        rows,
        P(),
        P("dp"),
        P("dp"),
        P("dp", None),
        P("dp"),
        P("dp", None),
        P("dp", None),
        *torso,
        *torso,
        *torso,
        *torso,
    )
    outs = tuple(spec for spec in torso for _ in range(3)) + (P(), P())
    return jax.shard_map(body, mesh=mesh, in_specs=placed, out_specs=outs, check_vma=False)
```
